512 devices in a mesh: gx: 32 (over z, y_lo), gy: 16 (over x, y_hi, core).
Axes of the slice: x: 4, y: 4 (y_hi: 2, y_lo: 2; y = y_hi * 2 + y_lo), z: 16, core: 2. Of those that a mesh axis runs over, the one named last changes fastest.
Arguments:
- e_fwd: float32 [3, 128, 512, 256], P(None, 'gx', 'gy'), may hold values from -6 to 6
- h_fwd: float32 [3, 128, 512, 256], P(None, 'gx', 'gy'), may hold values from -6 to 6
- e_adj: float32 [3, 128, 512, 256], P(None, 'gx', 'gy'), may hold values from -6 to 6
- h_adj: float32 [3, 128, 512, 256], P(None, 'gx', 'gy'), may hold values from -6 to 6
- eps_back: float32 [128, 512, 256], P('gx', 'gy'), may hold values from 1 to 12
- density: float32 [4, 128, 512], P(None, 'gx', 'gy'), may hold values from 0 to 1
- design_mask: int32 [4, 128, 512], P(None, 'gx', 'gy'), may hold values 0 or 1
- partner_map: int32 [4, 128, 512], P(None, 'gx', 'gy'), may hold values from 0 to 511, as said below
- mon_fwd: float32 [2, 3, 4, 128, 512], P(None, None, None, 'gx', 'gy'), may hold values from -6 to 6
- mon_adj: float32 [2, 3, 4, 128, 512], P(None, None, None, 'gx', 'gy'), may hold values from -6 to 6
Outputs:
- e_fwd_out: float32 [3, 128, 512, 256], P(None, 'gx', 'gy')
- h_fwd_out: float32 [3, 128, 512, 256], P(None, 'gx', 'gy')
- e_adj_out: float32 [3, 128, 512, 256], P(None, 'gx', 'gy')
- h_adj_out: float32 [3, 128, 512, 256], P(None, 'gx', 'gy')
- density_grad: float32 [4, 128, 512], P(None, 'gx', 'gy')
The draws below stay inside these ranges and needn't reach their ends.
Inputs may be any that keep to these rules, and one draw needn't show every extreme that they name: partner_map pairs cells of mirrored blocks one to one and is an involution: the partner of a cell's partner is the cell itself.
All inputs are finite; a program needn't handle non-finite values. No bound on the sum of `design_mask` on one device may be relied on, other than what follows from the above.
Results may differ from the reference program's by a relative error of at most 0.0003.
Values sent between devices are 32-bit elements; how exact they have to be, the bound alone decides.
No kernel may reach another device: no remote copies, remote signals or barrier semaphores. Data moves between devices by JAX's collectives and lax.ppermute only.
A program may use at most 64 MiB of HBM per device.

```python
import math
import jax
import jax.numpy as jnp
from jax import lax

CX = 4
CY = 32
PLANES = 4
STEPS = 2
Z0 = 126
NX = 128
NY = 512
NZ = 256
N_GX = 32
N_GY = 16


def draw_partner_map(key, part):
    key = jax.random.fold_in(key, 11)
    halves = N_GX // 2
    count = PLANES * CX * CY
    keys = jax.random.split(key, halves * N_GY)
    perms = jax.vmap(lambda single: jax.random.permutation(single, count))(keys)
    perms = perms.reshape(halves, N_GY, count).astype(jnp.int32)
    inverse = jnp.argsort(perms, axis=2, stable=True).astype(jnp.int32)
    full = jnp.concatenate([perms, inverse[::-1]], axis=0)
    shaped = full.reshape(N_GX, N_GY, PLANES, CX, CY).transpose(2, 0, 3, 1, 4)
    return shaped.reshape(PLANES, N_GX * CX, N_GY * CY).astype(jnp.int32)


def with_ends(result, rng, low, high):
    dims = result.shape
    index_at = [jax.random.randint(jax.random.fold_in(rng, axis), (), 0, dims[axis]) for axis in range(len(dims))]
    result = result.at[tuple(index_at)].set(low)
    longest = dims.index(max(dims))
    index_at[longest] = (index_at[longest] + 1) % dims[longest]
    return result.at[tuple(index_at)].set(high)


def levels(rng, extent, pieces, least, largest):
    def one(dim, blocks):
        heights = jax.random.uniform(jax.random.fold_in(jax.random.fold_in(rng, 6), dim), (blocks,), jnp.float32, least / len(pieces), largest / len(pieces))
        return jnp.repeat(jnp.exp(heights), extent[dim] // blocks).reshape((-1,) + (1,) * (len(extent) - dim - 1))

    gain = one(*pieces[0])
    for cut in pieces[1:]:
        gain = gain * one(*cut)
    return gain


def bell_draw(stream_key, dims, deviation, most, shards=(), dtype=jnp.bfloat16):
    array = deviation * jax.random.normal(stream_key, dims, jnp.float32)
    if shards:
        array = array * levels(stream_key, dims, shards, -0.22, 0.18)
    return jnp.clip(array, -most, most).astype(dtype)


def setup_inputs(seed: int = 0) -> dict:
    seeds = jax.random.split(jax.random.key(seed), 11)
    return {
        "e_fwd": bell_draw(seeds[0], (3, NX, NY, NZ), 1.0, 6.0, ((1, 32), (2, 16)), jnp.float32),
        "h_fwd": bell_draw(seeds[1], (3, NX, NY, NZ), 1.0, 6.0, ((1, 32), (2, 16)), jnp.float32),
        "e_adj": bell_draw(seeds[2], (3, NX, NY, NZ), 1.0, 6.0, ((1, 32), (2, 16)), jnp.float32),
        "h_adj": bell_draw(seeds[3], (3, NX, NY, NZ), 1.0, 6.0, ((1, 32), (2, 16)), jnp.float32),
        "eps_back": jnp.clip(1.0 + 11.0 * jax.random.uniform(seeds[4], (NX, NY, NZ), jnp.float32) ** levels(seeds[4], (NX, NY, NZ), ((0, 32), (1, 16)), -0.2, 0.2), 1.0, 12.0),
        "density": jnp.clip(1.0 * jax.random.uniform(seeds[5], (PLANES, NX, NY), jnp.float32) ** levels(seeds[5], (PLANES, NX, NY), ((1, 32), (2, 16)), -0.2, 0.2), 0.0, 1.0),
        "design_mask": with_ends((jax.random.randint(seeds[6], (PLANES, NX, NY), 0, 2) < 1).astype(jnp.int32), jax.random.fold_in(seeds[6], 1), 0, 1),
        "partner_map": draw_partner_map(jax.random.fold_in(seeds[10], 71), 0),
        "mon_fwd": bell_draw(seeds[8], (2, 3, PLANES, NX, NY), 1.0, 6.0, ((3, 32), (4, 16)), jnp.float32),
        "mon_adj": bell_draw(seeds[9], (2, 3, PLANES, NX, NY), 1.0, 6.0, ((3, 32), (4, 16)), jnp.float32),
    }


COURANT = 0.5
OMEGA = 0.7
CONTRAST = 10.0


def forward_diff(field, axis):
    widths = [(0, 0)] * field.ndim
    widths[axis] = (0, 1)
    extended = jnp.pad(field, widths)
    return lax.slice_in_dim(extended, 1, field.shape[axis] + 1, axis=axis) - field


def backward_diff(field, axis):
    widths = [(0, 0)] * field.ndim
    widths[axis] = (1, 0)
    extended = jnp.pad(field, widths)
    return field - lax.slice_in_dim(extended, 0, field.shape[axis], axis=axis)


def curl_forward(field):
    fx, fy, fz = field[0], field[1], field[2]
    return jnp.stack([forward_diff(fz, 1) - forward_diff(fy, 2),
                      forward_diff(fx, 2) - forward_diff(fz, 0),
                      forward_diff(fy, 0) - forward_diff(fx, 1)])


def curl_backward(field):
    fx, fy, fz = field[0], field[1], field[2]
    return jnp.stack([backward_diff(fz, 1) - backward_diff(fy, 2),
                      backward_diff(fx, 2) - backward_diff(fz, 0),
                      backward_diff(fy, 0) - backward_diff(fx, 1)])


def to_blocks(values):
    planes = values.shape[0]
    shaped = values.reshape(planes, N_GX, CX, N_GY, CY).transpose(1, 3, 0, 2, 4)
    return shaped.reshape(N_GX, N_GY, planes * CX * CY)


def from_blocks(blocks, planes):
    shaped = blocks.reshape(N_GX, N_GY, planes, CX, CY).transpose(2, 0, 3, 1, 4)
    return shaped.reshape(planes, N_GX * CX, N_GY * CY)


def mirror_pick(values, partner_map):
    flipped = to_blocks(values)[::-1]
    picked = jnp.take_along_axis(flipped, to_blocks(partner_map).astype(jnp.int32), axis=2)
    return from_blocks(picked, values.shape[0])


def leapfrog(electric, magnetic, eps):
    magnetic = magnetic - COURANT * curl_forward(electric)
    electric = electric + (COURANT / eps) * curl_backward(magnetic)
    return electric, magnetic


def slab_of(electric):
    return jnp.transpose(electric[:, :, :, Z0:Z0 + PLANES], (0, 3, 1, 2))


def reference(e_fwd, h_fwd, e_adj, h_adj, eps_back, density, design_mask, partner_map, mon_fwd, mon_adj):
    sym = 0.5 * (density + mirror_pick(density, partner_map))
    weight = CONTRAST * design_mask.astype(jnp.float32)
    slab_eps = jnp.transpose(eps_back[:, :, Z0:Z0 + PLANES], (2, 0, 1)) + weight * sym
    eps = eps_back.at[:, :, Z0:Z0 + PLANES].set(jnp.transpose(slab_eps, (1, 2, 0)))
    for step in range(STEPS):
        e_fwd, h_fwd = leapfrog(e_fwd, h_fwd, eps)
        e_adj, h_adj = leapfrog(e_adj, h_adj, eps)
        phase = OMEGA * (step + 1)
        cosine = math.cos(phase)
        sine = math.sin(phase)
        slab_f = slab_of(e_fwd)
        slab_a = slab_of(e_adj)
        mon_fwd = mon_fwd + jnp.stack([cosine * slab_f, -sine * slab_f])
        mon_adj = mon_adj + jnp.stack([cosine * slab_a, -sine * slab_a])
    local_grad = weight * jnp.sum(mon_fwd[0] * mon_adj[0] - mon_fwd[1] * mon_adj[1], axis=0)
    density_grad = 0.5 * (local_grad + mirror_pick(local_grad, partner_map))
    return e_fwd, h_fwd, e_adj, h_adj, density_grad
```

```python
import math

import jax
import jax.numpy as jnp
from jax import lax
from jax.experimental import pallas as pl
from jax.experimental.pallas import tpu as pltpu
from jax.sharding import PartitionSpec as P

PLANES = 4
Z0 = 126
COURANT = 0.5
OMEGA = 0.7
CONTRAST = 10.0
F32 = jnp.float32
VMEM_LIMIT = 24 * 1024 * 1024


def up_y(a, row):
    n = a.shape[0]
    at = lax.broadcasted_iota(jnp.int32, a.shape, 0)
    return jnp.where(at == n - 1, row, pltpu.roll(a, n - 1, 0))


def up_z(a):
    n = a.shape[1]
    at = lax.broadcasted_iota(jnp.int32, a.shape, 1)
    return jnp.where(at == n - 1, 0.0, pltpu.roll(a, n - 1, 1))


def down_y(a, row):
    at = lax.broadcasted_iota(jnp.int32, a.shape, 0)
    return jnp.where(at == 0, row, pltpu.roll(a, 1, 0))


def down_z(a):
    at = lax.broadcasted_iota(jnp.int32, a.shape, 1)
    return jnp.where(at == 0, 0.0, pltpu.roll(a, 1, 1))


def pick_z(nz):
    plane = lax.broadcasted_iota(jnp.int32, (8, nz), 0)
    z = lax.broadcasted_iota(jnp.int32, (8, nz), 1)
    return jnp.where((z == plane + Z0) & (plane < PLANES), 1.0, 0.0).astype(F32)


def face_low(ef, ea, xpay, ypay):
    nx = ef.shape[1]
    for f, e in enumerate((ef, ea)):
        for k, c in enumerate((1, 2)):
            xpay[f, k] = e[c, 0]
        for k, c in enumerate((0, 2)):
            for x in range(nx):
                r = (f * 2 + k) * nx + x
                ypay[pl.ds(r, 1), :] = e[c, x, pl.ds(0, 1), :]


def magnetic_kernel(ef, ea, hf, ha, xin, yin, of, oa, xpay, ypay):
    nx, ny = ef.shape[1], ef.shape[2]
    for f, (e, h, o) in enumerate(((ef, hf, of), (ea, ha, oa))):
        for x in range(nx):
            ex, ey, ez = e[0, x], e[1, x], e[2, x]
            ey_n = e[1, x + 1] if x + 1 < nx else xin[f, 0]
            ez_n = e[2, x + 1] if x + 1 < nx else xin[f, 1]
            row_x = yin[pl.ds((f * 2) * nx + x, 1), :]
            row_z = yin[pl.ds((f * 2 + 1) * nx + x, 1), :]
            hx = h[0, x] - COURANT * ((up_y(ez, row_z) - ez) - (up_z(ey) - ey))
            hy = h[1, x] - COURANT * ((up_z(ex) - ex) - (ez_n - ez))
            hz = h[2, x] - COURANT * ((ey_n - ey) - (up_y(ex, row_x) - ex))
            o[0, x] = hx
            o[1, x] = hy
            o[2, x] = hz
            if x == nx - 1:
                xpay[f, 0] = hy
                xpay[f, 1] = hz
            ypay[pl.ds((f * 2) * nx + x, 1), :] = hx[ny - 1:, :]
            ypay[pl.ds((f * 2 + 1) * nx + x, 1), :] = hz[ny - 1:, :]


def electric_step(ef, ea, hf, ha, coef, xin, yin, of, oa):
    nx = ef.shape[1]
    for f, (e, h, o) in enumerate(((ef, hf, of), (ea, ha, oa))):
        for x in range(nx):
            hx, hy, hz = h[0, x], h[1, x], h[2, x]
            hy_p = h[1, x - 1] if x else xin[f, 0]
            hz_p = h[2, x - 1] if x else xin[f, 1]
            row_x = yin[pl.ds((f * 2) * nx + x, 1), :]
            row_z = yin[pl.ds((f * 2 + 1) * nx + x, 1), :]
            k = coef[x]
            o[0, x] = e[0, x] + k * ((hz - down_y(hz, row_z)) - (hy - down_z(hy)))
            o[1, x] = e[1, x] + k * ((hx - down_z(hx)) - (hz - hz_p))
            o[2, x] = e[2, x] + k * ((hy - hy_p) - (hx - down_y(hx, row_x)))


def electric_kernel(ef, ea, hf, ha, coef, xin, yin, of, oa, xpay, ypay):
    electric_step(ef, ea, hf, ha, coef, xin, yin, of, oa)
    face_low(of, oa, xpay, ypay)


def slab_of(e, c, x, pick):
    return lax.dot_general(pick, e[c, x], (((1,), (1,)), ((), ())),
                           precision=lax.Precision.HIGHEST,
                           preferred_element_type=F32)[:PLANES]


def last_kernel(ef, ea, hf, ha, coef, xin, yin, mask, mon_f, mon_a, of, oa, grad):
    nx, nz = ef.shape[1], ef.shape[3]
    electric_step(ef, ea, hf, ha, coef, xin, yin, of, oa)
    pick = pick_z(nz)
    for x in range(nx):
        total = None
        for c in range(3):
            one_f, two_f = slab_of(ef, c, x, pick), slab_of(of, c, x, pick)
            one_a, two_a = slab_of(ea, c, x, pick), slab_of(oa, c, x, pick)
            cos = [math.cos(OMEGA), math.cos(2 * OMEGA)]
            sin = [math.sin(OMEGA), math.sin(2 * OMEGA)]
            re_f = mon_f[0, c, :, x, :] + cos[0] * one_f + cos[1] * two_f
            im_f = mon_f[1, c, :, x, :] - sin[0] * one_f - sin[1] * two_f
            re_a = mon_a[0, c, :, x, :] + cos[0] * one_a + cos[1] * two_a
            im_a = mon_a[1, c, :, x, :] - sin[0] * one_a - sin[1] * two_a
            term = re_f * re_a - im_f * im_a
            total = term if total is None else total + term
        grad[:, x, :] = CONTRAST * mask[:, x, :].astype(F32) * total


def mirror_take(other, partner, rows, index):
    planes, nx, ny = other.shape
    rows[...] = jnp.zeros_like(rows)
    index[...] = jnp.zeros_like(index)
    for p in range(planes):
        rows[pl.ds(p * nx, nx), pl.ds(0, ny)] = other[p]
        index[pl.ds(p * nx, nx), pl.ds(0, ny)] = partner[p]
    at = index[...]
    row, lane = at // ny, at % ny
    got = jnp.zeros(at.shape, F32)
    for r in range(planes * nx):
        line = jnp.broadcast_to(rows[pl.ds(r, 1), :], at.shape)
        got = jnp.where(row == r, jnp.take_along_axis(line, lane, axis=1), got)
    return got


def coef_kernel(eps, density, mask, partner, other, coef, rows, index):
    nx, ny, nz = eps.shape
    got = mirror_take(other, partner, rows, index)
    rows[...] = got
    pick = pick_z(nz)[:PLANES]
    for x in range(nx):
        theirs = jnp.concatenate([rows[pl.ds(p * nx + x, 1), pl.ds(0, ny)] for p in range(PLANES)], 0)
        sym = 0.5 * (density[:, x, :] + theirs)
        extra = CONTRAST * mask[:, x, :].astype(F32) * sym
        spread = lax.dot_general(extra, pick, (((0,), (0,)), ((), ())),
                                 precision=lax.Precision.HIGHEST, preferred_element_type=F32)
        coef[x] = COURANT / (eps[x] + spread)


def gradient_kernel(grad, partner, other, out, rows, index):
    nx, ny = grad.shape[1], grad.shape[2]
    got = mirror_take(other, partner, rows, index)
    rows[...] = got
    for p in range(PLANES):
        out[p] = 0.5 * (grad[p] + rows[pl.ds(p * nx, nx), pl.ds(0, ny)])


def call(kernel, outs, args, scratch=(), name=None, nbytes=4_000_000, flops=4_000_000):
    return pl.pallas_call(
        kernel,
        out_shape=outs,
        in_specs=[pl.BlockSpec(memory_space=pltpu.VMEM)] * len(args),
        out_specs=[pl.BlockSpec(memory_space=pltpu.VMEM)] * len(outs),
        scratch_shapes=list(scratch),
        compiler_params=pltpu.CompilerParams(vmem_limit_bytes=VMEM_LIMIT),
        cost_estimate=pl.CostEstimate(flops=flops, bytes_accessed=nbytes, transcendentals=0),
        name=name,
    )(*args)


def shifted(block, axis, distance):
    devices = range(lax.axis_size(axis))
    return lax.ppermute(block, axis, [(i - distance, i) for i in devices if i - distance in devices])


def mirrored(block, axis):
    size = lax.axis_size(axis)
    return lax.ppermute(block, axis, [(i, size - 1 - i) for i in range(size)])


def per_device(e_fwd, h_fwd, e_adj, h_adj, eps_back, density, design_mask, partner_map, mon_fwd, mon_adj):
    _, nx, ny, nz = e_fwd.shape
    field = jax.ShapeDtypeStruct(e_fwd.shape, F32)
    xface = jax.ShapeDtypeStruct((2, 2, ny, nz), F32)
    yface = jax.ShapeDtypeStruct((4 * nx, nz), F32)
    slab = jax.ShapeDtypeStruct(density.shape, F32)
    picks = [pltpu.VMEM((PLANES * nx, 128), F32), pltpu.VMEM((PLANES * nx, 128), jnp.int32)]

    other = mirrored(density, "gx")

    xpay, ypay = call(face_low, [xface, yface], [e_fwd, e_adj], name="faces")
    yin, xin = shifted(ypay, "gy", -1), shifted(xpay, "gx", -1)
    hf, ha, xpay, ypay = call(magnetic_kernel, [field, field, xface, yface],
                              [e_fwd, e_adj, h_fwd, h_adj, xin, yin], name="magnetic_1")
    yin, xin = shifted(ypay, "gy", 1), shifted(xpay, "gx", 1)
    coef, = call(coef_kernel, [jax.ShapeDtypeStruct(eps_back.shape, F32)],
                 [eps_back, density, design_mask, partner_map, other], picks, name="coefficient")
    ef, ea, xpay, ypay = call(electric_kernel, [field, field, xface, yface],
                              [e_fwd, e_adj, hf, ha, coef, xin, yin], name="electric_1")
    yin, xin = shifted(ypay, "gy", -1), shifted(xpay, "gx", -1)
    hf, ha, xpay, ypay = call(magnetic_kernel, [field, field, xface, yface],
                              [ef, ea, hf, ha, xin, yin], name="magnetic_2")
    yin, xin = shifted(ypay, "gy", 1), shifted(xpay, "gx", 1)
    ef, ea, grad = call(last_kernel, [field, field, slab],
                        [ef, ea, hf, ha, coef, xin, yin, design_mask, mon_fwd, mon_adj], name="electric_2")
    theirs = mirrored(grad, "gx")
    density_grad, = call(gradient_kernel, [slab], [grad, partner_map, theirs], picks, name="gradient")
    return ef, hf, ea, ha, density_grad


def solution(mesh):
    grid = P(None, "gx", "gy", None)
    slab = P(None, "gx", "gy")
    monitor = P(None, None, None, "gx", "gy")
    return jax.shard_map(
        per_device,
        mesh=mesh,
        in_specs=(grid, grid, grid, grid, P("gx", "gy", None), slab, slab, slab, monitor, monitor),
        out_specs=(grid, grid, grid, grid, slab),
        check_vma=False,
    )
```

```python
import math

import jax
import jax.numpy as jnp
from jax import lax
from jax.experimental import pallas as pl
from jax.experimental.pallas import tpu as pltpu
from jax.sharding import PartitionSpec as P

PLANES = 4
Z0 = 126
COURANT = 0.5
OMEGA = 0.7
CONTRAST = 10.0
F32 = jnp.float32
VMEM_LIMIT = 32 * 1024 * 1024

LANES = 128
FRAME = 48
TOP, END = 8, 40
WINDOW = 8
SHIFT = LANES - (Z0 - 2)
ROW_EPS, ROW_MON, MESSAGE = 96, 128, 192


def lane_of(shape):
    return lax.broadcasted_iota(jnp.int32, shape, len(shape) - 1)


def row_of(shape):
    return lax.broadcasted_iota(jnp.int32, shape, len(shape) - 2)


def turn(a, shift):
    shift = shift % a.shape[1]
    return pltpu.roll(a, shift, 1) if shift else a


def up_y(a):
    return pltpu.roll(a, a.shape[0] - 1, 0)


def down_y(a):
    return pltpu.roll(a, 1, 0)


def up_z(a):
    n = a.shape[1]
    return jnp.where(lane_of(a.shape) == n - 1, 0.0, pltpu.roll(a, n - 1, 1))


def down_z(a):
    return jnp.where(lane_of(a.shape) == 0, 0.0, pltpu.roll(a, 1, 1))


def pack_planes(planes):
    total = None
    for offset, plane in planes:
        near = jnp.where(lane_of((plane.shape[0], LANES)) >= LANES // 2,
                         plane[:, :LANES], plane[:, LANES:2 * LANES])
        part = turn(near, SHIFT + offset)
        lane = lane_of(part.shape)
        inside = (lane >= offset) & (lane < offset + WINDOW)
        total = jnp.where(inside, part, 0.0 if total is None else total)
    return total


def flipped(a, square):
    square[...] = jnp.zeros_like(square)
    square[pl.ds(0, a.shape[0]), pl.ds(0, a.shape[1])] = a
    return jnp.transpose(square[...])


def load_kernel(ef, hf, ea, ha, eps, density, mask, partner, mon_f, mon_a,
                message, fields, eps_out,
                small_f, small_i, mons, square, sems):
    nx, ny = ef.shape[1], ef.shape[2]
    copies = []
    for f, (e, h) in enumerate(((ef, hf), (ea, ha))):
        for k, source in enumerate((e, h)):
            copies.append(pltpu.make_async_copy(
                source, fields.at[f, k], sems.at[2 * f + k]))
    copies.append(pltpu.make_async_copy(eps, eps_out, sems.at[4]))
    copies.append(pltpu.make_async_copy(density, small_f, sems.at[5]))
    copies.append(pltpu.make_async_copy(mask, small_i.at[0], sems.at[6]))
    copies.append(pltpu.make_async_copy(partner, small_i.at[1], sems.at[7]))
    copies.append(pltpu.make_async_copy(mon_f, mons.at[0], sems.at[8]))
    copies.append(pltpu.make_async_copy(mon_a, mons.at[1], sems.at[9]))
    for copy in copies:
        copy.start()
    message[pl.ds(ROW_EPS, MESSAGE - ROW_EPS), :] = jnp.zeros((MESSAGE - ROW_EPS, LANES), F32)
    for copy in copies[4:]:
        copy.wait()
    for half, components in ((0, (0, 1)), (1, (2,))):
        square[...] = jnp.zeros_like(square)
        for k, c in enumerate(components):
            for f in range(2):
                for x in range(nx):
                    base = k * 64 + x * 16 + f * 8 + 2
                    square[pl.ds(base, PLANES), pl.ds(0, ny)] = mons[f, 0, c, :, x, :]
                    for p in range(PLANES):
                        at = (base + 4 + p) % LANES
                        square[pl.ds(at, 1), pl.ds(0, ny)] = mons[f, 1, c, p, pl.ds(x, 1), :]
        message[pl.ds(ROW_MON + 32 * half, ny), :] = jnp.transpose(square[...])[:ny]
    own_eps = [(x * 16 + f * 8, eps_out[x]) for x in range(nx) for f in range(2)]
    square[...] = jnp.zeros_like(square)
    for p in range(PLANES):
        square[pl.ds(p * nx, nx), pl.ds(0, ny)] = CONTRAST * small_i[0, p].astype(F32)
        square[pl.ds(16 + p * nx, nx), pl.ds(0, ny)] = small_f[p]
        square[pl.ds(32 + p * nx, nx), pl.ds(0, ny)] = small_i[1, p].astype(F32)
    small = turn(square[pl.ds(0, 32), :], 64)
    index = turn(square[pl.ds(32, 32), :], 96)
    message[pl.ds(ROW_EPS, ny), :] = pack_planes(own_eps) + small + index
    for copy in copies[:4]:
        copy.wait()
    for c in range(3):
        message[pl.ds(c * 32, ny), :] = pack_planes(
            [(k * 64 + x * 16 + f * 8, fields[f, k, c, x])
             for k in range(2) for x in range(nx) for f in range(2)])


def small_parts(message):
    weight = turn(message[pl.ds(ROW_EPS, 16), :], -64)
    density = turn(message[pl.ds(ROW_EPS + 16, 16), :], -64)
    partner = turn(message[pl.ds(ROW_EPS, 16), :], -96)
    return weight, density, partner


def mirror_take(table, partner, ny):
    inside = lane_of(partner.shape) < ny
    at = jnp.where(inside, partner, 0.0).astype(jnp.int32)
    row, lane = at // ny, at % ny
    got = jnp.zeros(at.shape, F32)
    for r in range(table.shape[0]):
        line = jnp.broadcast_to(table[pl.ds(r, 1), :], at.shape)
        got = jnp.where(row == r, jnp.take_along_axis(line, lane, axis=1), got)
    return got


def spread_slab(values, lines, square, nx, ny):
    lines[...] = values
    square[...] = jnp.zeros_like(square)
    for p in range(PLANES):
        for x in range(nx):
            row = lines[pl.ds(p * nx + x, 1), :]
            square[pl.ds(x * 16 + 2 + p, 1), :] = row
            square[pl.ds(x * 16 + 10 + p, 1), :] = row
    return jnp.transpose(square[...])[:ny]


def coef_kernel(eps, mine, theirs, fields, coef, mirror_coef, y_up, y_down, table, lines, square):
    nx = eps.shape[0]
    ny = END - TOP
    weight, density, partner = small_parts(mine)
    weight_m, density_m, partner_m = small_parts(theirs)
    table[...] = density_m
    extra = weight * (0.5 * (density + mirror_take(table, partner, ny)))
    table[...] = density
    extra_m = weight_m * (0.5 * (density_m + mirror_take(table, partner_m, ny)))
    packed = spread_slab(extra, lines, square, nx, ny)
    lane = lane_of(packed.shape)
    for x in range(nx):
        part = turn(packed, -16 * x - SHIFT)
        low = jnp.where(lane >= Z0, part, 0.0)
        high = jnp.where(lane < Z0 + PLANES - LANES, part, 0.0)
        coef[x] = COURANT / (eps[x] + jnp.concatenate([low, high], 1))
    packed = theirs[pl.ds(ROW_EPS, ny), :] + spread_slab(extra_m, lines, square, nx, ny)
    mirror_coef[...] = jnp.where(lane < 64, COURANT / jnp.where(lane < 64, packed, 1.0), 0.0)
    for out, first in ((y_up, ny - 2), (y_down, 0)):
        at = 0
        for f in range(2):
            for k in range(2):
                for c in range(3):
                    for x in range(nx):
                        out[pl.ds(at, 2), :] = fields[f, k, c, x, pl.ds(first, 2), :]
                        at += 2
        for x in range(nx):
            out[pl.ds(at, 2), :] = coef[x, pl.ds(first, 2), :]
            at += 2
        out[pl.ds(at, 8), :] = jnp.zeros((8, out.shape[1]), F32)
        for c in range(3):
            out[pl.ds(at, 2), pl.ds(0, LANES)] = theirs[pl.ds(c * 32 + first, 2), :]
            at += 2
        out[pl.ds(at, 2), pl.ds(0, LANES)] = mirror_coef[pl.ds(first, 2), :]


def plane_index(f, k, c, x, nx):
    return ((f * 2 + k) * 3 + c) * nx + x


def framed(middle, tops, ends, i):
    return jnp.concatenate([tops[i], middle, ends[i]], 0)


def edges_kernel(fields, coef, mirror_coef, theirs, y_low, y_high,
                 tops, ends, mirror, x_up, x_down):
    nx, ny = coef.shape[0], coef.shape[1]
    tops[...] = jnp.zeros_like(tops)
    ends[...] = jnp.zeros_like(ends)
    mirror[...] = jnp.zeros_like(mirror)
    for c in range(3):
        mirror[c, pl.ds(TOP, ny), :] = theirs[pl.ds(c * 32, ny), :]
    mirror[3, pl.ds(TOP, ny), :] = mirror_coef[...]
    for source, out, first in ((y_low, tops, TOP - 2), (y_high, ends, 0)):
        for i in range(13 * nx):
            out[i, pl.ds(first, 2), :] = source[pl.ds(2 * i, 2), :]
        for c in range(4):
            row = TOP - 2 if out is tops else END
            mirror[c, pl.ds(row, 2), :] = source[pl.ds(26 * nx + 2 * c, 2), pl.ds(0, LANES)]

    def put(out, plane, value):
        out[pl.ds(plane * ny, ny), :] = value[TOP:END]
        out[pl.ds(10 * ny + 4 * plane, 2), :] = value[TOP - 2:TOP]
        out[pl.ds(10 * ny + 4 * plane + 2, 2), :] = value[END:END + 2]

    def part(f, k, c, x):
        return framed(fields[f, k, c, x], tops, ends, plane_index(f, k, c, x, nx))

    ks = [framed(coef[x], tops, ends, 12 * nx + x) for x in range(nx)]
    last = nx - 1
    for f in range(2):
        e = lambda c, x: part(f, 0, c, x)
        h = lambda c, x: part(f, 1, c, x)
        k, before = ks[last], ks[last - 1] > 0
        inside = k > 0
        ex, ey, ez = e(0, last), e(1, last), e(2, last)
        ex_b, ey_b, ez_b = e(0, last - 1), e(1, last - 1), e(2, last - 1)
        hy_b = jnp.where(before, h(1, last - 1) - COURANT * ((up_z(ex_b) - ex_b) - (ez - ez_b)), 0.0)
        hz_b = jnp.where(before, h(2, last - 1) - COURANT * ((ey - ey_b) - (up_y(ex_b) - ex_b)), 0.0)
        hx = jnp.where(inside, h(0, last) - COURANT * ((up_y(ez) - ez) - (up_z(ey) - ey)), 0.0)
        hy = jnp.where(inside, h(1, last) - COURANT * ((up_z(ex) - ex) + ez), 0.0)
        hz = jnp.where(inside, h(2, last) - COURANT * (-ey - (up_y(ex) - ex)), 0.0)
        ex = ex + k * ((hz - down_y(hz)) - (hy - down_z(hy)))
        ey = ey + k * ((hx - down_z(hx)) - (hz - hz_b))
        ez = ez + k * ((hy - hy_b) - (hx - down_y(hx)))
        put(x_up, 4 * f, hy)
        put(x_up, 4 * f + 1, hz)
        put(x_up, 4 * f + 2, jnp.where(inside, hy - COURANT * ((up_z(ex) - ex) + ez), 0.0))
        put(x_up, 4 * f + 3, jnp.where(inside, hz - COURANT * (-ey - (up_y(ex) - ex)), 0.0))
        k = ks[0]
        inside = k > 0
        ex, ey, ez = e(0, 0), e(1, 0), e(2, 0)
        hx = jnp.where(inside, h(0, 0) - COURANT * ((up_y(ez) - ez) - (up_z(ey) - ey)), 0.0)
        hy = jnp.where(inside, h(1, 0) - COURANT * ((up_z(ex) - ex) - (e(2, 1) - ez)), 0.0)
        hz = jnp.where(inside, h(2, 0) - COURANT * ((e(1, 1) - ey) - (up_y(ex) - ex)), 0.0)
        put(x_down, 4 * f, ey)
        put(x_down, 4 * f + 1, ez)
        put(x_down, 4 * f + 2, ey + k * ((hx - down_z(hx)) - hz))
        put(x_down, 4 * f + 3, ez + k * (hy - (hx - down_y(hx))))
    put(x_up, 8, ks[last])
    put(x_down, 8, ks[0])
    m = [mirror[c] for c in range(3)]
    km = mirror[3]
    first = lane_of(km.shape) % 64 < 32
    put(x_up, 9, jnp.concatenate([jnp.where(first, m[0], turn(m[1], 32)),
                                  jnp.where(first, m[2], turn(km, 32))], 1))
    put(x_down, 9, jnp.concatenate([jnp.where(first, turn(m[1], -32), m[0]),
                                    jnp.where(first, turn(km, -32), m[2])], 1))


def slab_gradient(message, first, second, ny):
    total = None
    for c in range(3):
        mon = message[pl.ds(ROW_MON + 32 * (c // 2), ny), :]
        real = turn(mon, -64 * (c % 2))
        imag = turn(real, -4)
        real = real + math.cos(OMEGA) * first[c] + math.cos(2 * OMEGA) * second[c]
        imag = imag - math.sin(OMEGA) * first[c] - math.sin(2 * OMEGA) * second[c]
        term = real * turn(real, -8) - imag * turn(imag, -8)
        total = term if total is None else total + term
    return total


def slab_rows(packed, out, square, nx):
    square[...] = flipped(packed, square)
    for p in range(PLANES):
        for x in range(nx):
            out[pl.ds(p * nx + x, 1), :] = square[pl.ds(x * 16 + 2 + p, 1), :]


def step_kernel(fields, coef, tops, ends, mirror, x_low, x_high, mine, theirs,
                ef_out, hf_out, ea_out, ha_out, grad,
                ee, hh, halo, square, table, lines, sems):
    nx, ny, nz = coef.shape

    def take(source, plane, slot):
        halo[slot, pl.ds(0, TOP), :] = jnp.zeros((TOP, nz), F32)
        halo[slot, pl.ds(END, TOP), :] = jnp.zeros((TOP, nz), F32)
        halo[slot, pl.ds(TOP, ny), :] = source[pl.ds(plane * ny, ny), :]
        halo[slot, pl.ds(TOP - 2, 2), :] = source[pl.ds(10 * ny + 4 * plane, 2), :]
        halo[slot, pl.ds(END, 2), :] = source[pl.ds(10 * ny + 4 * plane + 2, 2), :]

    for plane in range(10):
        take(x_low, plane, plane)
        take(x_high, plane, 10 + plane)
    k_low, k_high = halo[8], halo[18]

    def part(f, k, c, x):
        return framed(fields[f, k, c, x], tops, ends, plane_index(f, k, c, x, nx))

    def inverse(x):
        return framed(coef[x], tops, ends, 12 * nx + x)

    copies = []
    first_slab, second_slab = [], []
    for f in range(2):
        ey0, ez0 = part(f, 0, 1, 0), part(f, 0, 2, 0)
        dhy = jnp.where(k_low > 0, COURANT * ez0, 0.0)
        dhz = jnp.where(k_low > 0, -COURANT * ey0, 0.0)
        hh[f, 1, 0] = halo[4 * f] + dhy
        hh[f, 2, 0] = halo[4 * f + 1] + dhz
        for x in range(nx):
            inside = inverse(x) > 0
            ex, ey, ez = part(f, 0, 0, x), part(f, 0, 1, x), part(f, 0, 2, x)
            ey_n = part(f, 0, 1, x + 1) if x + 1 < nx else halo[10 + 4 * f]
            ez_n = part(f, 0, 2, x + 1) if x + 1 < nx else halo[10 + 4 * f + 1]
            hx, hy, hz = part(f, 1, 0, x), part(f, 1, 1, x), part(f, 1, 2, x)
            hh[f, 0, x + 1] = jnp.where(inside, hx - COURANT * ((up_y(ez) - ez) - (up_z(ey) - ey)), 0.0)
            hh[f, 1, x + 1] = jnp.where(inside, hy - COURANT * ((up_z(ex) - ex) - (ez_n - ez)), 0.0)
            hh[f, 2, x + 1] = jnp.where(inside, hz - COURANT * ((ey_n - ey) - (up_y(ex) - ex)), 0.0)
        for x in range(nx):
            k = inverse(x)
            hx, hy, hz = hh[f, 0, x + 1], hh[f, 1, x + 1], hh[f, 2, x + 1]
            ee[f, 0, x] = part(f, 0, 0, x) + k * ((hz - down_y(hz)) - (hy - down_z(hy)))
            ee[f, 1, x] = part(f, 0, 1, x) + k * ((hx - down_z(hx)) - (hz - hh[f, 2, x]))
            ee[f, 2, x] = part(f, 0, 2, x) + k * ((hy - hh[f, 1, x]) - (hx - down_y(hx)))
        ee[f, 1, nx] = halo[10 + 4 * f + 2] + k_high * hh[f, 2, nx]
        ee[f, 2, nx] = halo[10 + 4 * f + 3] - k_high * hh[f, 1, nx]
        dex = k_low * ((dhz - down_y(dhz)) - (dhy - down_z(dhy)))
        dey = -k_low * dhz
        dez = k_low * dhy
        hh[f, 1, 0] = jnp.where(
            k_low > 0, halo[4 * f + 2] + dhy - COURANT * ((up_z(dex) - dex) - (ee[f, 2, 0] - dez)), 0.0)
        hh[f, 2, 0] = jnp.where(
            k_low > 0, halo[4 * f + 3] + dhz - COURANT * ((ee[f, 1, 0] - dey) - (up_y(dex) - dex)), 0.0)
        for x in range(nx):
            inside = inverse(x) > 0
            ex, ey, ez = ee[f, 0, x], ee[f, 1, x], ee[f, 2, x]
            hh[f, 0, x + 1] = jnp.where(
                inside, hh[f, 0, x + 1] - COURANT * ((up_y(ez) - ez) - (up_z(ey) - ey)), 0.0)
            hh[f, 1, x + 1] = jnp.where(
                inside, hh[f, 1, x + 1] - COURANT * ((up_z(ex) - ex) - (ee[f, 2, x + 1] - ez)), 0.0)
            hh[f, 2, x + 1] = jnp.where(
                inside, hh[f, 2, x + 1] - COURANT * ((ee[f, 1, x + 1] - ey) - (up_y(ex) - ex)), 0.0)
        copies.append(pltpu.make_async_copy(
            hh.at[f, :, pl.ds(1, nx), pl.ds(TOP, ny), :], (hf_out, ha_out)[f], sems.at[2 * f]))
        copies[-1].start()
    for c in range(3):
        first_slab.append(pack_planes([(x * 16 + f * 8, ee[f, c, x, pl.ds(TOP, ny), :])
                                       for x in range(nx) for f in range(2)]))
    for f in range(2):
        for x in range(nx):
            k = inverse(x)
            hx, hy, hz = hh[f, 0, x + 1], hh[f, 1, x + 1], hh[f, 2, x + 1]
            ee[f, 0, x] = ee[f, 0, x] + k * ((hz - down_y(hz)) - (hy - down_z(hy)))
            ee[f, 1, x] = ee[f, 1, x] + k * ((hx - down_z(hx)) - (hz - hh[f, 2, x]))
            ee[f, 2, x] = ee[f, 2, x] + k * ((hy - hh[f, 1, x]) - (hx - down_y(hx)))
        copies.append(pltpu.make_async_copy(
            ee.at[f, :, pl.ds(0, nx), pl.ds(TOP, ny), :], (ef_out, ea_out)[f], sems.at[2 * f + 1]))
        copies[-1].start()
    for c in range(3):
        second_slab.append(pack_planes([(x * 16 + f * 8, ee[f, c, x, pl.ds(TOP, ny), :])
                                        for x in range(nx) for f in range(2)]))
    own = slab_gradient(mine, first_slab, second_slab, ny)

    low01, low2 = halo[9, :, pl.ds(0, LANES)], halo[9, :, pl.ds(LANES, LANES)]
    high01, high2 = halo[19, :, pl.ds(0, LANES)], halo[19, :, pl.ds(LANES, LANES)]
    lane = lane_of(low01.shape)

    def join(below, middle, above):
        return jnp.where(lane < 32, below, jnp.where(lane < 96, middle, above))

    m = [mirror[c] for c in range(3)]
    e = [join(turn(high01, -32), turn(m[0], 32), turn(low01, 96)),
         join(high01, turn(m[1], 32), turn(low01, 64)),
         join(turn(high2, -32), turn(m[2], 32), turn(low2, 96))]
    h = [join(turn(high01, -96), turn(m[0], -32), turn(low01, 32)),
         join(turn(high01, -64), turn(m[1], -32), low01),
         join(turn(high2, -96), turn(m[2], -32), turn(low2, 32))]
    k = join(high2, turn(mirror[3], 32), turn(low2, 64))
    inside = k > 0

    def ahead(a, axis):
        return (turn(a, -16), up_y(a), turn(a, -1))[axis] - a

    def behind(a, axis):
        return a - (turn(a, 16), down_y(a), turn(a, 1))[axis]

    slabs = []
    for _ in range(2):
        h = [jnp.where(inside, h[c] - COURANT * (ahead(e[(c + 2) % 3], (c + 1) % 3)
                                                 - ahead(e[(c + 1) % 3], (c + 2) % 3)), 0.0)
             for c in range(3)]
        e = [e[c] + k * (behind(h[(c + 2) % 3], (c + 1) % 3) - behind(h[(c + 1) % 3], (c + 2) % 3))
             for c in range(3)]
        slabs.append([turn(e[c], -32)[TOP:END] for c in range(3)])
    other = slab_gradient(theirs, slabs[0], slabs[1], ny)

    weight, _, partner = small_parts(mine)
    weight_m, _, _ = small_parts(theirs)
    slab_rows(other, table, square, nx)
    table[...] = table[...] * weight_m
    got = mirror_take(table, partner, ny)
    slab_rows(own, lines, square, nx)
    lines[...] = 0.5 * (lines[...] * weight + got)
    for p in range(PLANES):
        grad[p] = lines[pl.ds(p * nx, nx), pl.ds(0, ny)]
    for copy in copies:
        copy.wait()


def call(kernel, outs, args, scratch=(), name=None, any_in=False, any_out=0):
    spaces = lambda count, far: [pl.BlockSpec(memory_space=pltpu.HBM if i < far else pltpu.VMEM)
                                 for i in range(count)]
    return pl.pallas_call(
        kernel,
        out_shape=outs,
        in_specs=spaces(len(args), len(args) if any_in else 0),
        out_specs=spaces(len(outs), any_out),
        scratch_shapes=list(scratch),
        compiler_params=pltpu.CompilerParams(vmem_limit_bytes=VMEM_LIMIT),
        cost_estimate=pl.CostEstimate(flops=4_000_000, bytes_accessed=4_000_000, transcendentals=0),
        name=name,
    )(*args)


def shifted(block, axis, distance):
    devices = range(lax.axis_size(axis))
    return lax.ppermute(block, axis, [(i - distance, i) for i in devices if i - distance in devices])


def mirrored(block, axis):
    size = lax.axis_size(axis)
    return lax.ppermute(block, axis, [(i, size - 1 - i) for i in range(size)])


def per_device(e_fwd, h_fwd, e_adj, h_adj, eps_back, density, design_mask, partner_map, mon_fwd, mon_adj):
    _, nx, ny, nz = e_fwd.shape
    shape = lambda *dims: jax.ShapeDtypeStruct(dims, F32)
    vmem = lambda *dims: pltpu.VMEM(dims, F32)
    square = vmem(LANES, LANES)
    lines = vmem(PLANES * nx, LANES)
    fields_shape = shape(2, 2, 3, nx, ny, nz)
    block = shape(nx, ny, nz)

    mine, fields, eps = call(
        load_kernel, [shape(MESSAGE, LANES), fields_shape, block],
        [e_fwd, h_fwd, e_adj, h_adj, eps_back, density, design_mask, partner_map, mon_fwd, mon_adj],
        [vmem(*density.shape), pltpu.VMEM((2,) + density.shape, jnp.int32), vmem(2, *mon_fwd.shape),
         square, pltpu.SemaphoreType.DMA((10,))], name="load", any_in=True)
    theirs = mirrored(mine, "gx")
    y_shape = shape(2 * (13 * nx) + 8, nz)
    coef, mirror_coef, y_up, y_down = call(
        coef_kernel, [block, shape(ny, LANES), y_shape, y_shape], [eps, mine, theirs, fields],
        [lines, lines, square], name="coefficient")
    y_low, y_high = shifted(y_up, "gy", 1), shifted(y_down, "gy", -1)
    x_shape = shape(10 * (ny + 4), nz)
    tile = shape(13 * nx, 8, nz)
    tops, ends, mirror, x_up, x_down = call(
        edges_kernel, [tile, tile, shape(4, FRAME, LANES), x_shape, x_shape],
        [fields, coef, mirror_coef, theirs, y_low, y_high], name="edges")
    x_low, x_high = shifted(x_up, "gx", 1), shifted(x_down, "gx", -1)
    ef, hf, ea, ha, grad = call(
        step_kernel, [shape(*e_fwd.shape)] * 4 + [shape(*density.shape)],
        [fields, coef, tops, ends, mirror, x_low, x_high, mine, theirs],
        [vmem(2, 3, nx + 1, FRAME, nz), vmem(2, 3, nx + 1, FRAME, nz), vmem(20, FRAME, nz),
         square, lines, lines, pltpu.SemaphoreType.DMA((4,))], name="steps", any_out=4)
    return ef, hf, ea, ha, grad


def solution(mesh):
    grid = P(None, "gx", "gy", None)
    slab = P(None, "gx", "gy")
    monitor = P(None, None, None, "gx", "gy")
    return jax.shard_map(
        per_device,
        mesh=mesh,
        in_specs=(grid, grid, grid, grid, P("gx", "gy", None), slab, slab, slab, monitor, monitor),
        out_specs=(grid, grid, grid, grid, slab),
        check_vma=False,
    )
```

```python
import math

import jax
import jax.numpy as jnp
from jax import lax
from jax.experimental import pallas as pl
from jax.experimental.pallas import tpu as pltpu
from jax.sharding import PartitionSpec as P

PLANES = 4
Z0 = 126
COURANT = 0.5
OMEGA = 0.7
CONTRAST = 10.0
F32 = jnp.float32
VMEM_LIMIT = 32 * 1024 * 1024
FAR_LIMIT = 60 * 1024 * 1024

LANES = 128
FRAME = 48
TOP, END = 8, 40
WINDOW = 8
SHIFT = LANES - (Z0 - 2)
ROW_EPS, ROW_MON, MESSAGE = 96, 128, 192


def lane_of(shape):
    return lax.broadcasted_iota(jnp.int32, shape, len(shape) - 1)


def row_of(shape):
    return lax.broadcasted_iota(jnp.int32, shape, len(shape) - 2)


def turn(a, shift):
    shift = shift % a.shape[1]
    return pltpu.roll(a, shift, 1) if shift else a


def up_y(a):
    return pltpu.roll(a, a.shape[0] - 1, 0)


def down_y(a):
    return pltpu.roll(a, 1, 0)


def up_z(a):
    n = a.shape[1]
    return jnp.where(lane_of(a.shape) == n - 1, 0.0, pltpu.roll(a, n - 1, 1))


def down_z(a):
    return jnp.where(lane_of(a.shape) == 0, 0.0, pltpu.roll(a, 1, 1))


def pack_planes(planes):
    total = None
    for offset, plane in planes:
        near = jnp.where(lane_of((plane.shape[0], LANES)) >= LANES // 2,
                         plane[:, :LANES], plane[:, LANES:2 * LANES])
        part = turn(near, SHIFT + offset)
        lane = lane_of(part.shape)
        inside = (lane >= offset) & (lane < offset + WINDOW)
        total = jnp.where(inside, part, 0.0 if total is None else total)
    return total


def flipped(a, square):
    square[...] = jnp.zeros_like(square)
    square[pl.ds(0, a.shape[0]), pl.ds(0, a.shape[1])] = a
    return jnp.transpose(square[...])


def message_kernel(ef, hf, ea, ha, eps, density, mask, partner, mon_f, mon_a, message,
                   fields, eps_in, small_f, small_i, mons, square, sems):
    nx, ny = ef.shape[1], ef.shape[2]
    copies = []
    for f, (e, h) in enumerate(((ef, hf), (ea, ha))):
        for k, source in enumerate((e, h)):
            copies.append(pltpu.make_async_copy(source, fields.at[f, k], sems.at[2 * f + k]))
    copies.append(pltpu.make_async_copy(eps, eps_in, sems.at[4]))
    copies.append(pltpu.make_async_copy(density, small_f, sems.at[5]))
    copies.append(pltpu.make_async_copy(mask, small_i.at[0], sems.at[6]))
    copies.append(pltpu.make_async_copy(partner, small_i.at[1], sems.at[7]))
    copies.append(pltpu.make_async_copy(mon_f, mons.at[0], sems.at[8]))
    copies.append(pltpu.make_async_copy(mon_a, mons.at[1], sems.at[9]))
    for copy in copies:
        copy.start()
    message[pl.ds(ROW_EPS, MESSAGE - ROW_EPS), :] = jnp.zeros((MESSAGE - ROW_EPS, LANES), F32)
    for copy in copies[4:]:
        copy.wait()
    for half, components in ((0, (0, 1)), (1, (2,))):
        square[...] = jnp.zeros_like(square)
        for k, c in enumerate(components):
            for f in range(2):
                for x in range(nx):
                    base = k * 64 + x * 16 + f * 8 + 2
                    square[pl.ds(base, PLANES), pl.ds(0, ny)] = mons[f, 0, c, :, x, :]
                    for p in range(PLANES):
                        at = (base + 4 + p) % LANES
                        square[pl.ds(at, 1), pl.ds(0, ny)] = mons[f, 1, c, p, pl.ds(x, 1), :]
        message[pl.ds(ROW_MON + 32 * half, ny), :] = jnp.transpose(square[...])[:ny]
    own_eps = [(x * 16 + f * 8, eps_in[x]) for x in range(nx) for f in range(2)]
    square[...] = jnp.zeros_like(square)
    for p in range(PLANES):
        square[pl.ds(p * nx, nx), pl.ds(0, ny)] = CONTRAST * small_i[0, p].astype(F32)
        square[pl.ds(16 + p * nx, nx), pl.ds(0, ny)] = small_f[p]
        square[pl.ds(32 + p * nx, nx), pl.ds(0, ny)] = small_i[1, p].astype(F32)
    small = turn(square[pl.ds(0, 32), :], 64)
    index = turn(square[pl.ds(32, 32), :], 96)
    message[pl.ds(ROW_EPS, ny), :] = pack_planes(own_eps) + small + index
    for copy in copies[:4]:
        copy.wait()
    for c in range(3):
        message[pl.ds(c * 32, ny), :] = pack_planes(
            [(k * 64 + x * 16 + f * 8, fields[f, k, c, x])
             for k in range(2) for x in range(nx) for f in range(2)])


def small_parts(message):
    weight = turn(message[pl.ds(ROW_EPS, 16), :], -64)
    density = turn(message[pl.ds(ROW_EPS + 16, 16), :], -64)
    partner = turn(message[pl.ds(ROW_EPS, 16), :], -96)
    return weight, density, partner


def mirror_take(table, partner, ny):
    inside = lane_of(partner.shape) < ny
    at = jnp.where(inside, partner, 0.0).astype(jnp.int32)
    row, lane = at // ny, at % ny
    got = jnp.zeros(at.shape, F32)
    for r in range(table.shape[0]):
        line = jnp.broadcast_to(table[pl.ds(r, 1), :], at.shape)
        got = jnp.where(row == r, jnp.take_along_axis(line, lane, axis=1), got)
    return got


def spread_slab(values, lines, square, nx, ny):
    lines[...] = values
    square[...] = jnp.zeros_like(square)
    for p in range(PLANES):
        for x in range(nx):
            row = lines[pl.ds(p * nx + x, 1), :]
            square[pl.ds(x * 16 + 2 + p, 1), :] = row
            square[pl.ds(x * 16 + 10 + p, 1), :] = row
    return jnp.transpose(square[...])[:ny]


def coef_kernel(eps, mine, theirs, ef, hf, ea, ha, coef, mirror_coef, y_up, y_down, table, lines, square):
    nx = eps.shape[0]
    ny = END - TOP
    weight, density, partner = small_parts(mine)
    weight_m, density_m, partner_m = small_parts(theirs)
    table[...] = density_m
    extra = weight * (0.5 * (density + mirror_take(table, partner, ny)))
    table[...] = density
    extra_m = weight_m * (0.5 * (density_m + mirror_take(table, partner_m, ny)))
    packed = spread_slab(extra, lines, square, nx, ny)
    lane = lane_of(packed.shape)
    for x in range(nx):
        part = turn(packed, -16 * x - SHIFT)
        low = jnp.where(lane >= Z0, part, 0.0)
        high = jnp.where(lane < Z0 + PLANES - LANES, part, 0.0)
        coef[x] = COURANT / (eps[x] + jnp.concatenate([low, high], 1))
    packed = theirs[pl.ds(ROW_EPS, ny), :] + spread_slab(extra_m, lines, square, nx, ny)
    mirror_coef[...] = jnp.where(lane < 64, COURANT / jnp.where(lane < 64, packed, 1.0), 0.0)
    for out, first in ((y_up, ny - 2), (y_down, 0)):
        at = 0
        for f in range(2):
            for k in range(2):
                for c in range(3):
                    for x in range(nx):
                        out[pl.ds(at, 2), :] = ((ef, hf), (ea, ha))[f][k][c, x, pl.ds(first, 2), :]
                        at += 2
        for x in range(nx):
            out[pl.ds(at, 2), :] = coef[x, pl.ds(first, 2), :]
            at += 2
        out[pl.ds(at, 8), :] = jnp.zeros((8, out.shape[1]), F32)
        for c in range(3):
            out[pl.ds(at, 2), pl.ds(0, LANES)] = theirs[pl.ds(c * 32 + first, 2), :]
            at += 2
        out[pl.ds(at, 2), pl.ds(0, LANES)] = mirror_coef[pl.ds(first, 2), :]


def plane_index(f, k, c, x, nx):
    return ((f * 2 + k) * 3 + c) * nx + x


def framed(middle, tops, ends, i):
    return jnp.concatenate([tops[i], middle, ends[i]], 0)


def edge_planes(part, ks, nx, mark):
    up, down = [], []
    last = nx - 1
    for f in range(2):
        e = lambda c, x: part(f, 0, c, x)
        h = lambda c, x: part(f, 1, c, x)
        k = ks[last]
        ex, ey, ez = e(0, last), e(1, last), e(2, last)
        ex_b, ey_b, ez_b = e(0, last - 1), e(1, last - 1), e(2, last - 1)
        hy_b = mark(h(1, last - 1) - COURANT * ((up_z(ex_b) - ex_b) - (ez - ez_b)), last - 1)
        hz_b = mark(h(2, last - 1) - COURANT * ((ey - ey_b) - (up_y(ex_b) - ex_b)), last - 1)
        hx = mark(h(0, last) - COURANT * ((up_y(ez) - ez) - (up_z(ey) - ey)), last)
        hy = mark(h(1, last) - COURANT * ((up_z(ex) - ex) + ez), last)
        hz = mark(h(2, last) - COURANT * (-ey - (up_y(ex) - ex)), last)
        ex = ex + k * ((hz - down_y(hz)) - (hy - down_z(hy)))
        ey = ey + k * ((hx - down_z(hx)) - (hz - hz_b))
        ez = ez + k * ((hy - hy_b) - (hx - down_y(hx)))
        up += [hy, hz, mark(hy - COURANT * ((up_z(ex) - ex) + ez), last),
               mark(hz - COURANT * (-ey - (up_y(ex) - ex)), last)]
        k = ks[0]
        ex, ey, ez = e(0, 0), e(1, 0), e(2, 0)
        hx = mark(h(0, 0) - COURANT * ((up_y(ez) - ez) - (up_z(ey) - ey)), 0)
        hy = mark(h(1, 0) - COURANT * ((up_z(ex) - ex) - (e(2, 1) - ez)), 0)
        hz = mark(h(2, 0) - COURANT * ((e(1, 1) - ey) - (up_y(ex) - ex)), 0)
        down += [ey, ez, ey + k * ((hx - down_z(hx)) - hz), ez + k * (hy - (hx - down_y(hx)))]
    return up + [ks[last]], down + [ks[0]]


LATER = (2, 3, 6, 7, 8)
SLIM = 6


def bulk_kernel(ef, hf, ea, ha, eps, x_up, x_down):
    nx, ny = eps.shape[0], eps.shape[1]
    fields = ((ef, hf), (ea, ha))
    ks = [COURANT / eps[x] if x in (0, nx - 1) else None for x in range(nx)]
    up, down = edge_planes(lambda f, k, c, x: fields[f][k][c, x], ks, nx, lambda v, x: v)
    for out, planes in ((x_up, up), (x_down, down)):
        for i, plane in enumerate(planes):
            out[pl.ds(i * ny, ny), :] = plane


def edges_kernel(ef, hf, ea, ha, coef, mirror_coef, theirs, y_low, y_high,
                 tops, ends, mirror, x_up, x_down):
    nx, ny = coef.shape[0], coef.shape[1]
    fields = ((ef, hf), (ea, ha))
    tops[...] = jnp.zeros_like(tops)
    ends[...] = jnp.zeros_like(ends)
    mirror[...] = jnp.zeros_like(mirror)
    for c in range(3):
        mirror[c, pl.ds(TOP, ny), :] = theirs[pl.ds(c * 32, ny), :]
    mirror[3, pl.ds(TOP, ny), :] = mirror_coef[...]
    for source, out, first in ((y_low, tops, TOP - 2), (y_high, ends, 0)):
        for i in range(13 * nx):
            out[i, pl.ds(first, 2), :] = source[pl.ds(2 * i, 2), :]
        for c in range(4):
            row = TOP - 2 if out is tops else END
            mirror[c, pl.ds(row, 2), :] = source[pl.ds(26 * nx + 2 * c, 2), pl.ds(0, LANES)]

    def part(f, k, c, x):
        return framed(fields[f][k][c, x], tops, ends, plane_index(f, k, c, x, nx))

    ks = [framed(coef[x], tops, ends, 12 * nx + x) for x in range(nx)]
    up, down = edge_planes(part, ks, nx, lambda v, x: jnp.where(ks[x] > 0, v, 0.0))
    m = [mirror[c] for c in range(3)]
    km = mirror[3]
    lane = lane_of(km.shape)
    first = lane % 64 < 32
    up_m = [jnp.where(first, m[0], turn(m[1], 32)), jnp.where(first, m[2], turn(km, 32))]
    down_m = [jnp.where(first, turn(m[1], -32), m[0]), jnp.where(first, turn(km, -32), m[2])]
    for out, planes, window, base in ((x_up, up, up_m, 96), (x_down, down, down_m, 64)):
        for i, plane in enumerate(planes):
            out[pl.ds(8 * i, 4), :] = plane[TOP - 2:TOP + 2]
            out[pl.ds(8 * i + 4, 4), :] = plane[END - 2:END + 2]
        side = window[1]
        for i, plane in enumerate(LATER):
            plane = planes[plane]
            near = jnp.where(lane >= LANES // 2, plane[:, :LANES], plane[:, LANES:])
            part_in = turn(near, SHIFT + base + SLIM * i - 1)
            inside = (lane >= base + SLIM * i) & (lane < base + SLIM * (i + 1))
            side = jnp.where(inside, part_in, side)
        value = jnp.concatenate([window[0], side], 1)
        out[pl.ds(72, ny), :] = value[TOP:END]
        out[pl.ds(72 + ny, 2), :] = value[TOP - 2:TOP]
        out[pl.ds(74 + ny, 2), :] = value[END:END + 2]


def slab_gradient(message, first, second, ny):
    total = None
    for c in range(3):
        mon = message[pl.ds(ROW_MON + 32 * (c // 2), ny), :]
        real = turn(mon, -64 * (c % 2))
        imag = turn(real, -4)
        real = real + math.cos(OMEGA) * first[c] + math.cos(2 * OMEGA) * second[c]
        imag = imag - math.sin(OMEGA) * first[c] - math.sin(2 * OMEGA) * second[c]
        term = real * turn(real, -8) - imag * turn(imag, -8)
        total = term if total is None else total + term
    return total


def slab_rows(packed, out, square, nx):
    square[...] = flipped(packed, square)
    for p in range(PLANES):
        for x in range(nx):
            out[pl.ds(p * nx + x, 1), :] = square[pl.ds(x * 16 + 2 + p, 1), :]


def step_kernel(ef_in, hf_in, ea_in, ha_in, coef, tops, ends, mirror, bulk_low, bulk_high,
                x_low, x_high, mine, theirs,
                ef_out, hf_out, ea_out, ha_out, grad,
                ee, hh, halo, square, table, lines, sems):
    nx, ny, nz = coef.shape

    fields = ((ef_in, hf_in), (ea_in, ha_in))
    lane = lane_of((ny, LANES))
    for bulk, source, slot, base in ((bulk_low, x_low, 0, 96), (bulk_high, x_high, 10, 64)):
        halo[slot + 9, pl.ds(0, TOP), :] = jnp.zeros((TOP, nz), F32)
        halo[slot + 9, pl.ds(END, TOP), :] = jnp.zeros((TOP, nz), F32)
        halo[slot + 9, pl.ds(TOP, ny), :] = source[pl.ds(72, ny), :]
        halo[slot + 9, pl.ds(TOP - 2, 2), :] = source[pl.ds(72 + ny, 2), :]
        halo[slot + 9, pl.ds(END, 2), :] = source[pl.ds(74 + ny, 2), :]
        side = source[pl.ds(72, ny), pl.ds(LANES, LANES)]
        for plane in range(9):
            at = slot + plane
            halo[at, pl.ds(0, TOP), :] = jnp.zeros((TOP, nz), F32)
            halo[at, pl.ds(END, TOP), :] = jnp.zeros((TOP, nz), F32)
            value = bulk[pl.ds(plane * ny, ny), :]
            if plane in LATER:
                near = turn(side, 1 - SHIFT - base - SLIM * LATER.index(plane))
                value = jnp.concatenate(
                    [jnp.where(lane >= Z0 - 1, near, value[:, :LANES]),
                     jnp.where(lane < Z0 + PLANES + 1 - LANES, near, value[:, LANES:])], 1)
            halo[at, pl.ds(TOP, ny), :] = value
            halo[at, pl.ds(TOP - 2, 4), :] = source[pl.ds(8 * plane, 4), :]
            halo[at, pl.ds(END - 2, 4), :] = source[pl.ds(8 * plane + 4, 4), :]
    k_low, k_high = halo[8], halo[18]

    def part(f, k, c, x):
        return framed(fields[f][k][c, x], tops, ends, plane_index(f, k, c, x, nx))

    def inverse(x):
        return framed(coef[x], tops, ends, 12 * nx + x)

    copies = []
    first_slab, second_slab = [], []
    for f in range(2):
        ey0, ez0 = part(f, 0, 1, 0), part(f, 0, 2, 0)
        dhy = jnp.where(k_low > 0, COURANT * ez0, 0.0)
        dhz = jnp.where(k_low > 0, -COURANT * ey0, 0.0)
        hh[f, 1, 0] = halo[4 * f] + dhy
        hh[f, 2, 0] = halo[4 * f + 1] + dhz
        for x in range(nx):
            inside = inverse(x) > 0
            ex, ey, ez = part(f, 0, 0, x), part(f, 0, 1, x), part(f, 0, 2, x)
            ey_n = part(f, 0, 1, x + 1) if x + 1 < nx else halo[10 + 4 * f]
            ez_n = part(f, 0, 2, x + 1) if x + 1 < nx else halo[10 + 4 * f + 1]
            hx, hy, hz = part(f, 1, 0, x), part(f, 1, 1, x), part(f, 1, 2, x)
            hh[f, 0, x + 1] = jnp.where(inside, hx - COURANT * ((up_y(ez) - ez) - (up_z(ey) - ey)), 0.0)
            hh[f, 1, x + 1] = jnp.where(inside, hy - COURANT * ((up_z(ex) - ex) - (ez_n - ez)), 0.0)
            hh[f, 2, x + 1] = jnp.where(inside, hz - COURANT * ((ey_n - ey) - (up_y(ex) - ex)), 0.0)
        for x in range(nx):
            k = inverse(x)
            hx, hy, hz = hh[f, 0, x + 1], hh[f, 1, x + 1], hh[f, 2, x + 1]
            ee[f, 0, x] = part(f, 0, 0, x) + k * ((hz - down_y(hz)) - (hy - down_z(hy)))
            ee[f, 1, x] = part(f, 0, 1, x) + k * ((hx - down_z(hx)) - (hz - hh[f, 2, x]))
            ee[f, 2, x] = part(f, 0, 2, x) + k * ((hy - hh[f, 1, x]) - (hx - down_y(hx)))
        ee[f, 1, nx] = halo[10 + 4 * f + 2] + k_high * hh[f, 2, nx]
        ee[f, 2, nx] = halo[10 + 4 * f + 3] - k_high * hh[f, 1, nx]
        dex = k_low * ((dhz - down_y(dhz)) - (dhy - down_z(dhy)))
        dey = -k_low * dhz
        dez = k_low * dhy
        hh[f, 1, 0] = jnp.where(
            k_low > 0, halo[4 * f + 2] + dhy - COURANT * ((up_z(dex) - dex) - (ee[f, 2, 0] - dez)), 0.0)
        hh[f, 2, 0] = jnp.where(
            k_low > 0, halo[4 * f + 3] + dhz - COURANT * ((ee[f, 1, 0] - dey) - (up_y(dex) - dex)), 0.0)
        for x in range(nx):
            inside = inverse(x) > 0
            ex, ey, ez = ee[f, 0, x], ee[f, 1, x], ee[f, 2, x]
            hh[f, 0, x + 1] = jnp.where(
                inside, hh[f, 0, x + 1] - COURANT * ((up_y(ez) - ez) - (up_z(ey) - ey)), 0.0)
            hh[f, 1, x + 1] = jnp.where(
                inside, hh[f, 1, x + 1] - COURANT * ((up_z(ex) - ex) - (ee[f, 2, x + 1] - ez)), 0.0)
            hh[f, 2, x + 1] = jnp.where(
                inside, hh[f, 2, x + 1] - COURANT * ((ee[f, 1, x + 1] - ey) - (up_y(ex) - ex)), 0.0)
        copies.append(pltpu.make_async_copy(
            hh.at[f, :, pl.ds(1, nx), pl.ds(TOP, ny), :], (hf_out, ha_out)[f], sems.at[2 * f]))
        copies[-1].start()
    for c in range(3):
        first_slab.append(pack_planes([(x * 16 + f * 8, ee[f, c, x, pl.ds(TOP, ny), :])
                                       for x in range(nx) for f in range(2)]))
    for f in range(2):
        for x in range(nx):
            k = inverse(x)
            hx, hy, hz = hh[f, 0, x + 1], hh[f, 1, x + 1], hh[f, 2, x + 1]
            ee[f, 0, x] = ee[f, 0, x] + k * ((hz - down_y(hz)) - (hy - down_z(hy)))
            ee[f, 1, x] = ee[f, 1, x] + k * ((hx - down_z(hx)) - (hz - hh[f, 2, x]))
            ee[f, 2, x] = ee[f, 2, x] + k * ((hy - hh[f, 1, x]) - (hx - down_y(hx)))
        copies.append(pltpu.make_async_copy(
            ee.at[f, :, pl.ds(0, nx), pl.ds(TOP, ny), :], (ef_out, ea_out)[f], sems.at[2 * f + 1]))
        copies[-1].start()
    for c in range(3):
        second_slab.append(pack_planes([(x * 16 + f * 8, ee[f, c, x, pl.ds(TOP, ny), :])
                                        for x in range(nx) for f in range(2)]))
    own = slab_gradient(mine, first_slab, second_slab, ny)

    low01, low2 = halo[9, :, pl.ds(0, LANES)], halo[9, :, pl.ds(LANES, LANES)]
    high01, high2 = halo[19, :, pl.ds(0, LANES)], halo[19, :, pl.ds(LANES, LANES)]
    lane = lane_of(low01.shape)

    def join(below, middle, above):
        return jnp.where(lane < 32, below, jnp.where(lane < 96, middle, above))

    m = [mirror[c] for c in range(3)]
    e = [join(turn(high01, -32), turn(m[0], 32), turn(low01, 96)),
         join(high01, turn(m[1], 32), turn(low01, 64)),
         join(turn(high2, -32), turn(m[2], 32), turn(low2, 96))]
    h = [join(turn(high01, -96), turn(m[0], -32), turn(low01, 32)),
         join(turn(high01, -64), turn(m[1], -32), low01),
         join(turn(high2, -96), turn(m[2], -32), turn(low2, 32))]
    k = join(high2, turn(mirror[3], 32), turn(low2, 64))
    inside = k > 0

    def ahead(a, axis):
        return (turn(a, -16), up_y(a), turn(a, -1))[axis] - a

    def behind(a, axis):
        return a - (turn(a, 16), down_y(a), turn(a, 1))[axis]

    slabs = []
    for _ in range(2):
        h = [jnp.where(inside, h[c] - COURANT * (ahead(e[(c + 2) % 3], (c + 1) % 3)
                                                 - ahead(e[(c + 1) % 3], (c + 2) % 3)), 0.0)
             for c in range(3)]
        e = [e[c] + k * (behind(h[(c + 2) % 3], (c + 1) % 3) - behind(h[(c + 1) % 3], (c + 2) % 3))
             for c in range(3)]
        slabs.append([turn(e[c], -32)[TOP:END] for c in range(3)])
    other = slab_gradient(theirs, slabs[0], slabs[1], ny)

    weight, _, partner = small_parts(mine)
    weight_m, _, _ = small_parts(theirs)
    slab_rows(other, table, square, nx)
    table[...] = table[...] * weight_m
    got = mirror_take(table, partner, ny)
    slab_rows(own, lines, square, nx)
    lines[...] = 0.5 * (lines[...] * weight + got)
    for p in range(PLANES):
        grad[p] = lines[pl.ds(p * nx, nx), pl.ds(0, ny)]
    for copy in copies:
        copy.wait()


def call(kernel, outs, args, scratch=(), name=None, any_in=False, any_out=0):
    spaces = lambda count, far: [pl.BlockSpec(memory_space=pltpu.HBM if i < far else pltpu.VMEM)
                                 for i in range(count)]
    return pl.pallas_call(
        kernel,
        out_shape=outs,
        in_specs=spaces(len(args), len(args) if any_in else 0),
        out_specs=spaces(len(outs), any_out),
        scratch_shapes=list(scratch),
        compiler_params=pltpu.CompilerParams(vmem_limit_bytes=FAR_LIMIT if any_in else VMEM_LIMIT),
        cost_estimate=pl.CostEstimate(flops=4_000_000, bytes_accessed=4_000_000, transcendentals=0),
        name=name,
    )(*args)


def shifted(block, axis, distance):
    devices = range(lax.axis_size(axis))
    return lax.ppermute(block, axis, [(i - distance, i) for i in devices if i - distance in devices])


def mirrored(block, axis):
    size = lax.axis_size(axis)
    return lax.ppermute(block, axis, [(i, size - 1 - i) for i in range(size)])


def per_device(e_fwd, h_fwd, e_adj, h_adj, eps_back, density, design_mask, partner_map, mon_fwd, mon_adj):
    _, nx, ny, nz = e_fwd.shape
    shape = lambda *dims: jax.ShapeDtypeStruct(dims, F32)
    vmem = lambda *dims: pltpu.VMEM(dims, F32)
    square = vmem(LANES, LANES)
    lines = vmem(PLANES * nx, LANES)
    block = shape(nx, ny, nz)
    fields = [e_fwd, h_fwd, e_adj, h_adj]

    mine, = call(
        message_kernel, [shape(MESSAGE, LANES)],
        fields + [eps_back, density, design_mask, partner_map, mon_fwd, mon_adj],
        [vmem(2, 2, 3, nx, ny, nz), vmem(nx, ny, nz), vmem(*density.shape),
         pltpu.VMEM((2,) + density.shape, jnp.int32), vmem(2, *mon_fwd.shape),
         square, pltpu.SemaphoreType.DMA((10,))], name="message", any_in=True)
    theirs = mirrored(mine, "gx")
    bulk_shape = shape(9 * ny, nz)
    bulk_up, bulk_down = call(bulk_kernel, [bulk_shape, bulk_shape], fields + [eps_back], name="bulk")
    bulk_low, bulk_high = shifted(bulk_up, "gx", 1), shifted(bulk_down, "gx", -1)
    y_shape = shape(2 * (13 * nx) + 8, nz)
    coef, mirror_coef, y_up, y_down = call(
        coef_kernel, [block, shape(ny, LANES), y_shape, y_shape], [eps_back, mine, theirs] + fields,
        [lines, lines, square], name="coefficient")
    y_low, y_high = shifted(y_up, "gy", 1), shifted(y_down, "gy", -1)
    x_shape = shape(9 * 8 + ny + 4, nz)
    tile = shape(13 * nx, 8, nz)
    tops, ends, mirror, x_up, x_down = call(
        edges_kernel, [tile, tile, shape(4, FRAME, LANES), x_shape, x_shape],
        fields + [coef, mirror_coef, theirs, y_low, y_high], name="edges")
    x_low, x_high = shifted(x_up, "gx", 1), shifted(x_down, "gx", -1)
    ef, hf, ea, ha, grad = call(
        step_kernel, [shape(*e_fwd.shape)] * 4 + [shape(*density.shape)],
        fields + [coef, tops, ends, mirror, bulk_low, bulk_high, x_low, x_high, mine, theirs],
        [vmem(2, 3, nx + 1, FRAME, nz), vmem(2, 3, nx + 1, FRAME, nz), vmem(20, FRAME, nz),
         square, lines, lines, pltpu.SemaphoreType.DMA((4,))], name="steps", any_out=4)
    return ef, hf, ea, ha, grad


def solution(mesh):
    grid = P(None, "gx", "gy", None)
    slab = P(None, "gx", "gy")
    monitor = P(None, None, None, "gx", "gy")
    return jax.shard_map(
        per_device,
        mesh=mesh,
        in_specs=(grid, grid, grid, grid, P("gx", "gy", None), slab, slab, slab, monitor, monitor),
        out_specs=(grid, grid, grid, grid, slab),
        check_vma=False,
    )
```

```python
import math

import jax
import jax.numpy as jnp
from jax import lax
from jax.experimental import pallas as pl
from jax.experimental.pallas import tpu as pltpu
from jax.sharding import PartitionSpec as P

PLANES = 4
Z0 = 126
COURANT = 0.5
OMEGA = 0.7
CONTRAST = 10.0
F32 = jnp.float32
VMEM_LIMIT = 32 * 1024 * 1024
FAR_LIMIT = 60 * 1024 * 1024

LANES = 128
FRAME = 48
TOP, END = 8, 40
WINDOW = 8
SHIFT = LANES - (Z0 - 2)
ROW_EPS, ROW_MON, MESSAGE = 96, 128, 192


def lane_of(shape):
    return lax.broadcasted_iota(jnp.int32, shape, len(shape) - 1)


def row_of(shape):
    return lax.broadcasted_iota(jnp.int32, shape, len(shape) - 2)


def turn(a, shift):
    shift = shift % a.shape[1]
    return pltpu.roll(a, shift, 1) if shift else a


def up_y(a):
    return pltpu.roll(a, a.shape[0] - 1, 0)


def down_y(a):
    return pltpu.roll(a, 1, 0)


def up_z(a):
    n = a.shape[1]
    return jnp.where(lane_of(a.shape) == n - 1, 0.0, pltpu.roll(a, n - 1, 1))


def down_z(a):
    return jnp.where(lane_of(a.shape) == 0, 0.0, pltpu.roll(a, 1, 1))


def is_odd(axis):
    return lax.axis_index(axis) % 2 == 1


def ordered(odd, up, down):
    return jnp.where(odd, up, down), jnp.where(odd, down, up)


def pack_planes(planes):
    total = None
    for offset, plane in planes:
        near = jnp.where(lane_of((plane.shape[0], LANES)) >= LANES // 2,
                         plane[:, :LANES], plane[:, LANES:2 * LANES])
        part = turn(near, SHIFT + offset)
        lane = lane_of(part.shape)
        inside = (lane >= offset) & (lane < offset + WINDOW)
        total = jnp.where(inside, part, 0.0 if total is None else total)
    return total


def flipped(a, square):
    square[...] = jnp.zeros_like(square)
    square[pl.ds(0, a.shape[0]), pl.ds(0, a.shape[1])] = a
    return jnp.transpose(square[...])


def message_kernel(ef, hf, ea, ha, eps, density, mask, partner, mon_f, mon_a, message,
                   fields, eps_in, small_f, small_i, mons, square, sems):
    nx, ny = ef.shape[1], ef.shape[2]
    copies = []
    for f, (e, h) in enumerate(((ef, hf), (ea, ha))):
        for k, source in enumerate((e, h)):
            copies.append(pltpu.make_async_copy(source, fields.at[f, k], sems.at[2 * f + k]))
    copies.append(pltpu.make_async_copy(eps, eps_in, sems.at[4]))
    copies.append(pltpu.make_async_copy(density, small_f, sems.at[5]))
    copies.append(pltpu.make_async_copy(mask, small_i.at[0], sems.at[6]))
    copies.append(pltpu.make_async_copy(partner, small_i.at[1], sems.at[7]))
    copies.append(pltpu.make_async_copy(mon_f, mons.at[0], sems.at[8]))
    copies.append(pltpu.make_async_copy(mon_a, mons.at[1], sems.at[9]))
    for copy in copies:
        copy.start()
    message[pl.ds(ROW_EPS, MESSAGE - ROW_EPS), :] = jnp.zeros((MESSAGE - ROW_EPS, LANES), F32)
    for copy in copies[4:]:
        copy.wait()
    for half, components in ((0, (0, 1)), (1, (2,))):
        square[...] = jnp.zeros_like(square)
        for k, c in enumerate(components):
            for f in range(2):
                for x in range(nx):
                    base = k * 64 + x * 16 + f * 8 + 2
                    square[pl.ds(base, PLANES), pl.ds(0, ny)] = mons[f, 0, c, :, x, :]
                    for p in range(PLANES):
                        at = (base + 4 + p) % LANES
                        square[pl.ds(at, 1), pl.ds(0, ny)] = mons[f, 1, c, p, pl.ds(x, 1), :]
        message[pl.ds(ROW_MON + 32 * half, ny), :] = jnp.transpose(square[...])[:ny]
    own_eps = [(x * 16 + f * 8, eps_in[x]) for x in range(nx) for f in range(2)]
    square[...] = jnp.zeros_like(square)
    for p in range(PLANES):
        square[pl.ds(p * nx, nx), pl.ds(0, ny)] = CONTRAST * small_i[0, p].astype(F32)
        square[pl.ds(16 + p * nx, nx), pl.ds(0, ny)] = small_f[p]
        square[pl.ds(32 + p * nx, nx), pl.ds(0, ny)] = small_i[1, p].astype(F32)
    small = turn(square[pl.ds(0, 32), :], 64)
    index = turn(square[pl.ds(32, 32), :], 96)
    message[pl.ds(ROW_EPS, ny), :] = pack_planes(own_eps) + small + index
    for copy in copies[:4]:
        copy.wait()
    for c in range(3):
        message[pl.ds(c * 32, ny), :] = pack_planes(
            [(k * 64 + x * 16 + f * 8, fields[f, k, c, x])
             for k in range(2) for x in range(nx) for f in range(2)])


def small_parts(message):
    weight = turn(message[pl.ds(ROW_EPS, 16), :], -64)
    density = turn(message[pl.ds(ROW_EPS + 16, 16), :], -64)
    partner = turn(message[pl.ds(ROW_EPS, 16), :], -96)
    return weight, density, partner


def mirror_take(table, partner, ny):
    inside = lane_of(partner.shape) < ny
    at = jnp.where(inside, partner, 0.0).astype(jnp.int32)
    row, lane = at // ny, at % ny
    got = jnp.zeros(at.shape, F32)
    for r in range(table.shape[0]):
        line = jnp.broadcast_to(table[pl.ds(r, 1), :], at.shape)
        got = jnp.where(row == r, jnp.take_along_axis(line, lane, axis=1), got)
    return got


def spread_slab(values, lines, square, nx, ny):
    lines[...] = values
    square[...] = jnp.zeros_like(square)
    for p in range(PLANES):
        for x in range(nx):
            row = lines[pl.ds(p * nx + x, 1), :]
            square[pl.ds(x * 16 + 2 + p, 1), :] = row
            square[pl.ds(x * 16 + 10 + p, 1), :] = row
    return jnp.transpose(square[...])[:ny]


def coef_kernel(eps, mine, theirs, ef, hf, ea, ha, coef, mirror_coef, y_far, y_near, table, lines, square):
    nx = eps.shape[0]
    ny = END - TOP
    weight, density, partner = small_parts(mine)
    weight_m, density_m, partner_m = small_parts(theirs)
    table[...] = density_m
    extra = weight * (0.5 * (density + mirror_take(table, partner, ny)))
    table[...] = density
    extra_m = weight_m * (0.5 * (density_m + mirror_take(table, partner_m, ny)))
    packed = spread_slab(extra, lines, square, nx, ny)
    lane = lane_of(packed.shape)
    for x in range(nx):
        part = turn(packed, -16 * x - SHIFT)
        low = jnp.where(lane >= Z0, part, 0.0)
        high = jnp.where(lane < Z0 + PLANES - LANES, part, 0.0)
        coef[x] = COURANT / (eps[x] + jnp.concatenate([low, high], 1))
    packed = theirs[pl.ds(ROW_EPS, ny), :] + spread_slab(extra_m, lines, square, nx, ny)
    mirror_coef[...] = jnp.where(lane < 64, COURANT / jnp.where(lane < 64, packed, 1.0), 0.0)
    odd = is_odd("gy")

    def put(at, ref, lanes):
        far, near = ordered(odd, ref[pl.ds(ny - 2, 2), :], ref[pl.ds(0, 2), :])
        y_far[pl.ds(at, 2), pl.ds(0, lanes)] = far
        y_near[pl.ds(at, 2), pl.ds(0, lanes)] = near

    for f, pair in enumerate(((ef, hf), (ea, ha))):
        for k, field in enumerate(pair):
            for c in range(3):
                for x in range(nx):
                    put(2 * plane_index(f, k, c, x, nx), field.at[c, x], y_far.shape[1])
    for x in range(nx):
        put(24 * nx + 2 * x, coef.at[x], y_far.shape[1])
    rest = jnp.zeros((8, y_far.shape[1]), F32)
    y_far[pl.ds(26 * nx, 8), :] = rest
    y_near[pl.ds(26 * nx, 8), :] = rest
    for c in range(3):
        put(26 * nx + 2 * c, theirs.at[pl.ds(c * 32, ny), :], LANES)
    put(26 * nx + 6, mirror_coef, LANES)


def plane_index(f, k, c, x, nx):
    return ((f * 2 + k) * 3 + c) * nx + x


def framed(middle, tops, ends, i):
    return jnp.concatenate([tops[i], middle, ends[i]], 0)


def edge_planes(part, ks, nx, mark):
    up, down = [], []
    last = nx - 1
    for f in range(2):
        e = lambda c, x: part(f, 0, c, x)
        h = lambda c, x: part(f, 1, c, x)
        k = ks[last]
        ex, ey, ez = e(0, last), e(1, last), e(2, last)
        ex_b, ey_b, ez_b = e(0, last - 1), e(1, last - 1), e(2, last - 1)
        hy_b = mark(h(1, last - 1) - COURANT * ((up_z(ex_b) - ex_b) - (ez - ez_b)), last - 1)
        hz_b = mark(h(2, last - 1) - COURANT * ((ey - ey_b) - (up_y(ex_b) - ex_b)), last - 1)
        hx = mark(h(0, last) - COURANT * ((up_y(ez) - ez) - (up_z(ey) - ey)), last)
        hy = mark(h(1, last) - COURANT * ((up_z(ex) - ex) + ez), last)
        hz = mark(h(2, last) - COURANT * (-ey - (up_y(ex) - ex)), last)
        ex = ex + k * ((hz - down_y(hz)) - (hy - down_z(hy)))
        ey = ey + k * ((hx - down_z(hx)) - (hz - hz_b))
        ez = ez + k * ((hy - hy_b) - (hx - down_y(hx)))
        up += [hy, hz, mark(hy - COURANT * ((up_z(ex) - ex) + ez), last),
               mark(hz - COURANT * (-ey - (up_y(ex) - ex)), last)]
        k = ks[0]
        ex, ey, ez = e(0, 0), e(1, 0), e(2, 0)
        hx = mark(h(0, 0) - COURANT * ((up_y(ez) - ez) - (up_z(ey) - ey)), 0)
        hy = mark(h(1, 0) - COURANT * ((up_z(ex) - ex) - (e(2, 1) - ez)), 0)
        hz = mark(h(2, 0) - COURANT * ((e(1, 1) - ey) - (up_y(ex) - ex)), 0)
        down += [ey, ez, ey + k * ((hx - down_z(hx)) - hz), ez + k * (hy - (hx - down_y(hx)))]
    return up + [ks[last]], down + [ks[0]]


LATER = (2, 3, 6, 7, 8)
SLIM = 6


def bulk_kernel(ef, hf, ea, ha, eps, x_far, x_near):
    nx, ny = eps.shape[0], eps.shape[1]
    fields = ((ef, hf), (ea, ha))
    ks = [COURANT / eps[x] if x in (0, nx - 1) else None for x in range(nx)]
    up, down = edge_planes(lambda f, k, c, x: fields[f][k][c, x], ks, nx, lambda v, x: v)
    odd = is_odd("gx")
    for i, planes in enumerate(zip(up, down)):
        far, near = ordered(odd, *planes)
        x_far[pl.ds(i * ny, ny), :] = far
        x_near[pl.ds(i * ny, ny), :] = near


def edges_kernel(ef, hf, ea, ha, coef, mirror_coef, theirs, y_far, y_near,
                 tops, ends, mirror, x_far, x_near, x_up, x_down):
    nx, ny = coef.shape[0], coef.shape[1]
    fields = ((ef, hf), (ea, ha))
    tops[...] = jnp.zeros_like(tops)
    ends[...] = jnp.zeros_like(ends)
    mirror[...] = jnp.zeros_like(mirror)
    for c in range(3):
        mirror[c, pl.ds(TOP, ny), :] = theirs[pl.ds(c * 32, ny), :]
    mirror[3, pl.ds(TOP, ny), :] = mirror_coef[...]
    odd = is_odd("gy")

    def came(at, lanes):
        high, low = ordered(odd, y_far[pl.ds(at, 2), pl.ds(0, lanes)], y_near[pl.ds(at, 2), pl.ds(0, lanes)])
        return low, high

    for i in range(13 * nx):
        low, high = came(2 * i, y_far.shape[1])
        tops[i, pl.ds(TOP - 2, 2), :] = low
        ends[i, pl.ds(0, 2), :] = high
    for c in range(4):
        low, high = came(26 * nx + 2 * c, LANES)
        mirror[c, pl.ds(TOP - 2, 2), :] = low
        mirror[c, pl.ds(END, 2), :] = high

    def part(f, k, c, x):
        return framed(fields[f][k][c, x], tops, ends, plane_index(f, k, c, x, nx))

    ks = [framed(coef[x], tops, ends, 12 * nx + x) for x in range(nx)]
    up, down = edge_planes(part, ks, nx, lambda v, x: jnp.where(ks[x] > 0, v, 0.0))
    m = [mirror[c] for c in range(3)]
    km = mirror[3]
    lane = lane_of(km.shape)
    first = lane % 64 < 32
    up_m = [jnp.where(first, m[0], turn(m[1], 32)), jnp.where(first, m[2], turn(km, 32))]
    down_m = [jnp.where(first, turn(m[1], -32), m[0]), jnp.where(first, turn(km, -32), m[2])]
    for out, planes, window, base in ((x_up, up, up_m, 96), (x_down, down, down_m, 64)):
        for i, plane in enumerate(planes):
            out[pl.ds(8 * i, 4), :] = plane[TOP - 2:TOP + 2]
            out[pl.ds(8 * i + 4, 4), :] = plane[END - 2:END + 2]
        side = window[1]
        for i, plane in enumerate(LATER):
            plane = planes[plane]
            near = jnp.where(lane >= LANES // 2, plane[:, :LANES], plane[:, LANES:])
            part_in = turn(near, SHIFT + base + SLIM * i - 1)
            inside = (lane >= base + SLIM * i) & (lane < base + SLIM * (i + 1))
            side = jnp.where(inside, part_in, side)
        value = jnp.concatenate([window[0], side], 1)
        out[pl.ds(72, ny), :] = value[TOP:END]
        out[pl.ds(72 + ny, 2), :] = value[TOP - 2:TOP]
        out[pl.ds(74 + ny, 2), :] = value[END:END + 2]
    x_far[...], x_near[...] = ordered(is_odd("gx"), x_up[...], x_down[...])


def slab_gradient(message, first, second, ny):
    total = None
    for c in range(3):
        mon = message[pl.ds(ROW_MON + 32 * (c // 2), ny), :]
        real = turn(mon, -64 * (c % 2))
        imag = turn(real, -4)
        real = real + math.cos(OMEGA) * first[c] + math.cos(2 * OMEGA) * second[c]
        imag = imag - math.sin(OMEGA) * first[c] - math.sin(2 * OMEGA) * second[c]
        term = real * turn(real, -8) - imag * turn(imag, -8)
        total = term if total is None else total + term
    return total


def slab_rows(packed, out, square, nx):
    square[...] = flipped(packed, square)
    for p in range(PLANES):
        for x in range(nx):
            out[pl.ds(p * nx + x, 1), :] = square[pl.ds(x * 16 + 2 + p, 1), :]


def step_kernel(ef_in, hf_in, ea_in, ha_in, coef, tops, ends, mirror, bulk_far, bulk_near,
                x_far, x_near, mine, theirs,
                ef_out, hf_out, ea_out, ha_out, grad,
                ee, hh, halo, square, table, lines, sems):
    nx, ny, nz = coef.shape

    fields = ((ef_in, hf_in), (ea_in, ha_in))
    lane = lane_of((ny, LANES))
    odd = is_odd("gx")
    for slot, base in ((0, 96), (10, 64)):
        def source_at(row, rows, slot=slot):
            pair = (x_near, x_far) if slot == 0 else (x_far, x_near)
            return jnp.where(odd, pair[0][pl.ds(row, rows), :], pair[1][pl.ds(row, rows), :])

        def bulk_at(row, rows, slot=slot):
            pair = (bulk_near, bulk_far) if slot == 0 else (bulk_far, bulk_near)
            return jnp.where(odd, pair[0][pl.ds(row, rows), :], pair[1][pl.ds(row, rows), :])

        halo[slot + 9, pl.ds(0, TOP), :] = jnp.zeros((TOP, nz), F32)
        halo[slot + 9, pl.ds(END, TOP), :] = jnp.zeros((TOP, nz), F32)
        window = source_at(72, ny)
        halo[slot + 9, pl.ds(TOP, ny), :] = window
        halo[slot + 9, pl.ds(TOP - 2, 2), :] = source_at(72 + ny, 2)
        halo[slot + 9, pl.ds(END, 2), :] = source_at(74 + ny, 2)
        side = window[:, LANES:]
        for plane in range(9):
            at = slot + plane
            halo[at, pl.ds(0, TOP), :] = jnp.zeros((TOP, nz), F32)
            halo[at, pl.ds(END, TOP), :] = jnp.zeros((TOP, nz), F32)
            value = bulk_at(plane * ny, ny)
            if plane in LATER:
                near = turn(side, 1 - SHIFT - base - SLIM * LATER.index(plane))
                value = jnp.concatenate(
                    [jnp.where(lane >= Z0 - 1, near, value[:, :LANES]),
                     jnp.where(lane < Z0 + PLANES + 1 - LANES, near, value[:, LANES:])], 1)
            halo[at, pl.ds(TOP, ny), :] = value
            halo[at, pl.ds(TOP - 2, 4), :] = source_at(8 * plane, 4)
            halo[at, pl.ds(END - 2, 4), :] = source_at(8 * plane + 4, 4)
    k_low, k_high = halo[8], halo[18]

    def part(f, k, c, x):
        return framed(fields[f][k][c, x], tops, ends, plane_index(f, k, c, x, nx))

    def inverse(x):
        return framed(coef[x], tops, ends, 12 * nx + x)

    copies = []
    first_slab, second_slab = [], []
    for f in range(2):
        ey0, ez0 = part(f, 0, 1, 0), part(f, 0, 2, 0)
        dhy = jnp.where(k_low > 0, COURANT * ez0, 0.0)
        dhz = jnp.where(k_low > 0, -COURANT * ey0, 0.0)
        hh[f, 1, 0] = halo[4 * f] + dhy
        hh[f, 2, 0] = halo[4 * f + 1] + dhz
        for x in range(nx):
            inside = inverse(x) > 0
            ex, ey, ez = part(f, 0, 0, x), part(f, 0, 1, x), part(f, 0, 2, x)
            ey_n = part(f, 0, 1, x + 1) if x + 1 < nx else halo[10 + 4 * f]
            ez_n = part(f, 0, 2, x + 1) if x + 1 < nx else halo[10 + 4 * f + 1]
            hx, hy, hz = part(f, 1, 0, x), part(f, 1, 1, x), part(f, 1, 2, x)
            hh[f, 0, x + 1] = jnp.where(inside, hx - COURANT * ((up_y(ez) - ez) - (up_z(ey) - ey)), 0.0)
            hh[f, 1, x + 1] = jnp.where(inside, hy - COURANT * ((up_z(ex) - ex) - (ez_n - ez)), 0.0)
            hh[f, 2, x + 1] = jnp.where(inside, hz - COURANT * ((ey_n - ey) - (up_y(ex) - ex)), 0.0)
        for x in range(nx):
            k = inverse(x)
            hx, hy, hz = hh[f, 0, x + 1], hh[f, 1, x + 1], hh[f, 2, x + 1]
            ee[f, 0, x] = part(f, 0, 0, x) + k * ((hz - down_y(hz)) - (hy - down_z(hy)))
            ee[f, 1, x] = part(f, 0, 1, x) + k * ((hx - down_z(hx)) - (hz - hh[f, 2, x]))
            ee[f, 2, x] = part(f, 0, 2, x) + k * ((hy - hh[f, 1, x]) - (hx - down_y(hx)))
        ee[f, 1, nx] = halo[10 + 4 * f + 2] + k_high * hh[f, 2, nx]
        ee[f, 2, nx] = halo[10 + 4 * f + 3] - k_high * hh[f, 1, nx]
        dex = k_low * ((dhz - down_y(dhz)) - (dhy - down_z(dhy)))
        dey = -k_low * dhz
        dez = k_low * dhy
        hh[f, 1, 0] = jnp.where(
            k_low > 0, halo[4 * f + 2] + dhy - COURANT * ((up_z(dex) - dex) - (ee[f, 2, 0] - dez)), 0.0)
        hh[f, 2, 0] = jnp.where(
            k_low > 0, halo[4 * f + 3] + dhz - COURANT * ((ee[f, 1, 0] - dey) - (up_y(dex) - dex)), 0.0)
        for x in range(nx):
            inside = inverse(x) > 0
            ex, ey, ez = ee[f, 0, x], ee[f, 1, x], ee[f, 2, x]
            hh[f, 0, x + 1] = jnp.where(
                inside, hh[f, 0, x + 1] - COURANT * ((up_y(ez) - ez) - (up_z(ey) - ey)), 0.0)
            hh[f, 1, x + 1] = jnp.where(
                inside, hh[f, 1, x + 1] - COURANT * ((up_z(ex) - ex) - (ee[f, 2, x + 1] - ez)), 0.0)
            hh[f, 2, x + 1] = jnp.where(
                inside, hh[f, 2, x + 1] - COURANT * ((ee[f, 1, x + 1] - ey) - (up_y(ex) - ex)), 0.0)
        copies.append(pltpu.make_async_copy(
            hh.at[f, :, pl.ds(1, nx), pl.ds(TOP, ny), :], (hf_out, ha_out)[f], sems.at[2 * f]))
        copies[-1].start()
    for c in range(3):
        first_slab.append(pack_planes([(x * 16 + f * 8, ee[f, c, x, pl.ds(TOP, ny), :])
                                       for x in range(nx) for f in range(2)]))
    for f in range(2):
        for x in range(nx):
            k = inverse(x)
            hx, hy, hz = hh[f, 0, x + 1], hh[f, 1, x + 1], hh[f, 2, x + 1]
            ee[f, 0, x] = ee[f, 0, x] + k * ((hz - down_y(hz)) - (hy - down_z(hy)))
            ee[f, 1, x] = ee[f, 1, x] + k * ((hx - down_z(hx)) - (hz - hh[f, 2, x]))
            ee[f, 2, x] = ee[f, 2, x] + k * ((hy - hh[f, 1, x]) - (hx - down_y(hx)))
        copies.append(pltpu.make_async_copy(
            ee.at[f, :, pl.ds(0, nx), pl.ds(TOP, ny), :], (ef_out, ea_out)[f], sems.at[2 * f + 1]))
        copies[-1].start()
    for c in range(3):
        second_slab.append(pack_planes([(x * 16 + f * 8, ee[f, c, x, pl.ds(TOP, ny), :])
                                        for x in range(nx) for f in range(2)]))
    own = slab_gradient(mine, first_slab, second_slab, ny)

    low01, low2 = halo[9, :, pl.ds(0, LANES)], halo[9, :, pl.ds(LANES, LANES)]
    high01, high2 = halo[19, :, pl.ds(0, LANES)], halo[19, :, pl.ds(LANES, LANES)]
    lane = lane_of(low01.shape)

    def join(below, middle, above):
        return jnp.where(lane < 32, below, jnp.where(lane < 96, middle, above))

    m = [mirror[c] for c in range(3)]
    e = [join(turn(high01, -32), turn(m[0], 32), turn(low01, 96)),
         join(high01, turn(m[1], 32), turn(low01, 64)),
         join(turn(high2, -32), turn(m[2], 32), turn(low2, 96))]
    h = [join(turn(high01, -96), turn(m[0], -32), turn(low01, 32)),
         join(turn(high01, -64), turn(m[1], -32), low01),
         join(turn(high2, -96), turn(m[2], -32), turn(low2, 32))]
    k = join(high2, turn(mirror[3], 32), turn(low2, 64))
    inside = k > 0

    def ahead(a, axis):
        return (turn(a, -16), up_y(a), turn(a, -1))[axis] - a

    def behind(a, axis):
        return a - (turn(a, 16), down_y(a), turn(a, 1))[axis]

    slabs = []
    for _ in range(2):
        h = [jnp.where(inside, h[c] - COURANT * (ahead(e[(c + 2) % 3], (c + 1) % 3)
                                                 - ahead(e[(c + 1) % 3], (c + 2) % 3)), 0.0)
             for c in range(3)]
        e = [e[c] + k * (behind(h[(c + 2) % 3], (c + 1) % 3) - behind(h[(c + 1) % 3], (c + 2) % 3))
             for c in range(3)]
        slabs.append([turn(e[c], -32)[TOP:END] for c in range(3)])
    other = slab_gradient(theirs, slabs[0], slabs[1], ny)

    weight, _, partner = small_parts(mine)
    weight_m, _, _ = small_parts(theirs)
    slab_rows(other, table, square, nx)
    table[...] = table[...] * weight_m
    got = mirror_take(table, partner, ny)
    slab_rows(own, lines, square, nx)
    lines[...] = 0.5 * (lines[...] * weight + got)
    for p in range(PLANES):
        grad[p] = lines[pl.ds(p * nx, nx), pl.ds(0, ny)]
    for copy in copies:
        copy.wait()


def call(kernel, outs, args, scratch=(), name=None, any_in=False, any_out=0):
    spaces = lambda count, far: [pl.BlockSpec(memory_space=pltpu.HBM if i < far else pltpu.VMEM)
                                 for i in range(count)]
    return pl.pallas_call(
        kernel,
        out_shape=outs,
        in_specs=spaces(len(args), len(args) if any_in else 0),
        out_specs=spaces(len(outs), any_out),
        scratch_shapes=list(scratch),
        compiler_params=pltpu.CompilerParams(vmem_limit_bytes=FAR_LIMIT if any_in else VMEM_LIMIT),
        cost_estimate=pl.CostEstimate(flops=4_000_000, bytes_accessed=4_000_000, transcendentals=0),
        name=name,
    )(*args)


def swapped(far, near, axis):
    def pairs(first):
        lows = range(first, lax.axis_size(axis) - 1, 2)
        return [(i, i + 1) for i in lows] + [(i + 1, i) for i in lows]

    return lax.ppermute(far, axis, pairs(1)), lax.ppermute(near, axis, pairs(0))


def mirrored(block, axis):
    size = lax.axis_size(axis)
    return lax.ppermute(block, axis, [(i, size - 1 - i) for i in range(size)])


def per_device(e_fwd, h_fwd, e_adj, h_adj, eps_back, density, design_mask, partner_map, mon_fwd, mon_adj):
    _, nx, ny, nz = e_fwd.shape
    shape = lambda *dims: jax.ShapeDtypeStruct(dims, F32)
    vmem = lambda *dims: pltpu.VMEM(dims, F32)
    square = vmem(LANES, LANES)
    lines = vmem(PLANES * nx, LANES)
    block = shape(nx, ny, nz)
    fields = [e_fwd, h_fwd, e_adj, h_adj]

    mine, = call(
        message_kernel, [shape(MESSAGE, LANES)],
        fields + [eps_back, density, design_mask, partner_map, mon_fwd, mon_adj],
        [vmem(2, 2, 3, nx, ny, nz), vmem(nx, ny, nz), vmem(*density.shape),
         pltpu.VMEM((2,) + density.shape, jnp.int32), vmem(2, *mon_fwd.shape),
         square, pltpu.SemaphoreType.DMA((10,))], name="message", any_in=True)
    theirs = mirrored(mine, "gx")
    bulk_shape = shape(9 * ny, nz)
    bulk = call(bulk_kernel, [bulk_shape, bulk_shape], fields + [eps_back], name="bulk")
    bulk_far, bulk_near = swapped(*bulk, "gx")
    y_shape = shape(2 * (13 * nx) + 8, nz)
    coef, mirror_coef, y_far, y_near = call(
        coef_kernel, [block, shape(ny, LANES), y_shape, y_shape], [eps_back, mine, theirs] + fields,
        [lines, lines, square], name="coefficient")
    y_far, y_near = swapped(y_far, y_near, "gy")
    x_shape = shape(9 * 8 + ny + 4, nz)
    tile = shape(13 * nx, 8, nz)
    tops, ends, mirror, x_far, x_near = call(
        edges_kernel, [tile, tile, shape(4, FRAME, LANES), x_shape, x_shape],
        fields + [coef, mirror_coef, theirs, y_far, y_near],
        [vmem(*x_shape.shape)] * 2, name="edges")
    x_far, x_near = swapped(x_far, x_near, "gx")
    ef, hf, ea, ha, grad = call(
        step_kernel, [shape(*e_fwd.shape)] * 4 + [shape(*density.shape)],
        fields + [coef, tops, ends, mirror, bulk_far, bulk_near, x_far, x_near, mine, theirs],
        [vmem(2, 3, nx + 1, FRAME, nz), vmem(2, 3, nx + 1, FRAME, nz), vmem(20, FRAME, nz),
         square, lines, lines, pltpu.SemaphoreType.DMA((4,))], name="steps", any_out=4)
    return ef, hf, ea, ha, grad


def solution(mesh):
    grid = P(None, "gx", "gy", None)
    slab = P(None, "gx", "gy")
    monitor = P(None, None, None, "gx", "gy")
    return jax.shard_map(
        per_device,
        mesh=mesh,
        in_specs=(grid, grid, grid, grid, P("gx", "gy", None), slab, slab, slab, monitor, monitor),
        out_specs=(grid, grid, grid, grid, slab),
        check_vma=False,
    )
```

```python
import math

import jax
import jax.numpy as jnp
from jax import lax
from jax.experimental import pallas as pl
from jax.experimental.pallas import tpu as pltpu
from jax.sharding import PartitionSpec as P

PLANES = 4
Z0 = 126
COURANT = 0.5
OMEGA = 0.7
CONTRAST = 10.0
F32 = jnp.float32
VMEM_LIMIT = 32 * 1024 * 1024
FAR_LIMIT = 60 * 1024 * 1024

LANES = 128
FRAME = 48
TOP, END = 8, 40
WINDOW = 8
SHIFT = LANES - (Z0 - 2)
ROW_EPS, ROW_MON, MESSAGE = 96, 128, 192


def lane_of(shape):
    return lax.broadcasted_iota(jnp.int32, shape, len(shape) - 1)


def row_of(shape):
    return lax.broadcasted_iota(jnp.int32, shape, len(shape) - 2)


def turn(a, shift):
    shift = shift % a.shape[1]
    return pltpu.roll(a, shift, 1) if shift else a


def up_y(a):
    return pltpu.roll(a, a.shape[0] - 1, 0)


def down_y(a):
    return pltpu.roll(a, 1, 0)


def up_z(a):
    n = a.shape[1]
    return jnp.where(lane_of(a.shape) == n - 1, 0.0, pltpu.roll(a, n - 1, 1))


def down_z(a):
    return jnp.where(lane_of(a.shape) == 0, 0.0, pltpu.roll(a, 1, 1))


def is_odd(axis):
    return lax.axis_index(axis) % 2 == 1


def ordered(odd, up, down):
    return jnp.where(odd, up, down), jnp.where(odd, down, up)


def pack_planes(planes):
    total = None
    for offset, plane in planes:
        near = jnp.where(lane_of((plane.shape[0], LANES)) >= LANES // 2,
                         plane[:, :LANES], plane[:, LANES:2 * LANES])
        part = turn(near, SHIFT + offset)
        lane = lane_of(part.shape)
        inside = (lane >= offset) & (lane < offset + WINDOW)
        total = jnp.where(inside, part, 0.0 if total is None else total)
    return total


def flipped(a, square):
    square[...] = jnp.zeros_like(square)
    square[pl.ds(0, a.shape[0]), pl.ds(0, a.shape[1])] = a
    return jnp.transpose(square[...])


def message_kernel(ef, hf, ea, ha, eps, density, mask, partner, mon_f, mon_a, message,
                   fields, eps_in, small_f, small_i, mons, square, sems):
    nx, ny = ef.shape[1], ef.shape[2]
    copies = []
    for f, (e, h) in enumerate(((ef, hf), (ea, ha))):
        for k, source in enumerate((e, h)):
            copies.append(pltpu.make_async_copy(source, fields.at[f, k], sems.at[2 * f + k]))
    copies.append(pltpu.make_async_copy(eps, eps_in, sems.at[4]))
    copies.append(pltpu.make_async_copy(density, small_f, sems.at[5]))
    copies.append(pltpu.make_async_copy(mask, small_i.at[0], sems.at[6]))
    copies.append(pltpu.make_async_copy(partner, small_i.at[1], sems.at[7]))
    copies.append(pltpu.make_async_copy(mon_f, mons.at[0], sems.at[8]))
    copies.append(pltpu.make_async_copy(mon_a, mons.at[1], sems.at[9]))
    for copy in copies:
        copy.start()
    message[pl.ds(ROW_EPS, MESSAGE - ROW_EPS), :] = jnp.zeros((MESSAGE - ROW_EPS, LANES), F32)
    for copy in copies[4:]:
        copy.wait()
    for half, components in ((0, (0, 1)), (1, (2,))):
        square[...] = jnp.zeros_like(square)
        for k, c in enumerate(components):
            for f in range(2):
                for x in range(nx):
                    base = k * 64 + x * 16 + f * 8 + 2
                    square[pl.ds(base, PLANES), pl.ds(0, ny)] = mons[f, 0, c, :, x, :]
                    for p in range(PLANES):
                        at = (base + 4 + p) % LANES
                        square[pl.ds(at, 1), pl.ds(0, ny)] = mons[f, 1, c, p, pl.ds(x, 1), :]
        message[pl.ds(ROW_MON + 32 * half, ny), :] = jnp.transpose(square[...])[:ny]
    own_eps = [(x * 16 + f * 8, eps_in[x]) for x in range(nx) for f in range(2)]
    square[...] = jnp.zeros_like(square)
    for p in range(PLANES):
        square[pl.ds(p * nx, nx), pl.ds(0, ny)] = CONTRAST * small_i[0, p].astype(F32)
        square[pl.ds(16 + p * nx, nx), pl.ds(0, ny)] = small_f[p]
        square[pl.ds(32 + p * nx, nx), pl.ds(0, ny)] = small_i[1, p].astype(F32)
    small = turn(square[pl.ds(0, 32), :], 64)
    index = turn(square[pl.ds(32, 32), :], 96)
    message[pl.ds(ROW_EPS, ny), :] = pack_planes(own_eps) + small + index
    for copy in copies[:4]:
        copy.wait()
    for c in range(3):
        message[pl.ds(c * 32, ny), :] = pack_planes(
            [(k * 64 + x * 16 + f * 8, fields[f, k, c, x])
             for k in range(2) for x in range(nx) for f in range(2)])


def small_parts(message):
    weight = turn(message[pl.ds(ROW_EPS, 16), :], -64)
    density = turn(message[pl.ds(ROW_EPS + 16, 16), :], -64)
    partner = turn(message[pl.ds(ROW_EPS, 16), :], -96)
    return weight, density, partner


def mirror_take(table, partner, ny):
    inside = lane_of(partner.shape) < ny
    at = jnp.where(inside, partner, 0.0).astype(jnp.int32)
    row, lane = at // ny, at % ny
    got = jnp.zeros(at.shape, F32)
    for r in range(table.shape[0]):
        line = jnp.broadcast_to(table[pl.ds(r, 1), :], at.shape)
        got = jnp.where(row == r, jnp.take_along_axis(line, lane, axis=1), got)
    return got


def spread_slab(values, lines, square, nx, ny):
    lines[...] = values
    square[...] = jnp.zeros_like(square)
    for p in range(PLANES):
        for x in range(nx):
            row = lines[pl.ds(p * nx + x, 1), :]
            square[pl.ds(x * 16 + 2 + p, 1), :] = row
            square[pl.ds(x * 16 + 10 + p, 1), :] = row
    return jnp.transpose(square[...])[:ny]


def coef_kernel(bulk_far, bulk_near, eps, mine, theirs, ef, hf, ea, ha, coef, mirror_coef, y_far, y_near, table, lines, square):
    del bulk_far, bulk_near
    nx = eps.shape[0]
    ny = END - TOP
    weight, density, partner = small_parts(mine)
    weight_m, density_m, partner_m = small_parts(theirs)
    table[...] = density_m
    extra = weight * (0.5 * (density + mirror_take(table, partner, ny)))
    table[...] = density
    extra_m = weight_m * (0.5 * (density_m + mirror_take(table, partner_m, ny)))
    packed = spread_slab(extra, lines, square, nx, ny)
    lane = lane_of(packed.shape)
    for x in range(nx):
        part = turn(packed, -16 * x - SHIFT)
        low = jnp.where(lane >= Z0, part, 0.0)
        high = jnp.where(lane < Z0 + PLANES - LANES, part, 0.0)
        coef[x] = COURANT / (eps[x] + jnp.concatenate([low, high], 1))
    packed = theirs[pl.ds(ROW_EPS, ny), :] + spread_slab(extra_m, lines, square, nx, ny)
    mirror_coef[...] = jnp.where(lane < 64, COURANT / jnp.where(lane < 64, packed, 1.0), 0.0)
    odd = is_odd("gy")

    def put(at, ref, lanes):
        far, near = ordered(odd, ref[pl.ds(ny - 2, 2), :], ref[pl.ds(0, 2), :])
        y_far[pl.ds(at, 2), pl.ds(0, lanes)] = far
        y_near[pl.ds(at, 2), pl.ds(0, lanes)] = near

    for f, pair in enumerate(((ef, hf), (ea, ha))):
        for k, field in enumerate(pair):
            for c in range(3):
                for x in range(nx):
                    put(2 * plane_index(f, k, c, x, nx), field.at[c, x], y_far.shape[1])
    for x in range(nx):
        put(24 * nx + 2 * x, coef.at[x], y_far.shape[1])
    rest = jnp.zeros((8, y_far.shape[1]), F32)
    y_far[pl.ds(26 * nx, 8), :] = rest
    y_near[pl.ds(26 * nx, 8), :] = rest
    for c in range(3):
        put(26 * nx + 2 * c, theirs.at[pl.ds(c * 32, ny), :], LANES)
    put(26 * nx + 6, mirror_coef, LANES)


def plane_index(f, k, c, x, nx):
    return ((f * 2 + k) * 3 + c) * nx + x


def framed(middle, tops, ends, i):
    return jnp.concatenate([tops[i], middle, ends[i]], 0)


def edge_planes(part, ks, nx, mark):
    up, down = [], []
    last = nx - 1
    for f in range(2):
        e = lambda c, x: part(f, 0, c, x)
        h = lambda c, x: part(f, 1, c, x)
        k = ks[last]
        ex, ey, ez = e(0, last), e(1, last), e(2, last)
        ex_b, ey_b, ez_b = e(0, last - 1), e(1, last - 1), e(2, last - 1)
        hy_b = mark(h(1, last - 1) - COURANT * ((up_z(ex_b) - ex_b) - (ez - ez_b)), last - 1)
        hz_b = mark(h(2, last - 1) - COURANT * ((ey - ey_b) - (up_y(ex_b) - ex_b)), last - 1)
        hx = mark(h(0, last) - COURANT * ((up_y(ez) - ez) - (up_z(ey) - ey)), last)
        hy = mark(h(1, last) - COURANT * ((up_z(ex) - ex) + ez), last)
        hz = mark(h(2, last) - COURANT * (-ey - (up_y(ex) - ex)), last)
        ex = ex + k * ((hz - down_y(hz)) - (hy - down_z(hy)))
        ey = ey + k * ((hx - down_z(hx)) - (hz - hz_b))
        ez = ez + k * ((hy - hy_b) - (hx - down_y(hx)))
        up += [hy, hz, mark(hy - COURANT * ((up_z(ex) - ex) + ez), last),
               mark(hz - COURANT * (-ey - (up_y(ex) - ex)), last)]
        k = ks[0]
        ex, ey, ez = e(0, 0), e(1, 0), e(2, 0)
        hx = mark(h(0, 0) - COURANT * ((up_y(ez) - ez) - (up_z(ey) - ey)), 0)
        hy = mark(h(1, 0) - COURANT * ((up_z(ex) - ex) - (e(2, 1) - ez)), 0)
        hz = mark(h(2, 0) - COURANT * ((e(1, 1) - ey) - (up_y(ex) - ex)), 0)
        down += [ey, ez, ey + k * ((hx - down_z(hx)) - hz), ez + k * (hy - (hx - down_y(hx)))]
    return up + [ks[last]], down + [ks[0]]


LATER = (2, 3, 6, 7, 8)
SLIM = 6


def bulk_kernel(ef, hf, ea, ha, eps, message, x_far, x_near):
    del message
    nx, ny = eps.shape[0], eps.shape[1]
    fields = ((ef, hf), (ea, ha))
    ks = [COURANT / eps[x] if x in (0, nx - 1) else None for x in range(nx)]
    up, down = edge_planes(lambda f, k, c, x: fields[f][k][c, x], ks, nx, lambda v, x: v)
    odd = is_odd("gx")
    for i, planes in enumerate(zip(up, down)):
        far, near = ordered(odd, *planes)
        x_far[pl.ds(i * ny, ny), :] = far
        x_near[pl.ds(i * ny, ny), :] = near


def edges_kernel(ef, hf, ea, ha, coef, mirror_coef, theirs, y_far, y_near,
                 tops, ends, mirror, x_far, x_near, x_up, x_down):
    nx, ny = coef.shape[0], coef.shape[1]
    fields = ((ef, hf), (ea, ha))
    tops[...] = jnp.zeros_like(tops)
    ends[...] = jnp.zeros_like(ends)
    mirror[...] = jnp.zeros_like(mirror)
    for c in range(3):
        mirror[c, pl.ds(TOP, ny), :] = theirs[pl.ds(c * 32, ny), :]
    mirror[3, pl.ds(TOP, ny), :] = mirror_coef[...]
    odd = is_odd("gy")

    def came(at, lanes):
        high, low = ordered(odd, y_far[pl.ds(at, 2), pl.ds(0, lanes)], y_near[pl.ds(at, 2), pl.ds(0, lanes)])
        return low, high

    for i in range(13 * nx):
        low, high = came(2 * i, y_far.shape[1])
        tops[i, pl.ds(TOP - 2, 2), :] = low
        ends[i, pl.ds(0, 2), :] = high
    for c in range(4):
        low, high = came(26 * nx + 2 * c, LANES)
        mirror[c, pl.ds(TOP - 2, 2), :] = low
        mirror[c, pl.ds(END, 2), :] = high

    def part(f, k, c, x):
        return framed(fields[f][k][c, x], tops, ends, plane_index(f, k, c, x, nx))

    ks = [framed(coef[x], tops, ends, 12 * nx + x) for x in range(nx)]
    up, down = edge_planes(part, ks, nx, lambda v, x: jnp.where(ks[x] > 0, v, 0.0))
    m = [mirror[c] for c in range(3)]
    km = mirror[3]
    lane = lane_of(km.shape)
    first = lane % 64 < 32
    up_m = [jnp.where(first, m[0], turn(m[1], 32)), jnp.where(first, m[2], turn(km, 32))]
    down_m = [jnp.where(first, turn(m[1], -32), m[0]), jnp.where(first, turn(km, -32), m[2])]
    for out, planes, window, base in ((x_up, up, up_m, 96), (x_down, down, down_m, 64)):
        for i, plane in enumerate(planes):
            out[pl.ds(8 * i, 4), :] = plane[TOP - 2:TOP + 2]
            out[pl.ds(8 * i + 4, 4), :] = plane[END - 2:END + 2]
        side = window[1]
        for i, plane in enumerate(LATER):
            plane = planes[plane]
            near = jnp.where(lane >= LANES // 2, plane[:, :LANES], plane[:, LANES:])
            part_in = turn(near, SHIFT + base + SLIM * i - 1)
            inside = (lane >= base + SLIM * i) & (lane < base + SLIM * (i + 1))
            side = jnp.where(inside, part_in, side)
        value = jnp.concatenate([window[0], side], 1)
        out[pl.ds(72, ny), :] = value[TOP:END]
        out[pl.ds(72 + ny, 2), :] = value[TOP - 2:TOP]
        out[pl.ds(74 + ny, 2), :] = value[END:END + 2]
    x_far[...], x_near[...] = ordered(is_odd("gx"), x_up[...], x_down[...])


def slab_gradient(message, first, second, ny):
    total = None
    for c in range(3):
        mon = message[pl.ds(ROW_MON + 32 * (c // 2), ny), :]
        real = turn(mon, -64 * (c % 2))
        imag = turn(real, -4)
        real = real + math.cos(OMEGA) * first[c] + math.cos(2 * OMEGA) * second[c]
        imag = imag - math.sin(OMEGA) * first[c] - math.sin(2 * OMEGA) * second[c]
        term = real * turn(real, -8) - imag * turn(imag, -8)
        total = term if total is None else total + term
    return total


def slab_rows(packed, out, square, nx):
    square[...] = flipped(packed, square)
    for p in range(PLANES):
        for x in range(nx):
            out[pl.ds(p * nx + x, 1), :] = square[pl.ds(x * 16 + 2 + p, 1), :]


def step_kernel(ef_in, hf_in, ea_in, ha_in, coef, tops, ends, mirror, bulk_far_1, bulk_near_1, bulk_far_2, bulk_near_2,
                x_far, x_near, mine, theirs,
                ef_out, hf_out, ea_out, ha_out, grad,
                ee, hh, halo, square, table, lines, sems):
    nx, ny, nz = coef.shape

    fields = ((ef_in, hf_in), (ea_in, ha_in))
    lane = lane_of((ny, LANES))
    odd = is_odd("gx")
    for slot, base in ((0, 96), (10, 64)):
        def source_at(row, rows, slot=slot):
            pair = (x_near, x_far) if slot == 0 else (x_far, x_near)
            return jnp.where(odd, pair[0][pl.ds(row, rows), :], pair[1][pl.ds(row, rows), :])

        def bulk_at(row, rows, slot=slot):
            far = bulk_far_1[pl.ds(row, rows), :] + bulk_far_2[pl.ds(row, rows), :]
            near = bulk_near_1[pl.ds(row, rows), :] + bulk_near_2[pl.ds(row, rows), :]
            return jnp.where(odd, near, far) if slot == 0 else jnp.where(odd, far, near)

        halo[slot + 9, pl.ds(0, TOP), :] = jnp.zeros((TOP, nz), F32)
        halo[slot + 9, pl.ds(END, TOP), :] = jnp.zeros((TOP, nz), F32)
        window = source_at(72, ny)
        halo[slot + 9, pl.ds(TOP, ny), :] = window
        halo[slot + 9, pl.ds(TOP - 2, 2), :] = source_at(72 + ny, 2)
        halo[slot + 9, pl.ds(END, 2), :] = source_at(74 + ny, 2)
        side = window[:, LANES:]
        for plane in range(9):
            at = slot + plane
            halo[at, pl.ds(0, TOP), :] = jnp.zeros((TOP, nz), F32)
            halo[at, pl.ds(END, TOP), :] = jnp.zeros((TOP, nz), F32)
            value = bulk_at(plane * ny, ny)
            if plane in LATER:
                near = turn(side, 1 - SHIFT - base - SLIM * LATER.index(plane))
                value = jnp.concatenate(
                    [jnp.where(lane >= Z0 - 1, near, value[:, :LANES]),
                     jnp.where(lane < Z0 + PLANES + 1 - LANES, near, value[:, LANES:])], 1)
            halo[at, pl.ds(TOP, ny), :] = value
            halo[at, pl.ds(TOP - 2, 4), :] = source_at(8 * plane, 4)
            halo[at, pl.ds(END - 2, 4), :] = source_at(8 * plane + 4, 4)
    k_low, k_high = halo[8], halo[18]

    def part(f, k, c, x):
        return framed(fields[f][k][c, x], tops, ends, plane_index(f, k, c, x, nx))

    def inverse(x):
        return framed(coef[x], tops, ends, 12 * nx + x)

    copies = []
    first_slab, second_slab = [], []
    for f in range(2):
        ey0, ez0 = part(f, 0, 1, 0), part(f, 0, 2, 0)
        dhy = jnp.where(k_low > 0, COURANT * ez0, 0.0)
        dhz = jnp.where(k_low > 0, -COURANT * ey0, 0.0)
        hh[f, 1, 0] = halo[4 * f] + dhy
        hh[f, 2, 0] = halo[4 * f + 1] + dhz
        for x in range(nx):
            inside = inverse(x) > 0
            ex, ey, ez = part(f, 0, 0, x), part(f, 0, 1, x), part(f, 0, 2, x)
            ey_n = part(f, 0, 1, x + 1) if x + 1 < nx else halo[10 + 4 * f]
            ez_n = part(f, 0, 2, x + 1) if x + 1 < nx else halo[10 + 4 * f + 1]
            hx, hy, hz = part(f, 1, 0, x), part(f, 1, 1, x), part(f, 1, 2, x)
            hh[f, 0, x + 1] = jnp.where(inside, hx - COURANT * ((up_y(ez) - ez) - (up_z(ey) - ey)), 0.0)
            hh[f, 1, x + 1] = jnp.where(inside, hy - COURANT * ((up_z(ex) - ex) - (ez_n - ez)), 0.0)
            hh[f, 2, x + 1] = jnp.where(inside, hz - COURANT * ((ey_n - ey) - (up_y(ex) - ex)), 0.0)
        for x in range(nx):
            k = inverse(x)
            hx, hy, hz = hh[f, 0, x + 1], hh[f, 1, x + 1], hh[f, 2, x + 1]
            ee[f, 0, x] = part(f, 0, 0, x) + k * ((hz - down_y(hz)) - (hy - down_z(hy)))
            ee[f, 1, x] = part(f, 0, 1, x) + k * ((hx - down_z(hx)) - (hz - hh[f, 2, x]))
            ee[f, 2, x] = part(f, 0, 2, x) + k * ((hy - hh[f, 1, x]) - (hx - down_y(hx)))
        ee[f, 1, nx] = halo[10 + 4 * f + 2] + k_high * hh[f, 2, nx]
        ee[f, 2, nx] = halo[10 + 4 * f + 3] - k_high * hh[f, 1, nx]
        dex = k_low * ((dhz - down_y(dhz)) - (dhy - down_z(dhy)))
        dey = -k_low * dhz
        dez = k_low * dhy
        hh[f, 1, 0] = jnp.where(
            k_low > 0, halo[4 * f + 2] + dhy - COURANT * ((up_z(dex) - dex) - (ee[f, 2, 0] - dez)), 0.0)
        hh[f, 2, 0] = jnp.where(
            k_low > 0, halo[4 * f + 3] + dhz - COURANT * ((ee[f, 1, 0] - dey) - (up_y(dex) - dex)), 0.0)
        for x in range(nx):
            inside = inverse(x) > 0
            ex, ey, ez = ee[f, 0, x], ee[f, 1, x], ee[f, 2, x]
            hh[f, 0, x + 1] = jnp.where(
                inside, hh[f, 0, x + 1] - COURANT * ((up_y(ez) - ez) - (up_z(ey) - ey)), 0.0)
            hh[f, 1, x + 1] = jnp.where(
                inside, hh[f, 1, x + 1] - COURANT * ((up_z(ex) - ex) - (ee[f, 2, x + 1] - ez)), 0.0)
            hh[f, 2, x + 1] = jnp.where(
                inside, hh[f, 2, x + 1] - COURANT * ((ee[f, 1, x + 1] - ey) - (up_y(ex) - ex)), 0.0)
        copies.append(pltpu.make_async_copy(
            hh.at[f, :, pl.ds(1, nx), pl.ds(TOP, ny), :], (hf_out, ha_out)[f], sems.at[2 * f]))
        copies[-1].start()
    for c in range(3):
        first_slab.append(pack_planes([(x * 16 + f * 8, ee[f, c, x, pl.ds(TOP, ny), :])
                                       for x in range(nx) for f in range(2)]))
    for f in range(2):
        for x in range(nx):
            k = inverse(x)
            hx, hy, hz = hh[f, 0, x + 1], hh[f, 1, x + 1], hh[f, 2, x + 1]
            ee[f, 0, x] = ee[f, 0, x] + k * ((hz - down_y(hz)) - (hy - down_z(hy)))
            ee[f, 1, x] = ee[f, 1, x] + k * ((hx - down_z(hx)) - (hz - hh[f, 2, x]))
            ee[f, 2, x] = ee[f, 2, x] + k * ((hy - hh[f, 1, x]) - (hx - down_y(hx)))
        copies.append(pltpu.make_async_copy(
            ee.at[f, :, pl.ds(0, nx), pl.ds(TOP, ny), :], (ef_out, ea_out)[f], sems.at[2 * f + 1]))
        copies[-1].start()
    for c in range(3):
        second_slab.append(pack_planes([(x * 16 + f * 8, ee[f, c, x, pl.ds(TOP, ny), :])
                                        for x in range(nx) for f in range(2)]))
    own = slab_gradient(mine, first_slab, second_slab, ny)

    low01, low2 = halo[9, :, pl.ds(0, LANES)], halo[9, :, pl.ds(LANES, LANES)]
    high01, high2 = halo[19, :, pl.ds(0, LANES)], halo[19, :, pl.ds(LANES, LANES)]
    lane = lane_of(low01.shape)

    def join(below, middle, above):
        return jnp.where(lane < 32, below, jnp.where(lane < 96, middle, above))

    m = [mirror[c] for c in range(3)]
    e = [join(turn(high01, -32), turn(m[0], 32), turn(low01, 96)),
         join(high01, turn(m[1], 32), turn(low01, 64)),
         join(turn(high2, -32), turn(m[2], 32), turn(low2, 96))]
    h = [join(turn(high01, -96), turn(m[0], -32), turn(low01, 32)),
         join(turn(high01, -64), turn(m[1], -32), low01),
         join(turn(high2, -96), turn(m[2], -32), turn(low2, 32))]
    k = join(high2, turn(mirror[3], 32), turn(low2, 64))
    inside = k > 0

    def ahead(a, axis):
        return (turn(a, -16), up_y(a), turn(a, -1))[axis] - a

    def behind(a, axis):
        return a - (turn(a, 16), down_y(a), turn(a, 1))[axis]

    slabs = []
    for _ in range(2):
        h = [jnp.where(inside, h[c] - COURANT * (ahead(e[(c + 2) % 3], (c + 1) % 3)
                                                 - ahead(e[(c + 1) % 3], (c + 2) % 3)), 0.0)
             for c in range(3)]
        e = [e[c] + k * (behind(h[(c + 2) % 3], (c + 1) % 3) - behind(h[(c + 1) % 3], (c + 2) % 3))
             for c in range(3)]
        slabs.append([turn(e[c], -32)[TOP:END] for c in range(3)])
    other = slab_gradient(theirs, slabs[0], slabs[1], ny)

    weight, _, partner = small_parts(mine)
    weight_m, _, _ = small_parts(theirs)
    slab_rows(other, table, square, nx)
    table[...] = table[...] * weight_m
    got = mirror_take(table, partner, ny)
    slab_rows(own, lines, square, nx)
    lines[...] = 0.5 * (lines[...] * weight + got)
    for p in range(PLANES):
        grad[p] = lines[pl.ds(p * nx, nx), pl.ds(0, ny)]
    for copy in copies:
        copy.wait()


def call(kernel, outs, args, scratch=(), name=None, any_in=False, any_out=0):
    spaces = lambda count, far: [pl.BlockSpec(memory_space=pltpu.HBM if i < far else pltpu.VMEM)
                                 for i in range(count)]
    return pl.pallas_call(
        kernel,
        out_shape=outs,
        in_specs=spaces(len(args), len(args) if any_in else 0),
        out_specs=spaces(len(outs), any_out),
        scratch_shapes=list(scratch),
        compiler_params=pltpu.CompilerParams(vmem_limit_bytes=FAR_LIMIT if any_in else VMEM_LIMIT),
        cost_estimate=pl.CostEstimate(flops=4_000_000, bytes_accessed=4_000_000, transcendentals=0),
        name=name,
    )(*args)


def swapped(far, near, axis, start=0, stop=None):
    size = lax.axis_size(axis)

    def pairs(first):
        lows = [i for i in range(first, size - 1, 2) if start <= i < (size if stop is None else stop)]
        return [(i, i + 1) for i in lows] + [(i + 1, i) for i in lows]

    return lax.ppermute(far, axis, pairs(1)), lax.ppermute(near, axis, pairs(0))


def mirrored(block, axis):
    size = lax.axis_size(axis)
    return lax.ppermute(block, axis, [(i, size - 1 - i) for i in range(size)])


def per_device(e_fwd, h_fwd, e_adj, h_adj, eps_back, density, design_mask, partner_map, mon_fwd, mon_adj):
    _, nx, ny, nz = e_fwd.shape
    shape = lambda *dims: jax.ShapeDtypeStruct(dims, F32)
    vmem = lambda *dims: pltpu.VMEM(dims, F32)
    square = vmem(LANES, LANES)
    lines = vmem(PLANES * nx, LANES)
    block = shape(nx, ny, nz)
    fields = [e_fwd, h_fwd, e_adj, h_adj]

    mine, = call(
        message_kernel, [shape(MESSAGE, LANES)],
        fields + [eps_back, density, design_mask, partner_map, mon_fwd, mon_adj],
        [vmem(2, 2, 3, nx, ny, nz), vmem(nx, ny, nz), vmem(*density.shape),
         pltpu.VMEM((2,) + density.shape, jnp.int32), vmem(2, *mon_fwd.shape),
         square, pltpu.SemaphoreType.DMA((10,))], name="message", any_in=True)
    theirs = mirrored(mine, "gx")
    bulk_shape = shape(9 * ny, nz)
    bulk = call(bulk_kernel, [bulk_shape, bulk_shape], fields + [eps_back, mine], name="bulk")
    half = lax.axis_size("gx") // 2
    bulk_lower = swapped(*bulk, "gx", stop=half)
    bulk_upper = swapped(*bulk, "gx", start=half)
    y_shape = shape(2 * (13 * nx) + 8, nz)
    coef, mirror_coef, y_far, y_near = call(
        coef_kernel, [block, shape(ny, LANES), y_shape, y_shape], [*bulk_lower, eps_back, mine, theirs] + fields,
        [lines, lines, square], name="coefficient")
    y_far, y_near = swapped(y_far, y_near, "gy")
    x_shape = shape(9 * 8 + ny + 4, nz)
    tile = shape(13 * nx, 8, nz)
    tops, ends, mirror, x_far, x_near = call(
        edges_kernel, [tile, tile, shape(4, FRAME, LANES), x_shape, x_shape],
        fields + [coef, mirror_coef, theirs, y_far, y_near],
        [vmem(*x_shape.shape)] * 2, name="edges")
    x_far, x_near = swapped(x_far, x_near, "gx")
    ef, hf, ea, ha, grad = call(
        step_kernel, [shape(*e_fwd.shape)] * 4 + [shape(*density.shape)],
        fields + [coef, tops, ends, mirror, *bulk_lower, *bulk_upper, x_far, x_near, mine, theirs],
        [vmem(2, 3, nx + 1, FRAME, nz), vmem(2, 3, nx + 1, FRAME, nz), vmem(20, FRAME, nz),
         square, lines, lines, pltpu.SemaphoreType.DMA((4,))], name="steps", any_out=4)
    return ef, hf, ea, ha, grad


def solution(mesh):
    grid = P(None, "gx", "gy", None)
    slab = P(None, "gx", "gy")
    monitor = P(None, None, None, "gx", "gy")
    return jax.shard_map(
        per_device,
        mesh=mesh,
        in_specs=(grid, grid, grid, grid, P("gx", "gy", None), slab, slab, slab, monitor, monitor),
        out_specs=(grid, grid, grid, grid, slab),
        check_vma=False,
    )
```

```python
import math

import jax
import jax.numpy as jnp
from jax import lax
from jax.experimental import pallas as pl
from jax.experimental.pallas import tpu as pltpu
from jax.sharding import PartitionSpec as P

PLANES = 4
Z0 = 126
COURANT = 0.5
OMEGA = 0.7
CONTRAST = 10.0
F32 = jnp.float32
VMEM_LIMIT = 32 * 1024 * 1024
FAR_LIMIT = 60 * 1024 * 1024

LANES = 128
FRAME = 48
TOP, END = 8, 40
WINDOW = 8
SHIFT = LANES - (Z0 - 2)
ROW_EPS, ROW_MON, MESSAGE = 96, 128, 192


def lane_of(shape):
    return lax.broadcasted_iota(jnp.int32, shape, len(shape) - 1)


def row_of(shape):
    return lax.broadcasted_iota(jnp.int32, shape, len(shape) - 2)


def turn(a, shift):
    shift = shift % a.shape[1]
    return pltpu.roll(a, shift, 1) if shift else a


def up_y(a):
    return pltpu.roll(a, a.shape[0] - 1, 0)


def down_y(a):
    return pltpu.roll(a, 1, 0)


def up_z(a):
    n = a.shape[1]
    return jnp.where(lane_of(a.shape) == n - 1, 0.0, pltpu.roll(a, n - 1, 1))


def down_z(a):
    return jnp.where(lane_of(a.shape) == 0, 0.0, pltpu.roll(a, 1, 1))


def is_odd(axis):
    return lax.axis_index(axis) % 2 == 1


def ordered(odd, up, down):
    return jnp.where(odd, up, down), jnp.where(odd, down, up)


def pack_planes(planes):
    total = None
    for offset, plane in planes:
        near = jnp.where(lane_of((plane.shape[0], LANES)) >= LANES // 2,
                         plane[:, :LANES], plane[:, LANES:2 * LANES])
        part = turn(near, SHIFT + offset)
        lane = lane_of(part.shape)
        inside = (lane >= offset) & (lane < offset + WINDOW)
        total = jnp.where(inside, part, 0.0 if total is None else total)
    return total


def flipped(a, square):
    square[...] = jnp.zeros_like(square)
    square[pl.ds(0, a.shape[0]), pl.ds(0, a.shape[1])] = a
    return jnp.transpose(square[...])


def edge_planes(part, ks, nx, mark):
    up, down = [], []
    last = nx - 1
    for f in range(2):
        e = lambda c, x: part(f, 0, c, x)
        h = lambda c, x: part(f, 1, c, x)
        k = ks[last]
        ex, ey, ez = e(0, last), e(1, last), e(2, last)
        ex_b, ey_b, ez_b = e(0, last - 1), e(1, last - 1), e(2, last - 1)
        hy_b = mark(h(1, last - 1) - COURANT * ((up_z(ex_b) - ex_b) - (ez - ez_b)), last - 1)
        hz_b = mark(h(2, last - 1) - COURANT * ((ey - ey_b) - (up_y(ex_b) - ex_b)), last - 1)
        hx = mark(h(0, last) - COURANT * ((up_y(ez) - ez) - (up_z(ey) - ey)), last)
        hy = mark(h(1, last) - COURANT * ((up_z(ex) - ex) + ez), last)
        hz = mark(h(2, last) - COURANT * (-ey - (up_y(ex) - ex)), last)
        ex = ex + k * ((hz - down_y(hz)) - (hy - down_z(hy)))
        ey = ey + k * ((hx - down_z(hx)) - (hz - hz_b))
        ez = ez + k * ((hy - hy_b) - (hx - down_y(hx)))
        up += [hy, hz, mark(hy - COURANT * ((up_z(ex) - ex) + ez), last),
               mark(hz - COURANT * (-ey - (up_y(ex) - ex)), last)]
        k = ks[0]
        ex, ey, ez = e(0, 0), e(1, 0), e(2, 0)
        hx = mark(h(0, 0) - COURANT * ((up_y(ez) - ez) - (up_z(ey) - ey)), 0)
        hy = mark(h(1, 0) - COURANT * ((up_z(ex) - ex) - (e(2, 1) - ez)), 0)
        hz = mark(h(2, 0) - COURANT * ((e(1, 1) - ey) - (up_y(ex) - ex)), 0)
        down += [ey, ez, ey + k * ((hx - down_z(hx)) - hz), ez + k * (hy - (hx - down_y(hx)))]
    return up + [ks[last]], down + [ks[0]]


def write_bulk(part, eps, x_far, x_near):
    nx, ny = eps.shape[0], eps.shape[1]
    ks = [COURANT / eps[x] if x in (0, nx - 1) else None for x in range(nx)]
    odd = is_odd("gx")
    for i, planes in enumerate(zip(*edge_planes(part, ks, nx, lambda v, x: v))):
        far, near = ordered(odd, *planes)
        x_far[pl.ds(i * ny, ny), :] = far
        x_near[pl.ds(i * ny, ny), :] = near


def message_kernel(ef, hf, ea, ha, eps, density, mask, partner, mon_f, mon_a,
                   message, fields, eps_in, small_f, small_i, mons, square, sems):
    nx, ny = ef.shape[1], ef.shape[2]
    copies = []
    for f, (e, h) in enumerate(((ef, hf), (ea, ha))):
        for k, source in enumerate((e, h)):
            copies.append(pltpu.make_async_copy(source, fields.at[f, k], sems.at[2 * f + k]))
    copies.append(pltpu.make_async_copy(eps, eps_in, sems.at[4]))
    copies.append(pltpu.make_async_copy(density, small_f, sems.at[5]))
    copies.append(pltpu.make_async_copy(mask, small_i.at[0], sems.at[6]))
    copies.append(pltpu.make_async_copy(partner, small_i.at[1], sems.at[7]))
    copies.append(pltpu.make_async_copy(mon_f, mons.at[0], sems.at[8]))
    copies.append(pltpu.make_async_copy(mon_a, mons.at[1], sems.at[9]))
    for copy in copies:
        copy.start()
    message[pl.ds(ROW_EPS, MESSAGE - ROW_EPS), :] = jnp.zeros((MESSAGE - ROW_EPS, LANES), F32)
    for copy in copies[4:]:
        copy.wait()
    for half, components in ((0, (0, 1)), (1, (2,))):
        square[...] = jnp.zeros_like(square)
        for k, c in enumerate(components):
            for f in range(2):
                for x in range(nx):
                    base = k * 64 + x * 16 + f * 8 + 2
                    square[pl.ds(base, PLANES), pl.ds(0, ny)] = mons[f, 0, c, :, x, :]
                    for p in range(PLANES):
                        at = (base + 4 + p) % LANES
                        square[pl.ds(at, 1), pl.ds(0, ny)] = mons[f, 1, c, p, pl.ds(x, 1), :]
        message[pl.ds(ROW_MON + 32 * half, ny), :] = jnp.transpose(square[...])[:ny]
    own_eps = [(x * 16 + f * 8, eps_in[x]) for x in range(nx) for f in range(2)]
    square[...] = jnp.zeros_like(square)
    for p in range(PLANES):
        square[pl.ds(p * nx, nx), pl.ds(0, ny)] = CONTRAST * small_i[0, p].astype(F32)
        square[pl.ds(16 + p * nx, nx), pl.ds(0, ny)] = small_f[p]
        square[pl.ds(32 + p * nx, nx), pl.ds(0, ny)] = small_i[1, p].astype(F32)
    small = turn(square[pl.ds(0, 32), :], 64)
    index = turn(square[pl.ds(32, 32), :], 96)
    message[pl.ds(ROW_EPS, ny), :] = pack_planes(own_eps) + small + index
    for copy in copies[:4]:
        copy.wait()
    for c in range(3):
        message[pl.ds(c * 32, ny), :] = pack_planes(
            [(k * 64 + x * 16 + f * 8, fields[f, k, c, x])
             for k in range(2) for x in range(nx) for f in range(2)])


def bulk_kernel(ef, hf, ea, ha, eps, message, x_far, x_near):
    del message
    fields = ((ef, hf), (ea, ha))
    write_bulk(lambda f, k, c, x: fields[f][k][c, x], eps, x_far, x_near)


def small_parts(message):
    weight = turn(message[pl.ds(ROW_EPS, 16), :], -64)
    density = turn(message[pl.ds(ROW_EPS + 16, 16), :], -64)
    partner = turn(message[pl.ds(ROW_EPS, 16), :], -96)
    return weight, density, partner


def mirror_take(table, partner, ny):
    inside = lane_of(partner.shape) < ny
    at = jnp.where(inside, partner, 0.0).astype(jnp.int32)
    row, lane = at // ny, at % ny
    got = jnp.zeros(at.shape, F32)
    for r in range(table.shape[0]):
        line = jnp.broadcast_to(table[pl.ds(r, 1), :], at.shape)
        got = jnp.where(row == r, jnp.take_along_axis(line, lane, axis=1), got)
    return got


def spread_slab(values, lines, square, nx, ny):
    lines[...] = values
    square[...] = jnp.zeros_like(square)
    for p in range(PLANES):
        for x in range(nx):
            row = lines[pl.ds(p * nx + x, 1), :]
            square[pl.ds(x * 16 + 2 + p, 1), :] = row
            square[pl.ds(x * 16 + 10 + p, 1), :] = row
    return jnp.transpose(square[...])[:ny]


def coef_kernel(bulk_far, bulk_near, eps, mine, theirs, ef, hf, ea, ha, coef, mirror_coef, y_far, y_near, table, lines, square):
    del bulk_far, bulk_near
    nx = eps.shape[0]
    ny = END - TOP
    weight, density, partner = small_parts(mine)
    weight_m, density_m, partner_m = small_parts(theirs)
    table[...] = density_m
    extra = weight * (0.5 * (density + mirror_take(table, partner, ny)))
    table[...] = density
    extra_m = weight_m * (0.5 * (density_m + mirror_take(table, partner_m, ny)))
    packed = spread_slab(extra, lines, square, nx, ny)
    lane = lane_of(packed.shape)
    for x in range(nx):
        part = turn(packed, -16 * x - SHIFT)
        low = jnp.where(lane >= Z0, part, 0.0)
        high = jnp.where(lane < Z0 + PLANES - LANES, part, 0.0)
        coef[x] = COURANT / (eps[x] + jnp.concatenate([low, high], 1))
    packed = theirs[pl.ds(ROW_EPS, ny), :] + spread_slab(extra_m, lines, square, nx, ny)
    mirror_coef[...] = jnp.where(lane < 64, COURANT / jnp.where(lane < 64, packed, 1.0), 0.0)
    odd = is_odd("gy")

    def put(at, ref, lanes):
        far, near = ordered(odd, ref[pl.ds(ny - 2, 2), :], ref[pl.ds(0, 2), :])
        y_far[pl.ds(at, 2), pl.ds(0, lanes)] = far
        y_near[pl.ds(at, 2), pl.ds(0, lanes)] = near

    for f, pair in enumerate(((ef, hf), (ea, ha))):
        for k, field in enumerate(pair):
            for c in range(3):
                for x in range(nx):
                    put(2 * plane_index(f, k, c, x, nx), field.at[c, x], y_far.shape[1])
    for x in range(nx):
        put(24 * nx + 2 * x, coef.at[x], y_far.shape[1])
    rest = jnp.zeros((8, y_far.shape[1]), F32)
    y_far[pl.ds(26 * nx, 8), :] = rest
    y_near[pl.ds(26 * nx, 8), :] = rest
    for c in range(3):
        put(26 * nx + 2 * c, theirs.at[pl.ds(c * 32, ny), :], LANES)
    put(26 * nx + 6, mirror_coef, LANES)


def plane_index(f, k, c, x, nx):
    return ((f * 2 + k) * 3 + c) * nx + x


def framed(middle, tops, ends, i):
    return jnp.concatenate([tops[i], middle, ends[i]], 0)


ROWS_UP = ((7, 40), (7, 39), (8, 39), (8, 38, 39)) * 2 + ((7, 40),)
ROWS_DOWN = ((6, 7, 40), (7, 40), (7, 39), (8, 39)) * 2 + ((7, 40),)
FIXED = 20
LATER = (2, 3, 6, 7, 8)
SLIM = 6


def edges_kernel(ef, hf, ea, ha, coef, mirror_coef, theirs, y_far, y_near,
                 tops, ends, mirror, x_far, x_near, x_up, x_down):
    nx, ny = coef.shape[0], coef.shape[1]
    fields = ((ef, hf), (ea, ha))
    tops[...] = jnp.zeros_like(tops)
    ends[...] = jnp.zeros_like(ends)
    mirror[...] = jnp.zeros_like(mirror)
    for c in range(3):
        mirror[c, pl.ds(TOP, ny), :] = theirs[pl.ds(c * 32, ny), :]
    mirror[3, pl.ds(TOP, ny), :] = mirror_coef[...]
    odd = is_odd("gy")

    def came(at, lanes):
        high, low = ordered(odd, y_far[pl.ds(at, 2), pl.ds(0, lanes)], y_near[pl.ds(at, 2), pl.ds(0, lanes)])
        return low, high

    for i in range(13 * nx):
        low, high = came(2 * i, y_far.shape[1])
        tops[i, pl.ds(TOP - 2, 2), :] = low
        ends[i, pl.ds(0, 2), :] = high
    for c in range(4):
        low, high = came(26 * nx + 2 * c, LANES)
        mirror[c, pl.ds(TOP - 2, 2), :] = low
        mirror[c, pl.ds(END, 2), :] = high

    def part(f, k, c, x):
        return framed(fields[f][k][c, x], tops, ends, plane_index(f, k, c, x, nx))

    ks = [framed(coef[x], tops, ends, 12 * nx + x) for x in range(nx)]
    up, down = edge_planes(part, ks, nx, lambda v, x: jnp.where(ks[x] > 0, v, 0.0))
    m = [mirror[c] for c in range(3)]
    km = mirror[3]
    lane = lane_of(km.shape)
    first = lane % 64 < 32
    up_m = [jnp.where(first, m[0], turn(m[1], 32)), jnp.where(first, m[2], turn(km, 32))]
    down_m = [jnp.where(first, turn(m[1], -32), m[0]), jnp.where(first, turn(km, -32), m[2])]
    for out, planes, wanted, window, base in ((x_up, up, ROWS_UP, up_m, 96),
                                              (x_down, down, ROWS_DOWN, down_m, 64)):
        at = 0
        for plane, rows in zip(planes, wanted):
            for row in rows:
                out[pl.ds(at, 1), :] = plane[row:row + 1]
                at += 1
        side = window[1]
        for i, plane in enumerate(LATER):
            plane = planes[plane]
            near = jnp.where(lane >= LANES // 2, plane[:, :LANES], plane[:, LANES:])
            part_in = turn(near, SHIFT + base + SLIM * i - 1)
            inside = (lane >= base + SLIM * i) & (lane < base + SLIM * (i + 1))
            side = jnp.where(inside, part_in, side)
        value = jnp.concatenate([window[0], side], 1)
        out[pl.ds(FIXED, 2), :] = value[TOP - 2:TOP]
        out[pl.ds(FIXED + 2, 2), :] = value[END:END + 2]
        out[pl.ds(FIXED + 4, ny), :] = value[TOP:END]
    x_far[...], x_near[...] = ordered(is_odd("gx"), x_up[...], x_down[...])


def slab_gradient(message, first, second, ny):
    total = None
    for c in range(3):
        mon = message[pl.ds(ROW_MON + 32 * (c // 2), ny), :]
        real = turn(mon, -64 * (c % 2))
        imag = turn(real, -4)
        real = real + math.cos(OMEGA) * first[c] + math.cos(2 * OMEGA) * second[c]
        imag = imag - math.sin(OMEGA) * first[c] - math.sin(2 * OMEGA) * second[c]
        term = real * turn(real, -8) - imag * turn(imag, -8)
        total = term if total is None else total + term
    return total


def slab_rows(packed, out, square, nx):
    square[...] = flipped(packed, square)
    for p in range(PLANES):
        for x in range(nx):
            out[pl.ds(p * nx + x, 1), :] = square[pl.ds(x * 16 + 2 + p, 1), :]


def step_kernel(ef_in, hf_in, ea_in, ha_in, coef, tops, ends, mirror, bulk_far_1, bulk_near_1, bulk_far_2, bulk_near_2,
                x_far, x_near, mine, theirs,
                ef_out, hf_out, ea_out, ha_out, grad,
                ee, hh, halo, square, table, lines, sems):
    nx, ny, nz = coef.shape

    fields = ((ef_in, hf_in), (ea_in, ha_in))
    lane = lane_of((ny, LANES))
    odd = is_odd("gx")
    for slot, base in ((0, 96), (10, 64)):
        def source_at(row, rows, slot=slot):
            pair = (x_near, x_far) if slot == 0 else (x_far, x_near)
            return jnp.where(odd, pair[0][pl.ds(row, rows), :], pair[1][pl.ds(row, rows), :])

        def bulk_at(row, rows, slot=slot):
            far = bulk_far_1[pl.ds(row, rows), :] + bulk_far_2[pl.ds(row, rows), :]
            near = bulk_near_1[pl.ds(row, rows), :] + bulk_near_2[pl.ds(row, rows), :]
            return jnp.where(odd, near, far) if slot == 0 else jnp.where(odd, far, near)

        halo[slot + 9, pl.ds(0, TOP), :] = jnp.zeros((TOP, nz), F32)
        halo[slot + 9, pl.ds(END, TOP), :] = jnp.zeros((TOP, nz), F32)
        window = source_at(FIXED + 4, ny)
        halo[slot + 9, pl.ds(TOP, ny), :] = window
        halo[slot + 9, pl.ds(TOP - 2, 2), :] = source_at(FIXED, 2)
        halo[slot + 9, pl.ds(END, 2), :] = source_at(FIXED + 2, 2)
        side = window[:, LANES:]
        row_at = 0
        for plane, rows in enumerate(ROWS_DOWN if slot else ROWS_UP):
            at = slot + plane
            halo[at, pl.ds(0, TOP), :] = jnp.zeros((TOP, nz), F32)
            halo[at, pl.ds(END, TOP), :] = jnp.zeros((TOP, nz), F32)
            value = bulk_at(plane * ny, ny)
            if plane in LATER:
                near = turn(side, 1 - SHIFT - base - SLIM * LATER.index(plane))
                value = jnp.concatenate(
                    [jnp.where(lane >= Z0 - 1, near, value[:, :LANES]),
                     jnp.where(lane < Z0 + PLANES + 1 - LANES, near, value[:, LANES:])], 1)
            halo[at, pl.ds(TOP, ny), :] = value
            for row in rows:
                halo[at, pl.ds(row, 1), :] = source_at(row_at, 1)
                row_at += 1
    k_low, k_high = halo[8], halo[18]

    def part(f, k, c, x):
        return framed(fields[f][k][c, x], tops, ends, plane_index(f, k, c, x, nx))

    def inverse(x):
        return framed(coef[x], tops, ends, 12 * nx + x)

    copies = []
    first_slab, second_slab = [], []
    for f in range(2):
        ey0, ez0 = part(f, 0, 1, 0), part(f, 0, 2, 0)
        dhy = jnp.where(k_low > 0, COURANT * ez0, 0.0)
        dhz = jnp.where(k_low > 0, -COURANT * ey0, 0.0)
        hh[f, 1, 0] = halo[4 * f] + dhy
        hh[f, 2, 0] = halo[4 * f + 1] + dhz
        for x in range(nx):
            inside = inverse(x) > 0
            ex, ey, ez = part(f, 0, 0, x), part(f, 0, 1, x), part(f, 0, 2, x)
            ey_n = part(f, 0, 1, x + 1) if x + 1 < nx else halo[10 + 4 * f]
            ez_n = part(f, 0, 2, x + 1) if x + 1 < nx else halo[10 + 4 * f + 1]
            hx, hy, hz = part(f, 1, 0, x), part(f, 1, 1, x), part(f, 1, 2, x)
            hh[f, 0, x + 1] = jnp.where(inside, hx - COURANT * ((up_y(ez) - ez) - (up_z(ey) - ey)), 0.0)
            hh[f, 1, x + 1] = jnp.where(inside, hy - COURANT * ((up_z(ex) - ex) - (ez_n - ez)), 0.0)
            hh[f, 2, x + 1] = jnp.where(inside, hz - COURANT * ((ey_n - ey) - (up_y(ex) - ex)), 0.0)
        for x in range(nx):
            k = inverse(x)
            hx, hy, hz = hh[f, 0, x + 1], hh[f, 1, x + 1], hh[f, 2, x + 1]
            ee[f, 0, x] = part(f, 0, 0, x) + k * ((hz - down_y(hz)) - (hy - down_z(hy)))
            ee[f, 1, x] = part(f, 0, 1, x) + k * ((hx - down_z(hx)) - (hz - hh[f, 2, x]))
            ee[f, 2, x] = part(f, 0, 2, x) + k * ((hy - hh[f, 1, x]) - (hx - down_y(hx)))
        ee[f, 1, nx] = halo[10 + 4 * f + 2] + k_high * hh[f, 2, nx]
        ee[f, 2, nx] = halo[10 + 4 * f + 3] - k_high * hh[f, 1, nx]
        dex = k_low * ((dhz - down_y(dhz)) - (dhy - down_z(dhy)))
        dey = -k_low * dhz
        dez = k_low * dhy
        hh[f, 1, 0] = jnp.where(
            k_low > 0, halo[4 * f + 2] + dhy - COURANT * ((up_z(dex) - dex) - (ee[f, 2, 0] - dez)), 0.0)
        hh[f, 2, 0] = jnp.where(
            k_low > 0, halo[4 * f + 3] + dhz - COURANT * ((ee[f, 1, 0] - dey) - (up_y(dex) - dex)), 0.0)
        for x in range(nx):
            inside = inverse(x) > 0
            ex, ey, ez = ee[f, 0, x], ee[f, 1, x], ee[f, 2, x]
            hh[f, 0, x + 1] = jnp.where(
                inside, hh[f, 0, x + 1] - COURANT * ((up_y(ez) - ez) - (up_z(ey) - ey)), 0.0)
            hh[f, 1, x + 1] = jnp.where(
                inside, hh[f, 1, x + 1] - COURANT * ((up_z(ex) - ex) - (ee[f, 2, x + 1] - ez)), 0.0)
            hh[f, 2, x + 1] = jnp.where(
                inside, hh[f, 2, x + 1] - COURANT * ((ee[f, 1, x + 1] - ey) - (up_y(ex) - ex)), 0.0)
        copies.append(pltpu.make_async_copy(
            hh.at[f, :, pl.ds(1, nx), pl.ds(TOP, ny), :], (hf_out, ha_out)[f], sems.at[2 * f]))
        copies[-1].start()
    for c in range(3):
        first_slab.append(pack_planes([(x * 16 + f * 8, ee[f, c, x, pl.ds(TOP, ny), :])
                                       for x in range(nx) for f in range(2)]))
    for f in range(2):
        for x in range(nx):
            k = inverse(x)
            hx, hy, hz = hh[f, 0, x + 1], hh[f, 1, x + 1], hh[f, 2, x + 1]
            ee[f, 0, x] = ee[f, 0, x] + k * ((hz - down_y(hz)) - (hy - down_z(hy)))
            ee[f, 1, x] = ee[f, 1, x] + k * ((hx - down_z(hx)) - (hz - hh[f, 2, x]))
            ee[f, 2, x] = ee[f, 2, x] + k * ((hy - hh[f, 1, x]) - (hx - down_y(hx)))
        copies.append(pltpu.make_async_copy(
            ee.at[f, :, pl.ds(0, nx), pl.ds(TOP, ny), :], (ef_out, ea_out)[f], sems.at[2 * f + 1]))
        copies[-1].start()
    for c in range(3):
        second_slab.append(pack_planes([(x * 16 + f * 8, ee[f, c, x, pl.ds(TOP, ny), :])
                                        for x in range(nx) for f in range(2)]))
    own = slab_gradient(mine, first_slab, second_slab, ny)

    low01, low2 = halo[9, :, pl.ds(0, LANES)], halo[9, :, pl.ds(LANES, LANES)]
    high01, high2 = halo[19, :, pl.ds(0, LANES)], halo[19, :, pl.ds(LANES, LANES)]
    lane = lane_of(low01.shape)

    def join(below, middle, above):
        return jnp.where(lane < 32, below, jnp.where(lane < 96, middle, above))

    m = [mirror[c] for c in range(3)]
    e = [join(turn(high01, -32), turn(m[0], 32), turn(low01, 96)),
         join(high01, turn(m[1], 32), turn(low01, 64)),
         join(turn(high2, -32), turn(m[2], 32), turn(low2, 96))]
    h = [join(turn(high01, -96), turn(m[0], -32), turn(low01, 32)),
         join(turn(high01, -64), turn(m[1], -32), low01),
         join(turn(high2, -96), turn(m[2], -32), turn(low2, 32))]
    k = join(high2, turn(mirror[3], 32), turn(low2, 64))
    inside = k > 0

    def ahead(a, axis):
        return (turn(a, -16), up_y(a), turn(a, -1))[axis] - a

    def behind(a, axis):
        return a - (turn(a, 16), down_y(a), turn(a, 1))[axis]

    slabs = []
    for _ in range(2):
        h = [jnp.where(inside, h[c] - COURANT * (ahead(e[(c + 2) % 3], (c + 1) % 3)
                                                 - ahead(e[(c + 1) % 3], (c + 2) % 3)), 0.0)
             for c in range(3)]
        e = [e[c] + k * (behind(h[(c + 2) % 3], (c + 1) % 3) - behind(h[(c + 1) % 3], (c + 2) % 3))
             for c in range(3)]
        slabs.append([turn(e[c], -32)[TOP:END] for c in range(3)])
    other = slab_gradient(theirs, slabs[0], slabs[1], ny)

    weight, _, partner = small_parts(mine)
    weight_m, _, _ = small_parts(theirs)
    slab_rows(other, table, square, nx)
    table[...] = table[...] * weight_m
    got = mirror_take(table, partner, ny)
    slab_rows(own, lines, square, nx)
    lines[...] = 0.5 * (lines[...] * weight + got)
    for p in range(PLANES):
        grad[p] = lines[pl.ds(p * nx, nx), pl.ds(0, ny)]
    for copy in copies:
        copy.wait()


def call(kernel, outs, args, scratch=(), name=None, any_in=False, any_out=0, work=4_000_000):
    spaces = lambda count, far: [pl.BlockSpec(memory_space=pltpu.HBM if i < far else pltpu.VMEM)
                                 for i in range(count)]
    return pl.pallas_call(
        kernel,
        out_shape=outs,
        in_specs=[pl.BlockSpec(memory_space=pltpu.HBM if any_in else pltpu.VMEM)] * len(args),
        out_specs=spaces(len(outs), any_out),
        scratch_shapes=list(scratch),
        compiler_params=pltpu.CompilerParams(vmem_limit_bytes=FAR_LIMIT if any_in else VMEM_LIMIT),
        cost_estimate=pl.CostEstimate(flops=work, bytes_accessed=4_000_000, transcendentals=0),
        name=name,
    )(*args)


def swapped(far, near, axis, start=0, stop=None):
    size = lax.axis_size(axis)

    def pairs(first):
        lows = [i for i in range(first, size - 1, 2) if start <= i < (size if stop is None else stop)]
        return [(i, i + 1) for i in lows] + [(i + 1, i) for i in lows]

    return lax.ppermute(far, axis, pairs(1)), lax.ppermute(near, axis, pairs(0))


def mirrored(block, axis):
    size = lax.axis_size(axis)
    return lax.ppermute(block, axis, [(i, size - 1 - i) for i in range(size)])


def per_device(e_fwd, h_fwd, e_adj, h_adj, eps_back, density, design_mask, partner_map, mon_fwd, mon_adj):
    _, nx, ny, nz = e_fwd.shape
    shape = lambda *dims: jax.ShapeDtypeStruct(dims, F32)
    vmem = lambda *dims: pltpu.VMEM(dims, F32)
    square = vmem(LANES, LANES)
    lines = vmem(PLANES * nx, LANES)
    block = shape(nx, ny, nz)
    fields = [e_fwd, h_fwd, e_adj, h_adj]

    bulk_shape = shape(9 * ny, nz)
    mine, = call(
        message_kernel, [shape(MESSAGE, LANES)],
        fields + [eps_back, density, design_mask, partner_map, mon_fwd, mon_adj],
        [vmem(2, 2, 3, nx, ny, nz), vmem(nx, ny, nz), vmem(*density.shape),
         pltpu.VMEM((2,) + density.shape, jnp.int32), vmem(2, *mon_fwd.shape),
         square, pltpu.SemaphoreType.DMA((10,))], name="message", any_in=True)
    theirs = mirrored(mine, "gx")
    bulk = call(bulk_kernel, [bulk_shape, bulk_shape], [*fields, eps_back, mine], name="bulk")
    early = lax.axis_size("gx") // 4
    bulk_lower = swapped(*bulk, "gx", stop=early)
    bulk_upper = swapped(*bulk, "gx", start=early)
    y_shape = shape(2 * (13 * nx) + 8, nz)
    coef, mirror_coef, y_far, y_near = call(
        coef_kernel, [block, shape(ny, LANES), y_shape, y_shape], [*bulk_lower, eps_back, mine, theirs] + fields,
        [lines, lines, square], name="coefficient")
    y_far, y_near = swapped(y_far, y_near, "gy")
    x_shape = shape(FIXED + 4 + ny, nz)
    tile = shape(13 * nx, 8, nz)
    tops, ends, mirror, x_far, x_near = call(
        edges_kernel, [tile, tile, shape(4, FRAME, LANES), x_shape, x_shape],
        fields + [coef, mirror_coef, theirs, y_far, y_near],
        [vmem(*x_shape.shape)] * 2, name="edges", work=1_000_000_000)
    x_far, x_near = swapped(x_far, x_near, "gx")
    ef, hf, ea, ha, grad = call(
        step_kernel, [shape(*e_fwd.shape)] * 4 + [shape(*density.shape)],
        fields + [coef, tops, ends, mirror, *bulk_lower, *bulk_upper, x_far, x_near, mine, theirs],
        [vmem(2, 3, nx + 1, FRAME, nz), vmem(2, 3, nx + 1, FRAME, nz), vmem(20, FRAME, nz),
         square, lines, lines, pltpu.SemaphoreType.DMA((4,))], name="steps", any_out=4)
    return ef, hf, ea, ha, grad


def solution(mesh):
    grid = P(None, "gx", "gy", None)
    slab = P(None, "gx", "gy")
    monitor = P(None, None, None, "gx", "gy")
    return jax.shard_map(
        per_device,
        mesh=mesh,
        in_specs=(grid, grid, grid, grid, P("gx", "gy", None), slab, slab, slab, monitor, monitor),
        out_specs=(grid, grid, grid, grid, slab),
        check_vma=False,
    )
```

```python
import math

import jax
import jax.numpy as jnp
from jax import lax
from jax.experimental import pallas as pl
from jax.experimental.pallas import tpu as pltpu
from jax.sharding import PartitionSpec as P

PLANES = 4
Z0 = 126
COURANT = 0.5
OMEGA = 0.7
CONTRAST = 10.0
F32 = jnp.float32
VMEM_LIMIT = 32 * 1024 * 1024
FAR_LIMIT = 60 * 1024 * 1024

LANES = 128
FRAME = 48
TOP, END = 8, 40
WINDOW = 8
SHIFT = LANES - (Z0 - 2)
ROW_EPS, ROW_MON, MESSAGE = 96, 128, 192


def lane_of(shape):
    return lax.broadcasted_iota(jnp.int32, shape, len(shape) - 1)


def row_of(shape):
    return lax.broadcasted_iota(jnp.int32, shape, len(shape) - 2)


def turn(a, shift):
    shift = shift % a.shape[1]
    return pltpu.roll(a, shift, 1) if shift else a


def up_y(a):
    return pltpu.roll(a, a.shape[0] - 1, 0)


def down_y(a):
    return pltpu.roll(a, 1, 0)


def up_z(a):
    n = a.shape[1]
    return jnp.where(lane_of(a.shape) == n - 1, 0.0, pltpu.roll(a, n - 1, 1))


def down_z(a):
    return jnp.where(lane_of(a.shape) == 0, 0.0, pltpu.roll(a, 1, 1))


def is_odd(axis):
    return lax.axis_index(axis) % 2 == 1


def ordered(odd, up, down):
    return jnp.where(odd, up, down), jnp.where(odd, down, up)


def pack_planes(planes):
    total = None
    for offset, plane in planes:
        near = jnp.where(lane_of((plane.shape[0], LANES)) >= LANES // 2,
                         plane[:, :LANES], plane[:, LANES:2 * LANES])
        part = turn(near, SHIFT + offset)
        lane = lane_of(part.shape)
        inside = (lane >= offset) & (lane < offset + WINDOW)
        total = jnp.where(inside, part, 0.0 if total is None else total)
    return total


def flipped(a, square):
    square[...] = jnp.zeros_like(square)
    square[pl.ds(0, a.shape[0]), pl.ds(0, a.shape[1])] = a
    return jnp.transpose(square[...])


def edge_planes(part, ks, nx, mark):
    up, down = [], []
    last = nx - 1
    for f in range(2):
        e = lambda c, x: part(f, 0, c, x)
        h = lambda c, x: part(f, 1, c, x)
        k = ks[last]
        ex, ey, ez = e(0, last), e(1, last), e(2, last)
        ex_b, ey_b, ez_b = e(0, last - 1), e(1, last - 1), e(2, last - 1)
        hy_b = mark(h(1, last - 1) - COURANT * ((up_z(ex_b) - ex_b) - (ez - ez_b)), last - 1)
        hz_b = mark(h(2, last - 1) - COURANT * ((ey - ey_b) - (up_y(ex_b) - ex_b)), last - 1)
        hx = mark(h(0, last) - COURANT * ((up_y(ez) - ez) - (up_z(ey) - ey)), last)
        hy = mark(h(1, last) - COURANT * ((up_z(ex) - ex) + ez), last)
        hz = mark(h(2, last) - COURANT * (-ey - (up_y(ex) - ex)), last)
        ex = ex + k * ((hz - down_y(hz)) - (hy - down_z(hy)))
        ey = ey + k * ((hx - down_z(hx)) - (hz - hz_b))
        ez = ez + k * ((hy - hy_b) - (hx - down_y(hx)))
        up += [hy, hz, mark(hy - COURANT * ((up_z(ex) - ex) + ez), last),
               mark(hz - COURANT * (-ey - (up_y(ex) - ex)), last)]
        k = ks[0]
        ex, ey, ez = e(0, 0), e(1, 0), e(2, 0)
        hx = mark(h(0, 0) - COURANT * ((up_y(ez) - ez) - (up_z(ey) - ey)), 0)
        hy = mark(h(1, 0) - COURANT * ((up_z(ex) - ex) - (e(2, 1) - ez)), 0)
        hz = mark(h(2, 0) - COURANT * ((e(1, 1) - ey) - (up_y(ex) - ex)), 0)
        down += [ey, ez, ey + k * ((hx - down_z(hx)) - hz), ez + k * (hy - (hx - down_y(hx)))]
    return up + [ks[last]], down + [ks[0]]


def write_bulk(part, eps, x_far, x_near):
    nx, ny = eps.shape[0], eps.shape[1]
    ks = [COURANT / eps[x] if x in (0, nx - 1) else None for x in range(nx)]
    odd = is_odd("gx")
    for i, planes in enumerate(zip(*edge_planes(part, ks, nx, lambda v, x: v))):
        far, near = ordered(odd, *planes)
        x_far[pl.ds(i * ny, ny), :] = far
        x_near[pl.ds(i * ny, ny), :] = near


def message_kernel(ef, hf, ea, ha, eps, density, mask, partner, mon_f, mon_a,
                   message, fields, eps_in, small_f, small_i, mons, square, sems):
    nx, ny = ef.shape[1], ef.shape[2]
    copies = []
    for f, (e, h) in enumerate(((ef, hf), (ea, ha))):
        for k, source in enumerate((e, h)):
            copies.append(pltpu.make_async_copy(source, fields.at[f, k], sems.at[2 * f + k]))
    copies.append(pltpu.make_async_copy(eps, eps_in, sems.at[4]))
    copies.append(pltpu.make_async_copy(density, small_f, sems.at[5]))
    copies.append(pltpu.make_async_copy(mask, small_i.at[0], sems.at[6]))
    copies.append(pltpu.make_async_copy(partner, small_i.at[1], sems.at[7]))
    copies.append(pltpu.make_async_copy(mon_f, mons.at[0], sems.at[8]))
    copies.append(pltpu.make_async_copy(mon_a, mons.at[1], sems.at[9]))
    for copy in copies:
        copy.start()
    message[pl.ds(ROW_EPS, MESSAGE - ROW_EPS), :] = jnp.zeros((MESSAGE - ROW_EPS, LANES), F32)
    for copy in copies[4:]:
        copy.wait()
    for half, components in ((0, (0, 1)), (1, (2,))):
        square[...] = jnp.zeros_like(square)
        for k, c in enumerate(components):
            for f in range(2):
                for x in range(nx):
                    base = k * 64 + x * 16 + f * 8 + 2
                    square[pl.ds(base, PLANES), pl.ds(0, ny)] = mons[f, 0, c, :, x, :]
                    for p in range(PLANES):
                        at = (base + 4 + p) % LANES
                        square[pl.ds(at, 1), pl.ds(0, ny)] = mons[f, 1, c, p, pl.ds(x, 1), :]
        message[pl.ds(ROW_MON + 32 * half, ny), :] = jnp.transpose(square[...])[:ny]
    own_eps = [(x * 16 + f * 8, eps_in[x]) for x in range(nx) for f in range(2)]
    square[...] = jnp.zeros_like(square)
    for p in range(PLANES):
        square[pl.ds(p * nx, nx), pl.ds(0, ny)] = CONTRAST * small_i[0, p].astype(F32)
        square[pl.ds(16 + p * nx, nx), pl.ds(0, ny)] = small_f[p]
        square[pl.ds(32 + p * nx, nx), pl.ds(0, ny)] = small_i[1, p].astype(F32)
    small = turn(square[pl.ds(0, 32), :], 64)
    index = turn(square[pl.ds(32, 32), :], 96)
    message[pl.ds(ROW_EPS, ny), :] = pack_planes(own_eps) + small + index
    for copy in copies[:4]:
        copy.wait()
    for c in range(3):
        message[pl.ds(c * 32, ny), :] = pack_planes(
            [(k * 64 + x * 16 + f * 8, fields[f, k, c, x])
             for k in range(2) for x in range(nx) for f in range(2)])


def bulk_kernel(ef, hf, ea, ha, eps, message, x_far, x_near):
    del message
    fields = ((ef, hf), (ea, ha))
    write_bulk(lambda f, k, c, x: fields[f][k][c, x], eps, x_far, x_near)


def small_parts(message):
    weight = turn(message[pl.ds(ROW_EPS, 16), :], -64)
    density = turn(message[pl.ds(ROW_EPS + 16, 16), :], -64)
    partner = turn(message[pl.ds(ROW_EPS, 16), :], -96)
    return weight, density, partner


def mirror_take(table, partner, ny):
    inside = lane_of(partner.shape) < ny
    at = jnp.where(inside, partner, 0.0).astype(jnp.int32)
    row, lane = at // ny, at % ny
    got = jnp.zeros(at.shape, F32)
    for r in range(table.shape[0]):
        line = jnp.broadcast_to(table[pl.ds(r, 1), :], at.shape)
        got = jnp.where(row == r, jnp.take_along_axis(line, lane, axis=1), got)
    return got


def spread_slab(values, lines, square, nx, ny):
    lines[...] = values
    square[...] = jnp.zeros_like(square)
    for p in range(PLANES):
        for x in range(nx):
            row = lines[pl.ds(p * nx + x, 1), :]
            square[pl.ds(x * 16 + 2 + p, 1), :] = row
            square[pl.ds(x * 16 + 10 + p, 1), :] = row
    return jnp.transpose(square[...])[:ny]


def coef_kernel(bulk_far, bulk_near, eps, mine, theirs, ef, hf, ea, ha, coef, mirror_coef, y_far, y_near, table, lines, square):
    del bulk_far, bulk_near
    nx = eps.shape[0]
    ny = END - TOP
    weight, density, partner = small_parts(mine)
    weight_m, density_m, partner_m = small_parts(theirs)
    table[...] = density_m
    extra = weight * (0.5 * (density + mirror_take(table, partner, ny)))
    table[...] = density
    extra_m = weight_m * (0.5 * (density_m + mirror_take(table, partner_m, ny)))
    packed = spread_slab(extra, lines, square, nx, ny)
    lane = lane_of(packed.shape)
    for x in range(nx):
        part = turn(packed, -16 * x - SHIFT)
        low = jnp.where(lane >= Z0, part, 0.0)
        high = jnp.where(lane < Z0 + PLANES - LANES, part, 0.0)
        coef[x] = COURANT / (eps[x] + jnp.concatenate([low, high], 1))
    packed = theirs[pl.ds(ROW_EPS, ny), :] + spread_slab(extra_m, lines, square, nx, ny)
    mirror_coef[...] = jnp.where(lane < 64, COURANT / jnp.where(lane < 64, packed, 1.0), 0.0)
    odd = is_odd("gy")

    def put(at, ref, lanes):
        far, near = ordered(odd, ref[pl.ds(ny - 2, 2), :], ref[pl.ds(0, 2), :])
        y_far[pl.ds(at, 2), pl.ds(0, lanes)] = far
        y_near[pl.ds(at, 2), pl.ds(0, lanes)] = near

    for f, pair in enumerate(((ef, hf), (ea, ha))):
        for k, field in enumerate(pair):
            for c in range(3):
                for x in range(nx):
                    put(2 * plane_index(f, k, c, x, nx), field.at[c, x], y_far.shape[1])
    for x in range(nx):
        put(24 * nx + 2 * x, coef.at[x], y_far.shape[1])
    rest = jnp.zeros((8, y_far.shape[1]), F32)
    y_far[pl.ds(26 * nx, 8), :] = rest
    y_near[pl.ds(26 * nx, 8), :] = rest
    for c in range(3):
        put(26 * nx + 2 * c, theirs.at[pl.ds(c * 32, ny), :], LANES)
    put(26 * nx + 6, mirror_coef, LANES)


def plane_index(f, k, c, x, nx):
    return ((f * 2 + k) * 3 + c) * nx + x


def framed(middle, tops, ends, i):
    return jnp.concatenate([tops[i], middle, ends[i]], 0)


ROWS_UP = ((7, 40), (7, 39), (8, 39), (8, 38, 39)) * 2 + ((7, 40),)
ROWS_DOWN = ((6, 7, 40), (7, 40), (7, 39), (8, 39)) * 2 + ((7, 40),)
FIXED = 20
LATER = (2, 3, 6, 7, 8)
SLIM = 6


def edges_kernel(ef, hf, ea, ha, coef, mirror_coef, theirs, y_far, y_near,
                 tops, ends, mirror, x_far, x_near, x_up, x_down):
    nx, ny = coef.shape[0], coef.shape[1]
    fields = ((ef, hf), (ea, ha))
    tops[...] = jnp.zeros_like(tops)
    ends[...] = jnp.zeros_like(ends)
    mirror[...] = jnp.zeros_like(mirror)
    for c in range(3):
        mirror[c, pl.ds(TOP, ny), :] = theirs[pl.ds(c * 32, ny), :]
    mirror[3, pl.ds(TOP, ny), :] = mirror_coef[...]
    odd = is_odd("gy")

    def came(at, lanes):
        high, low = ordered(odd, y_far[pl.ds(at, 2), pl.ds(0, lanes)], y_near[pl.ds(at, 2), pl.ds(0, lanes)])
        return low, high

    for i in range(13 * nx):
        low, high = came(2 * i, y_far.shape[1])
        tops[i, pl.ds(TOP - 2, 2), :] = low
        ends[i, pl.ds(0, 2), :] = high
    for c in range(4):
        low, high = came(26 * nx + 2 * c, LANES)
        mirror[c, pl.ds(TOP - 2, 2), :] = low
        mirror[c, pl.ds(END, 2), :] = high

    def part(f, k, c, x):
        return framed(fields[f][k][c, x], tops, ends, plane_index(f, k, c, x, nx))

    ks = [framed(coef[x], tops, ends, 12 * nx + x) for x in range(nx)]
    up, down = edge_planes(part, ks, nx, lambda v, x: jnp.where(ks[x] > 0, v, 0.0))
    m = [mirror[c] for c in range(3)]
    km = mirror[3]
    lane = lane_of(km.shape)
    first = lane % 64 < 32
    up_m = [jnp.where(first, m[0], turn(m[1], 32)), jnp.where(first, m[2], turn(km, 32))]
    down_m = [jnp.where(first, turn(m[1], -32), m[0]), jnp.where(first, turn(km, -32), m[2])]
    for out, planes, wanted, window, base in ((x_up, up, ROWS_UP, up_m, 96),
                                              (x_down, down, ROWS_DOWN, down_m, 64)):
        at = 0
        for plane, rows in zip(planes, wanted):
            for row in rows:
                out[pl.ds(at, 1), :] = plane[row:row + 1]
                at += 1
        side = window[1]
        for i, plane in enumerate(LATER):
            plane = planes[plane]
            near = jnp.where(lane >= LANES // 2, plane[:, :LANES], plane[:, LANES:])
            part_in = turn(near, SHIFT + base + SLIM * i - 1)
            inside = (lane >= base + SLIM * i) & (lane < base + SLIM * (i + 1))
            side = jnp.where(inside, part_in, side)
        value = jnp.concatenate([window[0], side], 1)
        out[pl.ds(FIXED, 2), :] = value[TOP - 2:TOP]
        out[pl.ds(FIXED + 2, 2), :] = value[END:END + 2]
        out[pl.ds(FIXED + 4, ny), :] = value[TOP:END]
    x_far[...], x_near[...] = ordered(is_odd("gx"), x_up[...], x_down[...])


def slab_gradient(message, first, second, ny):
    total = None
    for c in range(3):
        mon = message[pl.ds(ROW_MON + 32 * (c // 2), ny), :]
        real = turn(mon, -64 * (c % 2))
        imag = turn(real, -4)
        real = real + math.cos(OMEGA) * first[c] + math.cos(2 * OMEGA) * second[c]
        imag = imag - math.sin(OMEGA) * first[c] - math.sin(2 * OMEGA) * second[c]
        term = real * turn(real, -8) - imag * turn(imag, -8)
        total = term if total is None else total + term
    return total


def slab_rows(packed, out, square, nx):
    square[...] = flipped(packed, square)
    for p in range(PLANES):
        for x in range(nx):
            out[pl.ds(p * nx + x, 1), :] = square[pl.ds(x * 16 + 2 + p, 1), :]


def step_kernel(ef_in, hf_in, ea_in, ha_in, coef, tops, ends, mirror, bulk_far_1, bulk_near_1, bulk_far_2, bulk_near_2,
                x_far, x_near, mine, theirs,
                ef_out, hf_out, ea_out, ha_out, grad,
                ee, hh, halo, square, table, lines, sems):
    nx, ny, nz = coef.shape

    fields = ((ef_in, hf_in), (ea_in, ha_in))
    lane = lane_of((ny, LANES))
    odd = is_odd("gx")
    for slot, base in ((0, 96), (10, 64)):
        def source_at(row, rows, slot=slot):
            pair = (x_near, x_far) if slot == 0 else (x_far, x_near)
            return jnp.where(odd, pair[0][pl.ds(row, rows), :], pair[1][pl.ds(row, rows), :])

        def bulk_at(row, rows, slot=slot):
            far = bulk_far_1[pl.ds(row, rows), :] + bulk_far_2[pl.ds(row, rows), :]
            near = bulk_near_1[pl.ds(row, rows), :] + bulk_near_2[pl.ds(row, rows), :]
            return jnp.where(odd, near, far) if slot == 0 else jnp.where(odd, far, near)

        halo[slot + 9, pl.ds(0, TOP), :] = jnp.zeros((TOP, nz), F32)
        halo[slot + 9, pl.ds(END, TOP), :] = jnp.zeros((TOP, nz), F32)
        window = source_at(FIXED + 4, ny)
        halo[slot + 9, pl.ds(TOP, ny), :] = window
        halo[slot + 9, pl.ds(TOP - 2, 2), :] = source_at(FIXED, 2)
        halo[slot + 9, pl.ds(END, 2), :] = source_at(FIXED + 2, 2)
        side = window[:, LANES:]
        row_at = 0
        for plane, rows in enumerate(ROWS_DOWN if slot else ROWS_UP):
            at = slot + plane
            halo[at, pl.ds(0, TOP), :] = jnp.zeros((TOP, nz), F32)
            halo[at, pl.ds(END, TOP), :] = jnp.zeros((TOP, nz), F32)
            value = bulk_at(plane * ny, ny)
            if plane in LATER:
                near = turn(side, 1 - SHIFT - base - SLIM * LATER.index(plane))
                value = jnp.concatenate(
                    [jnp.where(lane >= Z0 - 1, near, value[:, :LANES]),
                     jnp.where(lane < Z0 + PLANES + 1 - LANES, near, value[:, LANES:])], 1)
            halo[at, pl.ds(TOP, ny), :] = value
            for row in rows:
                halo[at, pl.ds(row, 1), :] = source_at(row_at, 1)
                row_at += 1
    k_low, k_high = halo[8], halo[18]

    def part(f, k, c, x):
        return framed(fields[f][k][c, x], tops, ends, plane_index(f, k, c, x, nx))

    def inverse(x):
        return framed(coef[x], tops, ends, 12 * nx + x)

    copies = []
    first_slab, second_slab = [], []
    for f in range(2):
        ey0, ez0 = part(f, 0, 1, 0), part(f, 0, 2, 0)
        dhy = jnp.where(k_low > 0, COURANT * ez0, 0.0)
        dhz = jnp.where(k_low > 0, -COURANT * ey0, 0.0)
        hh[f, 1, 0] = halo[4 * f] + dhy
        hh[f, 2, 0] = halo[4 * f + 1] + dhz
        for x in range(nx):
            inside = inverse(x) > 0
            ex, ey, ez = part(f, 0, 0, x), part(f, 0, 1, x), part(f, 0, 2, x)
            ey_n = part(f, 0, 1, x + 1) if x + 1 < nx else halo[10 + 4 * f]
            ez_n = part(f, 0, 2, x + 1) if x + 1 < nx else halo[10 + 4 * f + 1]
            hx, hy, hz = part(f, 1, 0, x), part(f, 1, 1, x), part(f, 1, 2, x)
            hh[f, 0, x + 1] = jnp.where(inside, hx - COURANT * ((up_y(ez) - ez) - (up_z(ey) - ey)), 0.0)
            hh[f, 1, x + 1] = jnp.where(inside, hy - COURANT * ((up_z(ex) - ex) - (ez_n - ez)), 0.0)
            hh[f, 2, x + 1] = jnp.where(inside, hz - COURANT * ((ey_n - ey) - (up_y(ex) - ex)), 0.0)
        for x in range(nx):
            k = inverse(x)
            hx, hy, hz = hh[f, 0, x + 1], hh[f, 1, x + 1], hh[f, 2, x + 1]
            ee[f, 0, x] = part(f, 0, 0, x) + k * ((hz - down_y(hz)) - (hy - down_z(hy)))
            ee[f, 1, x] = part(f, 0, 1, x) + k * ((hx - down_z(hx)) - (hz - hh[f, 2, x]))
            ee[f, 2, x] = part(f, 0, 2, x) + k * ((hy - hh[f, 1, x]) - (hx - down_y(hx)))
        ee[f, 1, nx] = halo[10 + 4 * f + 2] + k_high * hh[f, 2, nx]
        ee[f, 2, nx] = halo[10 + 4 * f + 3] - k_high * hh[f, 1, nx]
        dex = k_low * ((dhz - down_y(dhz)) - (dhy - down_z(dhy)))
        dey = -k_low * dhz
        dez = k_low * dhy
        hh[f, 1, 0] = jnp.where(
            k_low > 0, halo[4 * f + 2] + dhy - COURANT * ((up_z(dex) - dex) - (ee[f, 2, 0] - dez)), 0.0)
        hh[f, 2, 0] = jnp.where(
            k_low > 0, halo[4 * f + 3] + dhz - COURANT * ((ee[f, 1, 0] - dey) - (up_y(dex) - dex)), 0.0)
        for x in range(nx):
            inside = inverse(x) > 0
            ex, ey, ez = ee[f, 0, x], ee[f, 1, x], ee[f, 2, x]
            hh[f, 0, x + 1] = jnp.where(
                inside, hh[f, 0, x + 1] - COURANT * ((up_y(ez) - ez) - (up_z(ey) - ey)), 0.0)
            hh[f, 1, x + 1] = jnp.where(
                inside, hh[f, 1, x + 1] - COURANT * ((up_z(ex) - ex) - (ee[f, 2, x + 1] - ez)), 0.0)
            hh[f, 2, x + 1] = jnp.where(
                inside, hh[f, 2, x + 1] - COURANT * ((ee[f, 1, x + 1] - ey) - (up_y(ex) - ex)), 0.0)
        copies.append(pltpu.make_async_copy(
            hh.at[f, :, pl.ds(1, nx), pl.ds(TOP, ny), :], (hf_out, ha_out)[f], sems.at[2 * f]))
        copies[-1].start()
    for c in range(3):
        first_slab.append(pack_planes([(x * 16 + f * 8, ee[f, c, x, pl.ds(TOP, ny), :])
                                       for x in range(nx) for f in range(2)]))
    for f in range(2):
        for x in range(nx):
            k = inverse(x)
            hx, hy, hz = hh[f, 0, x + 1], hh[f, 1, x + 1], hh[f, 2, x + 1]
            ee[f, 0, x] = ee[f, 0, x] + k * ((hz - down_y(hz)) - (hy - down_z(hy)))
            ee[f, 1, x] = ee[f, 1, x] + k * ((hx - down_z(hx)) - (hz - hh[f, 2, x]))
            ee[f, 2, x] = ee[f, 2, x] + k * ((hy - hh[f, 1, x]) - (hx - down_y(hx)))
        copies.append(pltpu.make_async_copy(
            ee.at[f, :, pl.ds(0, nx), pl.ds(TOP, ny), :], (ef_out, ea_out)[f], sems.at[2 * f + 1]))
        copies[-1].start()
    for c in range(3):
        second_slab.append(pack_planes([(x * 16 + f * 8, ee[f, c, x, pl.ds(TOP, ny), :])
                                        for x in range(nx) for f in range(2)]))
    own = slab_gradient(mine, first_slab, second_slab, ny)

    low01, low2 = halo[9, :, pl.ds(0, LANES)], halo[9, :, pl.ds(LANES, LANES)]
    high01, high2 = halo[19, :, pl.ds(0, LANES)], halo[19, :, pl.ds(LANES, LANES)]
    lane = lane_of(low01.shape)

    def join(below, middle, above):
        return jnp.where(lane < 32, below, jnp.where(lane < 96, middle, above))

    m = [mirror[c] for c in range(3)]
    e = [join(turn(high01, -32), turn(m[0], 32), turn(low01, 96)),
         join(high01, turn(m[1], 32), turn(low01, 64)),
         join(turn(high2, -32), turn(m[2], 32), turn(low2, 96))]
    h = [join(turn(high01, -96), turn(m[0], -32), turn(low01, 32)),
         join(turn(high01, -64), turn(m[1], -32), low01),
         join(turn(high2, -96), turn(m[2], -32), turn(low2, 32))]
    k = join(high2, turn(mirror[3], 32), turn(low2, 64))
    inside = k > 0

    def ahead(a, axis):
        return (turn(a, -16), up_y(a), turn(a, -1))[axis] - a

    def behind(a, axis):
        return a - (turn(a, 16), down_y(a), turn(a, 1))[axis]

    slabs = []
    for _ in range(2):
        h = [jnp.where(inside, h[c] - COURANT * (ahead(e[(c + 2) % 3], (c + 1) % 3)
                                                 - ahead(e[(c + 1) % 3], (c + 2) % 3)), 0.0)
             for c in range(3)]
        e = [e[c] + k * (behind(h[(c + 2) % 3], (c + 1) % 3) - behind(h[(c + 1) % 3], (c + 2) % 3))
             for c in range(3)]
        slabs.append([turn(e[c], -32)[TOP:END] for c in range(3)])
    other = slab_gradient(theirs, slabs[0], slabs[1], ny)

    weight, _, partner = small_parts(mine)
    weight_m, _, _ = small_parts(theirs)
    slab_rows(other, table, square, nx)
    table[...] = table[...] * weight_m
    got = mirror_take(table, partner, ny)
    slab_rows(own, lines, square, nx)
    lines[...] = 0.5 * (lines[...] * weight + got)
    for p in range(PLANES):
        grad[p] = lines[pl.ds(p * nx, nx), pl.ds(0, ny)]
    for copy in copies:
        copy.wait()


def call(kernel, outs, args, scratch=(), name=None, any_in=False, any_out=0, work=4_000_000):
    spaces = lambda count, far: [pl.BlockSpec(memory_space=pltpu.HBM if i < far else pltpu.VMEM)
                                 for i in range(count)]
    return pl.pallas_call(
        kernel,
        out_shape=outs,
        in_specs=[pl.BlockSpec(memory_space=pltpu.HBM if any_in else pltpu.VMEM)] * len(args),
        out_specs=spaces(len(outs), any_out),
        scratch_shapes=list(scratch),
        compiler_params=pltpu.CompilerParams(vmem_limit_bytes=FAR_LIMIT if any_in else VMEM_LIMIT),
        cost_estimate=pl.CostEstimate(flops=work, bytes_accessed=4_000_000, transcendentals=0),
        name=name,
    )(*args)


def swapped(far, near, axis, start=0, stop=None):
    size = lax.axis_size(axis)

    def pairs(first):
        lows = [i for i in range(first, size - 1, 2) if start <= i < (size if stop is None else stop)]
        return [(i, i + 1) for i in lows] + [(i + 1, i) for i in lows]

    return lax.ppermute(far, axis, pairs(1)), lax.ppermute(near, axis, pairs(0))


def mirrored(block, axis):
    size = lax.axis_size(axis)
    return lax.ppermute(block, axis, [(i, size - 1 - i) for i in range(size)])


def per_device(e_fwd, h_fwd, e_adj, h_adj, eps_back, density, design_mask, partner_map, mon_fwd, mon_adj):
    _, nx, ny, nz = e_fwd.shape
    shape = lambda *dims: jax.ShapeDtypeStruct(dims, F32)
    vmem = lambda *dims: pltpu.VMEM(dims, F32)
    square = vmem(LANES, LANES)
    lines = vmem(PLANES * nx, LANES)
    block = shape(nx, ny, nz)
    fields = [e_fwd, h_fwd, e_adj, h_adj]

    bulk_shape = shape(9 * ny, nz)
    mine, = call(
        message_kernel, [shape(MESSAGE, LANES)],
        fields + [eps_back, density, design_mask, partner_map, mon_fwd, mon_adj],
        [vmem(2, 2, 3, nx, ny, nz), vmem(nx, ny, nz), vmem(*density.shape),
         pltpu.VMEM((2,) + density.shape, jnp.int32), vmem(2, *mon_fwd.shape),
         square, pltpu.SemaphoreType.DMA((10,))], name="message", any_in=True)
    theirs = mirrored(mine, "gx")
    bulk = call(bulk_kernel, [bulk_shape, bulk_shape], [*fields, eps_back, mine], name="bulk")
    early = lax.axis_size("gx") // 4
    bulk_lower = swapped(*bulk, "gx", stop=early)
    bulk_upper = swapped(*bulk, "gx", start=early)
    y_shape = shape(2 * (13 * nx) + 8, nz)
    coef, mirror_coef, y_far, y_near = call(
        coef_kernel, [block, shape(ny, LANES), y_shape, y_shape], [*bulk_lower, eps_back, mine, theirs] + fields,
        [lines, lines, square], name="coefficient")
    y_far, y_near = swapped(y_far, y_near, "gy")
    x_shape = shape(FIXED + 4 + ny, nz)
    tile = shape(13 * nx, 8, nz)
    tops, ends, mirror, x_far, x_near = call(
        edges_kernel, [tile, tile, shape(4, FRAME, LANES), x_shape, x_shape],
        fields + [coef, mirror_coef, theirs, y_far, y_near],
        [vmem(*x_shape.shape)] * 2, name="edges", work=4_000_000_000)
    x_far, x_near = swapped(x_far, x_near, "gx")
    ef, hf, ea, ha, grad = call(
        step_kernel, [shape(*e_fwd.shape)] * 4 + [shape(*density.shape)],
        fields + [coef, tops, ends, mirror, *bulk_lower, *bulk_upper, x_far, x_near, mine, theirs],
        [vmem(2, 3, nx + 1, FRAME, nz), vmem(2, 3, nx + 1, FRAME, nz), vmem(20, FRAME, nz),
         square, lines, lines, pltpu.SemaphoreType.DMA((4,))], name="steps", any_out=4)
    return ef, hf, ea, ha, grad


def solution(mesh):
    grid = P(None, "gx", "gy", None)
    slab = P(None, "gx", "gy")
    monitor = P(None, None, None, "gx", "gy")
    return jax.shard_map(
        per_device,
        mesh=mesh,
        in_specs=(grid, grid, grid, grid, P("gx", "gy", None), slab, slab, slab, monitor, monitor),
        out_specs=(grid, grid, grid, grid, slab),
        check_vma=False,
    )
```

```python
import math

import jax
import jax.numpy as jnp
from jax import lax
from jax.experimental import pallas as pl
from jax.experimental.pallas import tpu as pltpu
from jax.sharding import PartitionSpec as P

PLANES = 4
Z0 = 126
COURANT = 0.5
OMEGA = 0.7
CONTRAST = 10.0
F32 = jnp.float32
VMEM_LIMIT = 32 * 1024 * 1024
FAR_LIMIT = 60 * 1024 * 1024

LANES = 128
FRAME = 48
TOP, END = 8, 40
WINDOW = 8
SHIFT = LANES - (Z0 - 2)
ROW_EPS, ROW_MON, MESSAGE = 96, 128, 192


def lane_of(shape):
    return lax.broadcasted_iota(jnp.int32, shape, len(shape) - 1)


def row_of(shape):
    return lax.broadcasted_iota(jnp.int32, shape, len(shape) - 2)


def turn(a, shift):
    shift = shift % a.shape[1]
    return pltpu.roll(a, shift, 1) if shift else a


def up_y(a):
    return pltpu.roll(a, a.shape[0] - 1, 0)


def down_y(a):
    return pltpu.roll(a, 1, 0)


def up_z(a):
    n = a.shape[1]
    return jnp.where(lane_of(a.shape) == n - 1, 0.0, pltpu.roll(a, n - 1, 1))


def down_z(a):
    return jnp.where(lane_of(a.shape) == 0, 0.0, pltpu.roll(a, 1, 1))


def is_odd(axis):
    return lax.axis_index(axis) % 2 == 1


def ordered(odd, up, down):
    return jnp.where(odd, up, down), jnp.where(odd, down, up)


def pack_planes(planes):
    total = None
    for offset, plane in planes:
        near = jnp.where(lane_of((plane.shape[0], LANES)) >= LANES // 2,
                         plane[:, :LANES], plane[:, LANES:2 * LANES])
        part = turn(near, SHIFT + offset)
        lane = lane_of(part.shape)
        inside = (lane >= offset) & (lane < offset + WINDOW)
        total = jnp.where(inside, part, 0.0 if total is None else total)
    return total


def flipped(a, square):
    square[...] = jnp.zeros_like(square)
    square[pl.ds(0, a.shape[0]), pl.ds(0, a.shape[1])] = a
    return jnp.transpose(square[...])


def edge_planes(part, ks, nx, mark):
    up, down = [], []
    last = nx - 1
    for f in range(2):
        e = lambda c, x: part(f, 0, c, x)
        h = lambda c, x: part(f, 1, c, x)
        k = ks[last]
        ex, ey, ez = e(0, last), e(1, last), e(2, last)
        ex_b, ey_b, ez_b = e(0, last - 1), e(1, last - 1), e(2, last - 1)
        hy_b = mark(h(1, last - 1) - COURANT * ((up_z(ex_b) - ex_b) - (ez - ez_b)), last - 1)
        hz_b = mark(h(2, last - 1) - COURANT * ((ey - ey_b) - (up_y(ex_b) - ex_b)), last - 1)
        hx = mark(h(0, last) - COURANT * ((up_y(ez) - ez) - (up_z(ey) - ey)), last)
        hy = mark(h(1, last) - COURANT * ((up_z(ex) - ex) + ez), last)
        hz = mark(h(2, last) - COURANT * (-ey - (up_y(ex) - ex)), last)
        ex = ex + k * ((hz - down_y(hz)) - (hy - down_z(hy)))
        ey = ey + k * ((hx - down_z(hx)) - (hz - hz_b))
        ez = ez + k * ((hy - hy_b) - (hx - down_y(hx)))
        up += [hy, hz, mark(hy - COURANT * ((up_z(ex) - ex) + ez), last),
               mark(hz - COURANT * (-ey - (up_y(ex) - ex)), last)]
        k = ks[0]
        ex, ey, ez = e(0, 0), e(1, 0), e(2, 0)
        hx = mark(h(0, 0) - COURANT * ((up_y(ez) - ez) - (up_z(ey) - ey)), 0)
        hy = mark(h(1, 0) - COURANT * ((up_z(ex) - ex) - (e(2, 1) - ez)), 0)
        hz = mark(h(2, 0) - COURANT * ((e(1, 1) - ey) - (up_y(ex) - ex)), 0)
        down += [ey, ez, ey + k * ((hx - down_z(hx)) - hz), ez + k * (hy - (hx - down_y(hx)))]
    return up + [ks[last]], down + [ks[0]]


def write_bulk(part, eps, x_far, x_near):
    nx, ny = eps.shape[0], eps.shape[1]
    ks = [COURANT / eps[x] if x in (0, nx - 1) else None for x in range(nx)]
    odd = is_odd("gx")
    for i, planes in enumerate(zip(*edge_planes(part, ks, nx, lambda v, x: v))):
        far, near = ordered(odd, *planes)
        x_far[pl.ds(i * ny, ny), :] = far
        x_near[pl.ds(i * ny, ny), :] = near


def message_kernel(ef, hf, ea, ha, eps, density, mask, partner, mon_f, mon_a,
                   message, fields, eps_in, small_f, small_i, mons, square, sems):
    nx, ny = ef.shape[1], ef.shape[2]
    copies = []
    for f, (e, h) in enumerate(((ef, hf), (ea, ha))):
        for k, source in enumerate((e, h)):
            copies.append(pltpu.make_async_copy(source, fields.at[f, k], sems.at[2 * f + k]))
    copies.append(pltpu.make_async_copy(eps, eps_in, sems.at[4]))
    copies.append(pltpu.make_async_copy(density, small_f, sems.at[5]))
    copies.append(pltpu.make_async_copy(mask, small_i.at[0], sems.at[6]))
    copies.append(pltpu.make_async_copy(partner, small_i.at[1], sems.at[7]))
    copies.append(pltpu.make_async_copy(mon_f, mons.at[0], sems.at[8]))
    copies.append(pltpu.make_async_copy(mon_a, mons.at[1], sems.at[9]))
    for copy in copies:
        copy.start()
    message[pl.ds(ROW_EPS, MESSAGE - ROW_EPS), :] = jnp.zeros((MESSAGE - ROW_EPS, LANES), F32)
    for copy in copies[4:]:
        copy.wait()
    for half, components in ((0, (0, 1)), (1, (2,))):
        square[...] = jnp.zeros_like(square)
        for k, c in enumerate(components):
            for f in range(2):
                for x in range(nx):
                    base = k * 64 + x * 16 + f * 8 + 2
                    square[pl.ds(base, PLANES), pl.ds(0, ny)] = mons[f, 0, c, :, x, :]
                    for p in range(PLANES):
                        at = (base + 4 + p) % LANES
                        square[pl.ds(at, 1), pl.ds(0, ny)] = mons[f, 1, c, p, pl.ds(x, 1), :]
        message[pl.ds(ROW_MON + 32 * half, ny), :] = jnp.transpose(square[...])[:ny]
    own_eps = [(x * 16 + f * 8, eps_in[x]) for x in range(nx) for f in range(2)]
    square[...] = jnp.zeros_like(square)
    for p in range(PLANES):
        square[pl.ds(p * nx, nx), pl.ds(0, ny)] = CONTRAST * small_i[0, p].astype(F32)
        square[pl.ds(16 + p * nx, nx), pl.ds(0, ny)] = small_f[p]
        square[pl.ds(32 + p * nx, nx), pl.ds(0, ny)] = small_i[1, p].astype(F32)
    small = turn(square[pl.ds(0, 32), :], 64)
    index = turn(square[pl.ds(32, 32), :], 96)
    message[pl.ds(ROW_EPS, ny), :] = pack_planes(own_eps) + small + index
    for copy in copies[:4]:
        copy.wait()
    for c in range(3):
        message[pl.ds(c * 32, ny), :] = pack_planes(
            [(k * 64 + x * 16 + f * 8, fields[f, k, c, x])
             for k in range(2) for x in range(nx) for f in range(2)])


def bulk_kernel(ef, hf, ea, ha, eps, message, x_far, x_near):
    del message
    fields = ((ef, hf), (ea, ha))
    write_bulk(lambda f, k, c, x: fields[f][k][c, x], eps, x_far, x_near)


def small_parts(message):
    weight = turn(message[pl.ds(ROW_EPS, 16), :], -64)
    density = turn(message[pl.ds(ROW_EPS + 16, 16), :], -64)
    partner = turn(message[pl.ds(ROW_EPS, 16), :], -96)
    return weight, density, partner


def mirror_take(table, partner, ny):
    inside = lane_of(partner.shape) < ny
    at = jnp.where(inside, partner, 0.0).astype(jnp.int32)
    row, lane = at // ny, at % ny
    got = jnp.zeros(at.shape, F32)
    for r in range(table.shape[0]):
        line = jnp.broadcast_to(table[pl.ds(r, 1), :], at.shape)
        got = jnp.where(row == r, jnp.take_along_axis(line, lane, axis=1), got)
    return got


def spread_slab(values, lines, square, nx, ny):
    lines[...] = values
    square[...] = jnp.zeros_like(square)
    for p in range(PLANES):
        for x in range(nx):
            row = lines[pl.ds(p * nx + x, 1), :]
            square[pl.ds(x * 16 + 2 + p, 1), :] = row
            square[pl.ds(x * 16 + 10 + p, 1), :] = row
    return jnp.transpose(square[...])[:ny]


def coef_kernel(bulk_far, bulk_near, eps, mine, theirs, ef, hf, ea, ha, coef, mirror_coef, y_far, y_near, table, lines, square):
    del bulk_far, bulk_near
    nx = eps.shape[0]
    ny = END - TOP
    weight, density, partner = small_parts(mine)
    weight_m, density_m, partner_m = small_parts(theirs)
    table[...] = density_m
    extra = weight * (0.5 * (density + mirror_take(table, partner, ny)))
    table[...] = density
    extra_m = weight_m * (0.5 * (density_m + mirror_take(table, partner_m, ny)))
    packed = spread_slab(extra, lines, square, nx, ny)
    lane = lane_of(packed.shape)
    for x in range(nx):
        part = turn(packed, -16 * x - SHIFT)
        low = jnp.where(lane >= Z0, part, 0.0)
        high = jnp.where(lane < Z0 + PLANES - LANES, part, 0.0)
        coef[x] = COURANT / (eps[x] + jnp.concatenate([low, high], 1))
    packed = theirs[pl.ds(ROW_EPS, ny), :] + spread_slab(extra_m, lines, square, nx, ny)
    mirror_coef[...] = jnp.where(lane < 64, COURANT / jnp.where(lane < 64, packed, 1.0), 0.0)
    odd = is_odd("gy")

    def put(at, ref, lanes):
        far, near = ordered(odd, ref[pl.ds(ny - 2, 2), :], ref[pl.ds(0, 2), :])
        y_far[pl.ds(at, 2), pl.ds(0, lanes)] = far
        y_near[pl.ds(at, 2), pl.ds(0, lanes)] = near

    for f, pair in enumerate(((ef, hf), (ea, ha))):
        for k, field in enumerate(pair):
            for c in range(3):
                for x in range(nx):
                    put(2 * plane_index(f, k, c, x, nx), field.at[c, x], y_far.shape[1])
    for x in range(nx):
        put(24 * nx + 2 * x, coef.at[x], y_far.shape[1])
    rest = jnp.zeros((8, y_far.shape[1]), F32)
    y_far[pl.ds(26 * nx, 8), :] = rest
    y_near[pl.ds(26 * nx, 8), :] = rest
    for c in range(3):
        put(26 * nx + 2 * c, theirs.at[pl.ds(c * 32, ny), :], LANES)
    put(26 * nx + 6, mirror_coef, LANES)


def plane_index(f, k, c, x, nx):
    return ((f * 2 + k) * 3 + c) * nx + x


def framed(middle, tops, ends, i):
    return jnp.concatenate([tops[i], middle, ends[i]], 0)


ROWS_UP = ((7, 40), (7, 39), (8, 39), (8, 38, 39)) * 2 + ((7, 40),)
ROWS_DOWN = ((6, 7, 40), (7, 40), (7, 39), (8, 39)) * 2 + ((7, 40),)
FIXED = 20
LATER = (2, 3, 6, 7, 8)
SLIM = 6


def edges_kernel(ef, hf, ea, ha, coef, mirror_coef, theirs, y_far, y_near,
                 tops, ends, mirror, x_far, x_near, x_up, x_down):
    nx, ny = coef.shape[0], coef.shape[1]
    fields = ((ef, hf), (ea, ha))
    tops[...] = jnp.zeros_like(tops)
    ends[...] = jnp.zeros_like(ends)
    mirror[...] = jnp.zeros_like(mirror)
    for c in range(3):
        mirror[c, pl.ds(TOP, ny), :] = theirs[pl.ds(c * 32, ny), :]
    mirror[3, pl.ds(TOP, ny), :] = mirror_coef[...]
    odd = is_odd("gy")

    def came(at, lanes):
        high, low = ordered(odd, y_far[pl.ds(at, 2), pl.ds(0, lanes)], y_near[pl.ds(at, 2), pl.ds(0, lanes)])
        return low, high

    for i in range(13 * nx):
        low, high = came(2 * i, y_far.shape[1])
        tops[i, pl.ds(TOP - 2, 2), :] = low
        ends[i, pl.ds(0, 2), :] = high
    for c in range(4):
        low, high = came(26 * nx + 2 * c, LANES)
        mirror[c, pl.ds(TOP - 2, 2), :] = low
        mirror[c, pl.ds(END, 2), :] = high

    def part(f, k, c, x):
        return framed(fields[f][k][c, x], tops, ends, plane_index(f, k, c, x, nx))

    ks = [framed(coef[x], tops, ends, 12 * nx + x) for x in range(nx)]
    up, down = edge_planes(part, ks, nx, lambda v, x: jnp.where(ks[x] > 0, v, 0.0))
    m = [mirror[c] for c in range(3)]
    km = mirror[3]
    lane = lane_of(km.shape)
    first = lane % 64 < 32
    up_m = [jnp.where(first, m[0], turn(m[1], 32)), jnp.where(first, m[2], turn(km, 32))]
    down_m = [jnp.where(first, turn(m[1], -32), m[0]), jnp.where(first, turn(km, -32), m[2])]
    for out, planes, wanted, window, base in ((x_up, up, ROWS_UP, up_m, 96),
                                              (x_down, down, ROWS_DOWN, down_m, 64)):
        at = 0
        for plane, rows in zip(planes, wanted):
            for row in rows:
                out[pl.ds(at, 1), :] = plane[row:row + 1]
                at += 1
        side = window[1]
        for i, plane in enumerate(LATER):
            plane = planes[plane]
            near = jnp.where(lane >= LANES // 2, plane[:, :LANES], plane[:, LANES:])
            part_in = turn(near, SHIFT + base + SLIM * i - 1)
            inside = (lane >= base + SLIM * i) & (lane < base + SLIM * (i + 1))
            side = jnp.where(inside, part_in, side)
        value = jnp.concatenate([window[0], side], 1)
        out[pl.ds(FIXED, 2), :] = value[TOP - 2:TOP]
        out[pl.ds(FIXED + 2, 2), :] = value[END:END + 2]
        out[pl.ds(FIXED + 4, ny), :] = value[TOP:END]
    x_far[...], x_near[...] = ordered(is_odd("gx"), x_up[...], x_down[...])


def slab_gradient(message, first, second, ny):
    total = None
    for c in range(3):
        mon = message[pl.ds(ROW_MON + 32 * (c // 2), ny), :]
        real = turn(mon, -64 * (c % 2))
        imag = turn(real, -4)
        real = real + math.cos(OMEGA) * first[c] + math.cos(2 * OMEGA) * second[c]
        imag = imag - math.sin(OMEGA) * first[c] - math.sin(2 * OMEGA) * second[c]
        term = real * turn(real, -8) - imag * turn(imag, -8)
        total = term if total is None else total + term
    return total


def slab_rows(packed, out, square, nx):
    square[...] = flipped(packed, square)
    for p in range(PLANES):
        for x in range(nx):
            out[pl.ds(p * nx + x, 1), :] = square[pl.ds(x * 16 + 2 + p, 1), :]


def step_kernel(ef_in, hf_in, ea_in, ha_in, coef, tops, ends, mirror, bulk_far_1, bulk_near_1, bulk_far_2, bulk_near_2,
                x_far, x_near, mine, theirs,
                ef_out, hf_out, ea_out, ha_out, grad,
                ee, hh, halo, square, table, lines, sems):
    nx, ny, nz = coef.shape

    fields = ((ef_in, hf_in), (ea_in, ha_in))
    lane = lane_of((ny, LANES))
    odd = is_odd("gx")
    for slot, base in ((0, 96), (10, 64)):
        def source_at(row, rows, slot=slot):
            pair = (x_near, x_far) if slot == 0 else (x_far, x_near)
            return jnp.where(odd, pair[0][pl.ds(row, rows), :], pair[1][pl.ds(row, rows), :])

        def bulk_at(row, rows, slot=slot):
            far = bulk_far_1[pl.ds(row, rows), :] + bulk_far_2[pl.ds(row, rows), :]
            near = bulk_near_1[pl.ds(row, rows), :] + bulk_near_2[pl.ds(row, rows), :]
            return jnp.where(odd, near, far) if slot == 0 else jnp.where(odd, far, near)

        halo[slot + 9, pl.ds(0, TOP), :] = jnp.zeros((TOP, nz), F32)
        halo[slot + 9, pl.ds(END, TOP), :] = jnp.zeros((TOP, nz), F32)
        window = source_at(FIXED + 4, ny)
        halo[slot + 9, pl.ds(TOP, ny), :] = window
        halo[slot + 9, pl.ds(TOP - 2, 2), :] = source_at(FIXED, 2)
        halo[slot + 9, pl.ds(END, 2), :] = source_at(FIXED + 2, 2)
        side = window[:, LANES:]
        row_at = 0
        for plane, rows in enumerate(ROWS_DOWN if slot else ROWS_UP):
            at = slot + plane
            halo[at, pl.ds(0, TOP), :] = jnp.zeros((TOP, nz), F32)
            halo[at, pl.ds(END, TOP), :] = jnp.zeros((TOP, nz), F32)
            value = bulk_at(plane * ny, ny)
            if plane in LATER:
                near = turn(side, 1 - SHIFT - base - SLIM * LATER.index(plane))
                value = jnp.concatenate(
                    [jnp.where(lane >= Z0 - 1, near, value[:, :LANES]),
                     jnp.where(lane < Z0 + PLANES + 1 - LANES, near, value[:, LANES:])], 1)
            halo[at, pl.ds(TOP, ny), :] = value
            for row in rows:
                halo[at, pl.ds(row, 1), :] = source_at(row_at, 1)
                row_at += 1
    k_low, k_high = halo[8], halo[18]

    def part(f, k, c, x):
        return framed(fields[f][k][c, x], tops, ends, plane_index(f, k, c, x, nx))

    def inverse(x):
        return framed(coef[x], tops, ends, 12 * nx + x)

    copies = []
    first_slab, second_slab = [], []
    for f in range(2):
        ey0, ez0 = part(f, 0, 1, 0), part(f, 0, 2, 0)
        dhy = jnp.where(k_low > 0, COURANT * ez0, 0.0)
        dhz = jnp.where(k_low > 0, -COURANT * ey0, 0.0)
        hh[f, 1, 0] = halo[4 * f] + dhy
        hh[f, 2, 0] = halo[4 * f + 1] + dhz
        for x in range(nx):
            inside = inverse(x) > 0
            ex, ey, ez = part(f, 0, 0, x), part(f, 0, 1, x), part(f, 0, 2, x)
            ey_n = part(f, 0, 1, x + 1) if x + 1 < nx else halo[10 + 4 * f]
            ez_n = part(f, 0, 2, x + 1) if x + 1 < nx else halo[10 + 4 * f + 1]
            hx, hy, hz = part(f, 1, 0, x), part(f, 1, 1, x), part(f, 1, 2, x)
            hh[f, 0, x + 1] = jnp.where(inside, hx - COURANT * ((up_y(ez) - ez) - (up_z(ey) - ey)), 0.0)
            hh[f, 1, x + 1] = jnp.where(inside, hy - COURANT * ((up_z(ex) - ex) - (ez_n - ez)), 0.0)
            hh[f, 2, x + 1] = jnp.where(inside, hz - COURANT * ((ey_n - ey) - (up_y(ex) - ex)), 0.0)
        for x in range(nx):
            k = inverse(x)
            hx, hy, hz = hh[f, 0, x + 1], hh[f, 1, x + 1], hh[f, 2, x + 1]
            ee[f, 0, x] = part(f, 0, 0, x) + k * ((hz - down_y(hz)) - (hy - down_z(hy)))
            ee[f, 1, x] = part(f, 0, 1, x) + k * ((hx - down_z(hx)) - (hz - hh[f, 2, x]))
            ee[f, 2, x] = part(f, 0, 2, x) + k * ((hy - hh[f, 1, x]) - (hx - down_y(hx)))
        ee[f, 1, nx] = halo[10 + 4 * f + 2] + k_high * hh[f, 2, nx]
        ee[f, 2, nx] = halo[10 + 4 * f + 3] - k_high * hh[f, 1, nx]
        dex = k_low * ((dhz - down_y(dhz)) - (dhy - down_z(dhy)))
        dey = -k_low * dhz
        dez = k_low * dhy
        hh[f, 1, 0] = jnp.where(
            k_low > 0, halo[4 * f + 2] + dhy - COURANT * ((up_z(dex) - dex) - (ee[f, 2, 0] - dez)), 0.0)
        hh[f, 2, 0] = jnp.where(
            k_low > 0, halo[4 * f + 3] + dhz - COURANT * ((ee[f, 1, 0] - dey) - (up_y(dex) - dex)), 0.0)
        for x in range(nx):
            inside = inverse(x) > 0
            ex, ey, ez = ee[f, 0, x], ee[f, 1, x], ee[f, 2, x]
            hh[f, 0, x + 1] = jnp.where(
                inside, hh[f, 0, x + 1] - COURANT * ((up_y(ez) - ez) - (up_z(ey) - ey)), 0.0)
            hh[f, 1, x + 1] = jnp.where(
                inside, hh[f, 1, x + 1] - COURANT * ((up_z(ex) - ex) - (ee[f, 2, x + 1] - ez)), 0.0)
            hh[f, 2, x + 1] = jnp.where(
                inside, hh[f, 2, x + 1] - COURANT * ((ee[f, 1, x + 1] - ey) - (up_y(ex) - ex)), 0.0)
        copies.append(pltpu.make_async_copy(
            hh.at[f, :, pl.ds(1, nx), pl.ds(TOP, ny), :], (hf_out, ha_out)[f], sems.at[2 * f]))
        copies[-1].start()
    for c in range(3):
        first_slab.append(pack_planes([(x * 16 + f * 8, ee[f, c, x, pl.ds(TOP, ny), :])
                                       for x in range(nx) for f in range(2)]))
    for f in range(2):
        for x in range(nx):
            k = inverse(x)
            hx, hy, hz = hh[f, 0, x + 1], hh[f, 1, x + 1], hh[f, 2, x + 1]
            ee[f, 0, x] = ee[f, 0, x] + k * ((hz - down_y(hz)) - (hy - down_z(hy)))
            ee[f, 1, x] = ee[f, 1, x] + k * ((hx - down_z(hx)) - (hz - hh[f, 2, x]))
            ee[f, 2, x] = ee[f, 2, x] + k * ((hy - hh[f, 1, x]) - (hx - down_y(hx)))
        copies.append(pltpu.make_async_copy(
            ee.at[f, :, pl.ds(0, nx), pl.ds(TOP, ny), :], (ef_out, ea_out)[f], sems.at[2 * f + 1]))
        copies[-1].start()
    for c in range(3):
        second_slab.append(pack_planes([(x * 16 + f * 8, ee[f, c, x, pl.ds(TOP, ny), :])
                                        for x in range(nx) for f in range(2)]))
    own = slab_gradient(mine, first_slab, second_slab, ny)

    low01, low2 = halo[9, :, pl.ds(0, LANES)], halo[9, :, pl.ds(LANES, LANES)]
    high01, high2 = halo[19, :, pl.ds(0, LANES)], halo[19, :, pl.ds(LANES, LANES)]
    lane = lane_of(low01.shape)

    def join(below, middle, above):
        return jnp.where(lane < 32, below, jnp.where(lane < 96, middle, above))

    m = [mirror[c] for c in range(3)]
    e = [join(turn(high01, -32), turn(m[0], 32), turn(low01, 96)),
         join(high01, turn(m[1], 32), turn(low01, 64)),
         join(turn(high2, -32), turn(m[2], 32), turn(low2, 96))]
    h = [join(turn(high01, -96), turn(m[0], -32), turn(low01, 32)),
         join(turn(high01, -64), turn(m[1], -32), low01),
         join(turn(high2, -96), turn(m[2], -32), turn(low2, 32))]
    k = join(high2, turn(mirror[3], 32), turn(low2, 64))
    inside = k > 0

    def ahead(a, axis):
        return (turn(a, -16), up_y(a), turn(a, -1))[axis] - a

    def behind(a, axis):
        return a - (turn(a, 16), down_y(a), turn(a, 1))[axis]

    slabs = []
    for _ in range(2):
        h = [jnp.where(inside, h[c] - COURANT * (ahead(e[(c + 2) % 3], (c + 1) % 3)
                                                 - ahead(e[(c + 1) % 3], (c + 2) % 3)), 0.0)
             for c in range(3)]
        e = [e[c] + k * (behind(h[(c + 2) % 3], (c + 1) % 3) - behind(h[(c + 1) % 3], (c + 2) % 3))
             for c in range(3)]
        slabs.append([turn(e[c], -32)[TOP:END] for c in range(3)])
    other = slab_gradient(theirs, slabs[0], slabs[1], ny)

    weight, _, partner = small_parts(mine)
    weight_m, _, _ = small_parts(theirs)
    slab_rows(other, table, square, nx)
    table[...] = table[...] * weight_m
    got = mirror_take(table, partner, ny)
    slab_rows(own, lines, square, nx)
    lines[...] = 0.5 * (lines[...] * weight + got)
    for p in range(PLANES):
        grad[p] = lines[pl.ds(p * nx, nx), pl.ds(0, ny)]
    for copy in copies:
        copy.wait()


def call(kernel, outs, args, scratch=(), name=None, any_in=False, any_out=0, work=4_000_000):
    spaces = lambda count, far: [pl.BlockSpec(memory_space=pltpu.HBM if i < far else pltpu.VMEM)
                                 for i in range(count)]
    return pl.pallas_call(
        kernel,
        out_shape=outs,
        in_specs=[pl.BlockSpec(memory_space=pltpu.HBM if any_in else pltpu.VMEM)] * len(args),
        out_specs=spaces(len(outs), any_out),
        scratch_shapes=list(scratch),
        compiler_params=pltpu.CompilerParams(vmem_limit_bytes=FAR_LIMIT if any_in else VMEM_LIMIT),
        cost_estimate=pl.CostEstimate(flops=work, bytes_accessed=4_000_000, transcendentals=0),
        name=name,
    )(*args)


def swapped(far, near, axis, start=0, stop=None):
    size = lax.axis_size(axis)

    def pairs(first):
        lows = [i for i in range(first, size - 1, 2) if start <= i < (size if stop is None else stop)]
        return [(i, i + 1) for i in lows] + [(i + 1, i) for i in lows]

    return lax.ppermute(far, axis, pairs(1)), lax.ppermute(near, axis, pairs(0))


def mirrored(block, axis):
    size = lax.axis_size(axis)
    return lax.ppermute(block, axis, [(i, size - 1 - i) for i in range(size)])


def per_device(e_fwd, h_fwd, e_adj, h_adj, eps_back, density, design_mask, partner_map, mon_fwd, mon_adj):
    _, nx, ny, nz = e_fwd.shape
    shape = lambda *dims: jax.ShapeDtypeStruct(dims, F32)
    vmem = lambda *dims: pltpu.VMEM(dims, F32)
    square = vmem(LANES, LANES)
    lines = vmem(PLANES * nx, LANES)
    block = shape(nx, ny, nz)
    fields = [e_fwd, h_fwd, e_adj, h_adj]

    bulk_shape = shape(9 * ny, nz)
    mine, = call(
        message_kernel, [shape(MESSAGE, LANES)],
        fields + [eps_back, density, design_mask, partner_map, mon_fwd, mon_adj],
        [vmem(2, 2, 3, nx, ny, nz), vmem(nx, ny, nz), vmem(*density.shape),
         pltpu.VMEM((2,) + density.shape, jnp.int32), vmem(2, *mon_fwd.shape),
         square, pltpu.SemaphoreType.DMA((10,))], name="message", any_in=True)
    theirs = mirrored(mine, "gx")
    bulk = call(bulk_kernel, [bulk_shape, bulk_shape], [*fields, eps_back, mine], name="bulk")
    early = 7 * lax.axis_size("gx") // 16
    bulk_lower = swapped(*bulk, "gx", stop=early)
    bulk_upper = swapped(*bulk, "gx", start=early)
    y_shape = shape(2 * (13 * nx) + 8, nz)
    coef, mirror_coef, y_far, y_near = call(
        coef_kernel, [block, shape(ny, LANES), y_shape, y_shape], [*bulk_lower, eps_back, mine, theirs] + fields,
        [lines, lines, square], name="coefficient")
    y_far, y_near = swapped(y_far, y_near, "gy")
    x_shape = shape(FIXED + 4 + ny, nz)
    tile = shape(13 * nx, 8, nz)
    tops, ends, mirror, x_far, x_near = call(
        edges_kernel, [tile, tile, shape(4, FRAME, LANES), x_shape, x_shape],
        fields + [coef, mirror_coef, theirs, y_far, y_near],
        [vmem(*x_shape.shape)] * 2, name="edges", work=1_000_000_000)
    x_far, x_near = swapped(x_far, x_near, "gx")
    ef, hf, ea, ha, grad = call(
        step_kernel, [shape(*e_fwd.shape)] * 4 + [shape(*density.shape)],
        fields + [coef, tops, ends, mirror, *bulk_lower, *bulk_upper, x_far, x_near, mine, theirs],
        [vmem(2, 3, nx + 1, FRAME, nz), vmem(2, 3, nx + 1, FRAME, nz), vmem(20, FRAME, nz),
         square, lines, lines, pltpu.SemaphoreType.DMA((4,))], name="steps", any_out=4)
    return ef, hf, ea, ha, grad


def solution(mesh):
    grid = P(None, "gx", "gy", None)
    slab = P(None, "gx", "gy")
    monitor = P(None, None, None, "gx", "gy")
    return jax.shard_map(
        per_device,
        mesh=mesh,
        in_specs=(grid, grid, grid, grid, P("gx", "gy", None), slab, slab, slab, monitor, monitor),
        out_specs=(grid, grid, grid, grid, slab),
        check_vma=False,
    )
```

```python
import math

import jax
import jax.numpy as jnp
from jax import lax
from jax.experimental import pallas as pl
from jax.experimental.pallas import tpu as pltpu
from jax.sharding import PartitionSpec as P

PLANES = 4
Z0 = 126
COURANT = 0.5
OMEGA = 0.7
CONTRAST = 10.0
F32 = jnp.float32
VMEM_LIMIT = 32 * 1024 * 1024
FAR_LIMIT = 60 * 1024 * 1024

LANES = 128
FRAME = 48
TOP, END = 8, 40
WINDOW = 8
SHIFT = LANES - (Z0 - 2)
ROW_EPS, ROW_MON, MESSAGE = 96, 128, 192


def lane_of(shape):
    return lax.broadcasted_iota(jnp.int32, shape, len(shape) - 1)


def row_of(shape):
    return lax.broadcasted_iota(jnp.int32, shape, len(shape) - 2)


def turn(a, shift):
    shift = shift % a.shape[1]
    return pltpu.roll(a, shift, 1) if shift else a


def up_y(a):
    return pltpu.roll(a, a.shape[0] - 1, 0)


def down_y(a):
    return pltpu.roll(a, 1, 0)


def up_z(a):
    n = a.shape[1]
    return jnp.where(lane_of(a.shape) == n - 1, 0.0, pltpu.roll(a, n - 1, 1))


def down_z(a):
    return jnp.where(lane_of(a.shape) == 0, 0.0, pltpu.roll(a, 1, 1))


def is_odd(axis):
    return lax.axis_index(axis) % 2 == 1


def ordered(odd, up, down):
    return jnp.where(odd, up, down), jnp.where(odd, down, up)


def pack_planes(planes):
    total = None
    for offset, plane in planes:
        near = jnp.where(lane_of((plane.shape[0], LANES)) >= LANES // 2,
                         plane[:, :LANES], plane[:, LANES:2 * LANES])
        part = turn(near, SHIFT + offset)
        lane = lane_of(part.shape)
        inside = (lane >= offset) & (lane < offset + WINDOW)
        total = jnp.where(inside, part, 0.0 if total is None else total)
    return total


def flipped(a, square):
    square[...] = jnp.zeros_like(square)
    square[pl.ds(0, a.shape[0]), pl.ds(0, a.shape[1])] = a
    return jnp.transpose(square[...])


def edge_planes(part, ks, nx, mark):
    up, down = [], []
    last = nx - 1
    for f in range(2):
        e = lambda c, x: part(f, 0, c, x)
        h = lambda c, x: part(f, 1, c, x)
        k = ks[last]
        ex, ey, ez = e(0, last), e(1, last), e(2, last)
        ex_b, ey_b, ez_b = e(0, last - 1), e(1, last - 1), e(2, last - 1)
        hy_b = mark(h(1, last - 1) - COURANT * ((up_z(ex_b) - ex_b) - (ez - ez_b)), last - 1)
        hz_b = mark(h(2, last - 1) - COURANT * ((ey - ey_b) - (up_y(ex_b) - ex_b)), last - 1)
        hx = mark(h(0, last) - COURANT * ((up_y(ez) - ez) - (up_z(ey) - ey)), last)
        hy = mark(h(1, last) - COURANT * ((up_z(ex) - ex) + ez), last)
        hz = mark(h(2, last) - COURANT * (-ey - (up_y(ex) - ex)), last)
        ex = ex + k * ((hz - down_y(hz)) - (hy - down_z(hy)))
        ey = ey + k * ((hx - down_z(hx)) - (hz - hz_b))
        ez = ez + k * ((hy - hy_b) - (hx - down_y(hx)))
        up += [hy, hz, mark(hy - COURANT * ((up_z(ex) - ex) + ez), last),
               mark(hz - COURANT * (-ey - (up_y(ex) - ex)), last)]
        k = ks[0]
        ex, ey, ez = e(0, 0), e(1, 0), e(2, 0)
        hx = mark(h(0, 0) - COURANT * ((up_y(ez) - ez) - (up_z(ey) - ey)), 0)
        hy = mark(h(1, 0) - COURANT * ((up_z(ex) - ex) - (e(2, 1) - ez)), 0)
        hz = mark(h(2, 0) - COURANT * ((e(1, 1) - ey) - (up_y(ex) - ex)), 0)
        down += [ey, ez, ey + k * ((hx - down_z(hx)) - hz), ez + k * (hy - (hx - down_y(hx)))]
    return up + [ks[last]], down + [ks[0]]


def write_bulk(part, eps, x_far, x_near):
    nx, ny = eps.shape[0], eps.shape[1]
    ks = [COURANT / eps[x] if x in (0, nx - 1) else None for x in range(nx)]
    odd = is_odd("gx")
    for i, planes in enumerate(zip(*edge_planes(part, ks, nx, lambda v, x: v))):
        far, near = ordered(odd, *planes)
        x_far[pl.ds(i * ny, ny), :] = far
        x_near[pl.ds(i * ny, ny), :] = near


def message_kernel(ef, hf, ea, ha, eps, density, mask, partner, mon_f, mon_a,
                   message, fields, eps_in, small_f, small_i, mons, square, sems):
    nx, ny = ef.shape[1], ef.shape[2]
    copies = []
    for f, (e, h) in enumerate(((ef, hf), (ea, ha))):
        for k, source in enumerate((e, h)):
            copies.append(pltpu.make_async_copy(source, fields.at[f, k], sems.at[2 * f + k]))
    copies.append(pltpu.make_async_copy(eps, eps_in, sems.at[4]))
    copies.append(pltpu.make_async_copy(density, small_f, sems.at[5]))
    copies.append(pltpu.make_async_copy(mask, small_i.at[0], sems.at[6]))
    copies.append(pltpu.make_async_copy(partner, small_i.at[1], sems.at[7]))
    copies.append(pltpu.make_async_copy(mon_f, mons.at[0], sems.at[8]))
    copies.append(pltpu.make_async_copy(mon_a, mons.at[1], sems.at[9]))
    for copy in copies:
        copy.start()
    message[pl.ds(ROW_EPS, MESSAGE - ROW_EPS), :] = jnp.zeros((MESSAGE - ROW_EPS, LANES), F32)
    for copy in copies[4:]:
        copy.wait()
    for half, components in ((0, (0, 1)), (1, (2,))):
        square[...] = jnp.zeros_like(square)
        for k, c in enumerate(components):
            for f in range(2):
                for x in range(nx):
                    base = k * 64 + x * 16 + f * 8 + 2
                    square[pl.ds(base, PLANES), pl.ds(0, ny)] = mons[f, 0, c, :, x, :]
                    for p in range(PLANES):
                        at = (base + 4 + p) % LANES
                        square[pl.ds(at, 1), pl.ds(0, ny)] = mons[f, 1, c, p, pl.ds(x, 1), :]
        message[pl.ds(ROW_MON + 32 * half, ny), :] = jnp.transpose(square[...])[:ny]
    own_eps = [(x * 16 + f * 8, eps_in[x]) for x in range(nx) for f in range(2)]
    square[...] = jnp.zeros_like(square)
    for p in range(PLANES):
        square[pl.ds(p * nx, nx), pl.ds(0, ny)] = CONTRAST * small_i[0, p].astype(F32)
        square[pl.ds(16 + p * nx, nx), pl.ds(0, ny)] = small_f[p]
        square[pl.ds(32 + p * nx, nx), pl.ds(0, ny)] = small_i[1, p].astype(F32)
    small = turn(square[pl.ds(0, 32), :], 64)
    index = turn(square[pl.ds(32, 32), :], 96)
    message[pl.ds(ROW_EPS, ny), :] = pack_planes(own_eps) + small + index
    for copy in copies[:4]:
        copy.wait()
    for c in range(3):
        message[pl.ds(c * 32, ny), :] = pack_planes(
            [(k * 64 + x * 16 + f * 8, fields[f, k, c, x])
             for k in range(2) for x in range(nx) for f in range(2)])


def bulk_kernel(ef, hf, ea, ha, eps, message, x_far, x_near):
    del message
    fields = ((ef, hf), (ea, ha))
    write_bulk(lambda f, k, c, x: fields[f][k][c, x], eps, x_far, x_near)


def small_parts(message):
    weight = turn(message[pl.ds(ROW_EPS, 16), :], -64)
    density = turn(message[pl.ds(ROW_EPS + 16, 16), :], -64)
    partner = turn(message[pl.ds(ROW_EPS, 16), :], -96)
    return weight, density, partner


def mirror_take(table, partner, ny):
    inside = lane_of(partner.shape) < ny
    at = jnp.where(inside, partner, 0.0).astype(jnp.int32)
    row, lane = at // ny, at % ny
    got = jnp.zeros(at.shape, F32)
    for r in range(table.shape[0]):
        line = jnp.broadcast_to(table[pl.ds(r, 1), :], at.shape)
        got = jnp.where(row == r, jnp.take_along_axis(line, lane, axis=1), got)
    return got


def spread_slab(values, lines, square, nx, ny):
    lines[...] = values
    square[...] = jnp.zeros_like(square)
    for p in range(PLANES):
        for x in range(nx):
            row = lines[pl.ds(p * nx + x, 1), :]
            square[pl.ds(x * 16 + 2 + p, 1), :] = row
            square[pl.ds(x * 16 + 10 + p, 1), :] = row
    return jnp.transpose(square[...])[:ny]


def coef_kernel(bulk_far, bulk_near, eps, mine, theirs, ef, hf, ea, ha, coef, mirror_coef, y_far, y_near, table, lines, square):
    del bulk_far, bulk_near
    nx = eps.shape[0]
    ny = END - TOP
    weight, density, partner = small_parts(mine)
    weight_m, density_m, partner_m = small_parts(theirs)
    table[...] = density_m
    extra = weight * (0.5 * (density + mirror_take(table, partner, ny)))
    table[...] = density
    extra_m = weight_m * (0.5 * (density_m + mirror_take(table, partner_m, ny)))
    packed = spread_slab(extra, lines, square, nx, ny)
    lane = lane_of(packed.shape)
    for x in range(nx):
        part = turn(packed, -16 * x - SHIFT)
        low = jnp.where(lane >= Z0, part, 0.0)
        high = jnp.where(lane < Z0 + PLANES - LANES, part, 0.0)
        coef[x] = COURANT / (eps[x] + jnp.concatenate([low, high], 1))
    packed = theirs[pl.ds(ROW_EPS, ny), :] + spread_slab(extra_m, lines, square, nx, ny)
    mirror_coef[...] = jnp.where(lane < 64, COURANT / jnp.where(lane < 64, packed, 1.0), 0.0)
    odd = is_odd("gy")

    def put(at, ref, lanes):
        far, near = ordered(odd, ref[pl.ds(ny - 2, 2), :], ref[pl.ds(0, 2), :])
        y_far[pl.ds(at, 2), pl.ds(0, lanes)] = far
        y_near[pl.ds(at, 2), pl.ds(0, lanes)] = near

    for f, pair in enumerate(((ef, hf), (ea, ha))):
        for k, field in enumerate(pair):
            for c in range(3):
                for x in range(nx):
                    put(2 * plane_index(f, k, c, x, nx), field.at[c, x], y_far.shape[1])
    for x in range(nx):
        put(24 * nx + 2 * x, coef.at[x], y_far.shape[1])
    rest = jnp.zeros((8, y_far.shape[1]), F32)
    y_far[pl.ds(26 * nx, 8), :] = rest
    y_near[pl.ds(26 * nx, 8), :] = rest
    for c in range(3):
        put(26 * nx + 2 * c, theirs.at[pl.ds(c * 32, ny), :], LANES)
    put(26 * nx + 6, mirror_coef, LANES)


def plane_index(f, k, c, x, nx):
    return ((f * 2 + k) * 3 + c) * nx + x


def framed(middle, tops, ends, i):
    return jnp.concatenate([tops[i], middle, ends[i]], 0)


ROWS_UP = ((7, 40), (7, 39), (8, 39), (8, 38, 39)) * 2 + ((7, 40),)
ROWS_DOWN = ((6, 7, 40), (7, 40), (7, 39), (8, 39)) * 2 + ((7, 40),)
FIXED = 20
LATER = (2, 3, 6, 7, 8)
SLIM = 6


def edges_kernel(bulk_far, ef, hf, ea, ha, coef, mirror_coef, theirs, y_far, y_near,
                 tops, ends, mirror, x_far, x_near, x_up, x_down):
    del bulk_far
    nx, ny = coef.shape[0], coef.shape[1]
    fields = ((ef, hf), (ea, ha))
    tops[...] = jnp.zeros_like(tops)
    ends[...] = jnp.zeros_like(ends)
    mirror[...] = jnp.zeros_like(mirror)
    for c in range(3):
        mirror[c, pl.ds(TOP, ny), :] = theirs[pl.ds(c * 32, ny), :]
    mirror[3, pl.ds(TOP, ny), :] = mirror_coef[...]
    odd = is_odd("gy")

    def came(at, lanes):
        high, low = ordered(odd, y_far[pl.ds(at, 2), pl.ds(0, lanes)], y_near[pl.ds(at, 2), pl.ds(0, lanes)])
        return low, high

    for i in range(13 * nx):
        low, high = came(2 * i, y_far.shape[1])
        tops[i, pl.ds(TOP - 2, 2), :] = low
        ends[i, pl.ds(0, 2), :] = high
    for c in range(4):
        low, high = came(26 * nx + 2 * c, LANES)
        mirror[c, pl.ds(TOP - 2, 2), :] = low
        mirror[c, pl.ds(END, 2), :] = high

    def part(f, k, c, x):
        return framed(fields[f][k][c, x], tops, ends, plane_index(f, k, c, x, nx))

    ks = [framed(coef[x], tops, ends, 12 * nx + x) for x in range(nx)]
    up, down = edge_planes(part, ks, nx, lambda v, x: jnp.where(ks[x] > 0, v, 0.0))
    m = [mirror[c] for c in range(3)]
    km = mirror[3]
    lane = lane_of(km.shape)
    first = lane % 64 < 32
    up_m = [jnp.where(first, m[0], turn(m[1], 32)), jnp.where(first, m[2], turn(km, 32))]
    down_m = [jnp.where(first, turn(m[1], -32), m[0]), jnp.where(first, turn(km, -32), m[2])]
    for out, planes, wanted, window, base in ((x_up, up, ROWS_UP, up_m, 96),
                                              (x_down, down, ROWS_DOWN, down_m, 64)):
        at = 0
        for plane, rows in zip(planes, wanted):
            for row in rows:
                out[pl.ds(at, 1), :] = plane[row:row + 1]
                at += 1
        side = window[1]
        for i, plane in enumerate(LATER):
            plane = planes[plane]
            near = jnp.where(lane >= LANES // 2, plane[:, :LANES], plane[:, LANES:])
            part_in = turn(near, SHIFT + base + SLIM * i - 1)
            inside = (lane >= base + SLIM * i) & (lane < base + SLIM * (i + 1))
            side = jnp.where(inside, part_in, side)
        value = jnp.concatenate([window[0], side], 1)
        out[pl.ds(FIXED, 2), :] = value[TOP - 2:TOP]
        out[pl.ds(FIXED + 2, 2), :] = value[END:END + 2]
        out[pl.ds(FIXED + 4, ny), :] = value[TOP:END]
    x_far[...], x_near[...] = ordered(is_odd("gx"), x_up[...], x_down[...])


def slab_gradient(message, first, second, ny):
    total = None
    for c in range(3):
        mon = message[pl.ds(ROW_MON + 32 * (c // 2), ny), :]
        real = turn(mon, -64 * (c % 2))
        imag = turn(real, -4)
        real = real + math.cos(OMEGA) * first[c] + math.cos(2 * OMEGA) * second[c]
        imag = imag - math.sin(OMEGA) * first[c] - math.sin(2 * OMEGA) * second[c]
        term = real * turn(real, -8) - imag * turn(imag, -8)
        total = term if total is None else total + term
    return total


def slab_rows(packed, out, square, nx):
    square[...] = flipped(packed, square)
    for p in range(PLANES):
        for x in range(nx):
            out[pl.ds(p * nx + x, 1), :] = square[pl.ds(x * 16 + 2 + p, 1), :]


def step_kernel(ef_in, hf_in, ea_in, ha_in, coef, tops, ends, mirror, bulk_far_1, bulk_near_1, bulk_far_2, bulk_near_2,
                x_far, x_near, mine, theirs,
                ef_out, hf_out, ea_out, ha_out, grad,
                ee, hh, halo, square, table, lines, sems):
    nx, ny, nz = coef.shape

    fields = ((ef_in, hf_in), (ea_in, ha_in))
    lane = lane_of((ny, LANES))
    odd = is_odd("gx")
    for slot, base in ((0, 96), (10, 64)):
        def source_at(row, rows, slot=slot):
            pair = (x_near, x_far) if slot == 0 else (x_far, x_near)
            return jnp.where(odd, pair[0][pl.ds(row, rows), :], pair[1][pl.ds(row, rows), :])

        def bulk_at(row, rows, slot=slot):
            far = bulk_far_1[pl.ds(row, rows), :] + bulk_far_2[pl.ds(row, rows), :]
            near = bulk_near_1[pl.ds(row, rows), :] + bulk_near_2[pl.ds(row, rows), :]
            return jnp.where(odd, near, far) if slot == 0 else jnp.where(odd, far, near)

        halo[slot + 9, pl.ds(0, TOP), :] = jnp.zeros((TOP, nz), F32)
        halo[slot + 9, pl.ds(END, TOP), :] = jnp.zeros((TOP, nz), F32)
        window = source_at(FIXED + 4, ny)
        halo[slot + 9, pl.ds(TOP, ny), :] = window
        halo[slot + 9, pl.ds(TOP - 2, 2), :] = source_at(FIXED, 2)
        halo[slot + 9, pl.ds(END, 2), :] = source_at(FIXED + 2, 2)
        side = window[:, LANES:]
        row_at = 0
        for plane, rows in enumerate(ROWS_DOWN if slot else ROWS_UP):
            at = slot + plane
            halo[at, pl.ds(0, TOP), :] = jnp.zeros((TOP, nz), F32)
            halo[at, pl.ds(END, TOP), :] = jnp.zeros((TOP, nz), F32)
            value = bulk_at(plane * ny, ny)
            if plane in LATER:
                near = turn(side, 1 - SHIFT - base - SLIM * LATER.index(plane))
                value = jnp.concatenate(
                    [jnp.where(lane >= Z0 - 1, near, value[:, :LANES]),
                     jnp.where(lane < Z0 + PLANES + 1 - LANES, near, value[:, LANES:])], 1)
            halo[at, pl.ds(TOP, ny), :] = value
            for row in rows:
                halo[at, pl.ds(row, 1), :] = source_at(row_at, 1)
                row_at += 1
    k_low, k_high = halo[8], halo[18]

    def part(f, k, c, x):
        return framed(fields[f][k][c, x], tops, ends, plane_index(f, k, c, x, nx))

    def inverse(x):
        return framed(coef[x], tops, ends, 12 * nx + x)

    copies = []
    first_slab, second_slab = [], []
    for f in range(2):
        ey0, ez0 = part(f, 0, 1, 0), part(f, 0, 2, 0)
        dhy = jnp.where(k_low > 0, COURANT * ez0, 0.0)
        dhz = jnp.where(k_low > 0, -COURANT * ey0, 0.0)
        hh[f, 1, 0] = halo[4 * f] + dhy
        hh[f, 2, 0] = halo[4 * f + 1] + dhz
        for x in range(nx):
            inside = inverse(x) > 0
            ex, ey, ez = part(f, 0, 0, x), part(f, 0, 1, x), part(f, 0, 2, x)
            ey_n = part(f, 0, 1, x + 1) if x + 1 < nx else halo[10 + 4 * f]
            ez_n = part(f, 0, 2, x + 1) if x + 1 < nx else halo[10 + 4 * f + 1]
            hx, hy, hz = part(f, 1, 0, x), part(f, 1, 1, x), part(f, 1, 2, x)
            hh[f, 0, x + 1] = jnp.where(inside, hx - COURANT * ((up_y(ez) - ez) - (up_z(ey) - ey)), 0.0)
            hh[f, 1, x + 1] = jnp.where(inside, hy - COURANT * ((up_z(ex) - ex) - (ez_n - ez)), 0.0)
            hh[f, 2, x + 1] = jnp.where(inside, hz - COURANT * ((ey_n - ey) - (up_y(ex) - ex)), 0.0)
        for x in range(nx):
            k = inverse(x)
            hx, hy, hz = hh[f, 0, x + 1], hh[f, 1, x + 1], hh[f, 2, x + 1]
            ee[f, 0, x] = part(f, 0, 0, x) + k * ((hz - down_y(hz)) - (hy - down_z(hy)))
            ee[f, 1, x] = part(f, 0, 1, x) + k * ((hx - down_z(hx)) - (hz - hh[f, 2, x]))
            ee[f, 2, x] = part(f, 0, 2, x) + k * ((hy - hh[f, 1, x]) - (hx - down_y(hx)))
        ee[f, 1, nx] = halo[10 + 4 * f + 2] + k_high * hh[f, 2, nx]
        ee[f, 2, nx] = halo[10 + 4 * f + 3] - k_high * hh[f, 1, nx]
        dex = k_low * ((dhz - down_y(dhz)) - (dhy - down_z(dhy)))
        dey = -k_low * dhz
        dez = k_low * dhy
        hh[f, 1, 0] = jnp.where(
            k_low > 0, halo[4 * f + 2] + dhy - COURANT * ((up_z(dex) - dex) - (ee[f, 2, 0] - dez)), 0.0)
        hh[f, 2, 0] = jnp.where(
            k_low > 0, halo[4 * f + 3] + dhz - COURANT * ((ee[f, 1, 0] - dey) - (up_y(dex) - dex)), 0.0)
        for x in range(nx):
            inside = inverse(x) > 0
            ex, ey, ez = ee[f, 0, x], ee[f, 1, x], ee[f, 2, x]
            hh[f, 0, x + 1] = jnp.where(
                inside, hh[f, 0, x + 1] - COURANT * ((up_y(ez) - ez) - (up_z(ey) - ey)), 0.0)
            hh[f, 1, x + 1] = jnp.where(
                inside, hh[f, 1, x + 1] - COURANT * ((up_z(ex) - ex) - (ee[f, 2, x + 1] - ez)), 0.0)
            hh[f, 2, x + 1] = jnp.where(
                inside, hh[f, 2, x + 1] - COURANT * ((ee[f, 1, x + 1] - ey) - (up_y(ex) - ex)), 0.0)
        copies.append(pltpu.make_async_copy(
            hh.at[f, :, pl.ds(1, nx), pl.ds(TOP, ny), :], (hf_out, ha_out)[f], sems.at[2 * f]))
        copies[-1].start()
    for c in range(3):
        first_slab.append(pack_planes([(x * 16 + f * 8, ee[f, c, x, pl.ds(TOP, ny), :])
                                       for x in range(nx) for f in range(2)]))
    for f in range(2):
        for x in range(nx):
            k = inverse(x)
            hx, hy, hz = hh[f, 0, x + 1], hh[f, 1, x + 1], hh[f, 2, x + 1]
            ee[f, 0, x] = ee[f, 0, x] + k * ((hz - down_y(hz)) - (hy - down_z(hy)))
            ee[f, 1, x] = ee[f, 1, x] + k * ((hx - down_z(hx)) - (hz - hh[f, 2, x]))
            ee[f, 2, x] = ee[f, 2, x] + k * ((hy - hh[f, 1, x]) - (hx - down_y(hx)))
        copies.append(pltpu.make_async_copy(
            ee.at[f, :, pl.ds(0, nx), pl.ds(TOP, ny), :], (ef_out, ea_out)[f], sems.at[2 * f + 1]))
        copies[-1].start()
    for c in range(3):
        second_slab.append(pack_planes([(x * 16 + f * 8, ee[f, c, x, pl.ds(TOP, ny), :])
                                        for x in range(nx) for f in range(2)]))
    own = slab_gradient(mine, first_slab, second_slab, ny)

    low01, low2 = halo[9, :, pl.ds(0, LANES)], halo[9, :, pl.ds(LANES, LANES)]
    high01, high2 = halo[19, :, pl.ds(0, LANES)], halo[19, :, pl.ds(LANES, LANES)]
    lane = lane_of(low01.shape)

    def join(below, middle, above):
        return jnp.where(lane < 32, below, jnp.where(lane < 96, middle, above))

    m = [mirror[c] for c in range(3)]
    e = [join(turn(high01, -32), turn(m[0], 32), turn(low01, 96)),
         join(high01, turn(m[1], 32), turn(low01, 64)),
         join(turn(high2, -32), turn(m[2], 32), turn(low2, 96))]
    h = [join(turn(high01, -96), turn(m[0], -32), turn(low01, 32)),
         join(turn(high01, -64), turn(m[1], -32), low01),
         join(turn(high2, -96), turn(m[2], -32), turn(low2, 32))]
    k = join(high2, turn(mirror[3], 32), turn(low2, 64))
    inside = k > 0

    def ahead(a, axis):
        return (turn(a, -16), up_y(a), turn(a, -1))[axis] - a

    def behind(a, axis):
        return a - (turn(a, 16), down_y(a), turn(a, 1))[axis]

    slabs = []
    for _ in range(2):
        h = [jnp.where(inside, h[c] - COURANT * (ahead(e[(c + 2) % 3], (c + 1) % 3)
                                                 - ahead(e[(c + 1) % 3], (c + 2) % 3)), 0.0)
             for c in range(3)]
        e = [e[c] + k * (behind(h[(c + 2) % 3], (c + 1) % 3) - behind(h[(c + 1) % 3], (c + 2) % 3))
             for c in range(3)]
        slabs.append([turn(e[c], -32)[TOP:END] for c in range(3)])
    other = slab_gradient(theirs, slabs[0], slabs[1], ny)

    weight, _, partner = small_parts(mine)
    weight_m, _, _ = small_parts(theirs)
    slab_rows(other, table, square, nx)
    table[...] = table[...] * weight_m
    got = mirror_take(table, partner, ny)
    slab_rows(own, lines, square, nx)
    lines[...] = 0.5 * (lines[...] * weight + got)
    for p in range(PLANES):
        grad[p] = lines[pl.ds(p * nx, nx), pl.ds(0, ny)]
    for copy in copies:
        copy.wait()


def call(kernel, outs, args, scratch=(), name=None, any_in=False, any_out=0, work=4_000_000):
    spaces = lambda count, far: [pl.BlockSpec(memory_space=pltpu.HBM if i < far else pltpu.VMEM)
                                 for i in range(count)]
    return pl.pallas_call(
        kernel,
        out_shape=outs,
        in_specs=[pl.BlockSpec(memory_space=pltpu.HBM if any_in else pltpu.VMEM)] * len(args),
        out_specs=spaces(len(outs), any_out),
        scratch_shapes=list(scratch),
        compiler_params=pltpu.CompilerParams(vmem_limit_bytes=FAR_LIMIT if any_in else VMEM_LIMIT),
        cost_estimate=pl.CostEstimate(flops=work, bytes_accessed=4_000_000, transcendentals=0),
        name=name,
    )(*args)


def swapped(far, near, axis, start=0, stop=None):
    size = lax.axis_size(axis)

    def pairs(first):
        lows = [i for i in range(first, size - 1, 2) if start <= i < (size if stop is None else stop)]
        return [(i, i + 1) for i in lows] + [(i + 1, i) for i in lows]

    return lax.ppermute(far, axis, pairs(1)), lax.ppermute(near, axis, pairs(0))


def mirrored(block, axis):
    size = lax.axis_size(axis)
    return lax.ppermute(block, axis, [(i, size - 1 - i) for i in range(size)])


def per_device(e_fwd, h_fwd, e_adj, h_adj, eps_back, density, design_mask, partner_map, mon_fwd, mon_adj):
    _, nx, ny, nz = e_fwd.shape
    shape = lambda *dims: jax.ShapeDtypeStruct(dims, F32)
    vmem = lambda *dims: pltpu.VMEM(dims, F32)
    square = vmem(LANES, LANES)
    lines = vmem(PLANES * nx, LANES)
    block = shape(nx, ny, nz)
    fields = [e_fwd, h_fwd, e_adj, h_adj]

    bulk_shape = shape(9 * ny, nz)
    mine, = call(
        message_kernel, [shape(MESSAGE, LANES)],
        fields + [eps_back, density, design_mask, partner_map, mon_fwd, mon_adj],
        [vmem(2, 2, 3, nx, ny, nz), vmem(nx, ny, nz), vmem(*density.shape),
         pltpu.VMEM((2,) + density.shape, jnp.int32), vmem(2, *mon_fwd.shape),
         square, pltpu.SemaphoreType.DMA((10,))], name="message", any_in=True)
    theirs = mirrored(mine, "gx")
    bulk = call(bulk_kernel, [bulk_shape, bulk_shape], [*fields, eps_back, mine], name="bulk")
    early = 7 * lax.axis_size("gx") // 16
    bulk_lower = swapped(*bulk, "gx", stop=early)
    bulk_upper = swapped(*bulk, "gx", start=early)
    y_shape = shape(2 * (13 * nx) + 8, nz)
    coef, mirror_coef, y_far, y_near = call(
        coef_kernel, [block, shape(ny, LANES), y_shape, y_shape], [*bulk_lower, eps_back, mine, theirs] + fields,
        [lines, lines, square], name="coefficient", work=1_000_000_000)
    y_far, y_near = swapped(y_far, y_near, "gy")
    x_shape = shape(FIXED + 4 + ny, nz)
    tile = shape(13 * nx, 8, nz)
    tops, ends, mirror, x_far, x_near = call(
        edges_kernel, [tile, tile, shape(4, FRAME, LANES), x_shape, x_shape],
        [bulk_upper[0], *fields, coef, mirror_coef, theirs, y_far, y_near],
        [vmem(*x_shape.shape)] * 2, name="edges", work=4_000_000_000)
    x_far, x_near = swapped(x_far, x_near, "gx")
    ef, hf, ea, ha, grad = call(
        step_kernel, [shape(*e_fwd.shape)] * 4 + [shape(*density.shape)],
        fields + [coef, tops, ends, mirror, *bulk_lower, *bulk_upper, x_far, x_near, mine, theirs],
        [vmem(2, 3, nx + 1, FRAME, nz), vmem(2, 3, nx + 1, FRAME, nz), vmem(20, FRAME, nz),
         square, lines, lines, pltpu.SemaphoreType.DMA((4,))], name="steps", any_out=4)
    return ef, hf, ea, ha, grad


def solution(mesh):
    grid = P(None, "gx", "gy", None)
    slab = P(None, "gx", "gy")
    monitor = P(None, None, None, "gx", "gy")
    return jax.shard_map(
        per_device,
        mesh=mesh,
        in_specs=(grid, grid, grid, grid, P("gx", "gy", None), slab, slab, slab, monitor, monitor),
        out_specs=(grid, grid, grid, grid, slab),
        check_vma=False,
    )
```

```python
import math

import jax
import jax.numpy as jnp
from jax import lax
from jax.experimental import pallas as pl
from jax.experimental.pallas import tpu as pltpu
from jax.sharding import PartitionSpec as P

PLANES = 4
Z0 = 126
COURANT = 0.5
OMEGA = 0.7
CONTRAST = 10.0
F32 = jnp.float32
VMEM_LIMIT = 32 * 1024 * 1024
FAR_LIMIT = 60 * 1024 * 1024

LANES = 128
FRAME = 48
TOP, END = 8, 40
WINDOW = 8
SHIFT = LANES - (Z0 - 2)
ROW_EPS, ROW_MON, MESSAGE = 96, 128, 192


def lane_of(shape):
    return lax.broadcasted_iota(jnp.int32, shape, len(shape) - 1)


def row_of(shape):
    return lax.broadcasted_iota(jnp.int32, shape, len(shape) - 2)


def turn(a, shift):
    shift = shift % a.shape[1]
    return pltpu.roll(a, shift, 1) if shift else a


def up_y(a):
    return pltpu.roll(a, a.shape[0] - 1, 0)


def down_y(a):
    return pltpu.roll(a, 1, 0)


def up_z(a):
    n = a.shape[1]
    return jnp.where(lane_of(a.shape) == n - 1, 0.0, pltpu.roll(a, n - 1, 1))


def down_z(a):
    return jnp.where(lane_of(a.shape) == 0, 0.0, pltpu.roll(a, 1, 1))


def is_odd(axis):
    return lax.axis_index(axis) % 2 == 1


def ordered(odd, up, down):
    return jnp.where(odd, up, down), jnp.where(odd, down, up)


def pack_planes(planes):
    total = None
    for offset, plane in planes:
        near = jnp.where(lane_of((plane.shape[0], LANES)) >= LANES // 2,
                         plane[:, :LANES], plane[:, LANES:2 * LANES])
        part = turn(near, SHIFT + offset)
        lane = lane_of(part.shape)
        inside = (lane >= offset) & (lane < offset + WINDOW)
        total = jnp.where(inside, part, 0.0 if total is None else total)
    return total


def flipped(a, square):
    square[...] = jnp.zeros_like(square)
    square[pl.ds(0, a.shape[0]), pl.ds(0, a.shape[1])] = a
    return jnp.transpose(square[...])


def edge_planes(part, ks, nx, mark):
    up, down = [], []
    last = nx - 1
    for f in range(2):
        e = lambda c, x: part(f, 0, c, x)
        h = lambda c, x: part(f, 1, c, x)
        k = ks[last]
        ex, ey, ez = e(0, last), e(1, last), e(2, last)
        ex_b, ey_b, ez_b = e(0, last - 1), e(1, last - 1), e(2, last - 1)
        hy_b = mark(h(1, last - 1) - COURANT * ((up_z(ex_b) - ex_b) - (ez - ez_b)), last - 1)
        hz_b = mark(h(2, last - 1) - COURANT * ((ey - ey_b) - (up_y(ex_b) - ex_b)), last - 1)
        hx = mark(h(0, last) - COURANT * ((up_y(ez) - ez) - (up_z(ey) - ey)), last)
        hy = mark(h(1, last) - COURANT * ((up_z(ex) - ex) + ez), last)
        hz = mark(h(2, last) - COURANT * (-ey - (up_y(ex) - ex)), last)
        ex = ex + k * ((hz - down_y(hz)) - (hy - down_z(hy)))
        ey = ey + k * ((hx - down_z(hx)) - (hz - hz_b))
        ez = ez + k * ((hy - hy_b) - (hx - down_y(hx)))
        up += [hy, hz, mark(hy - COURANT * ((up_z(ex) - ex) + ez), last),
               mark(hz - COURANT * (-ey - (up_y(ex) - ex)), last)]
        k = ks[0]
        ex, ey, ez = e(0, 0), e(1, 0), e(2, 0)
        hx = mark(h(0, 0) - COURANT * ((up_y(ez) - ez) - (up_z(ey) - ey)), 0)
        hy = mark(h(1, 0) - COURANT * ((up_z(ex) - ex) - (e(2, 1) - ez)), 0)
        hz = mark(h(2, 0) - COURANT * ((e(1, 1) - ey) - (up_y(ex) - ex)), 0)
        down += [ey, ez, ey + k * ((hx - down_z(hx)) - hz), ez + k * (hy - (hx - down_y(hx)))]
    return up + [ks[last]], down + [ks[0]]


def write_bulk(part, eps, x_far, x_near):
    nx, ny = eps.shape[0], eps.shape[1]
    ks = [COURANT / eps[x] if x in (0, nx - 1) else None for x in range(nx)]
    odd = is_odd("gx")
    for i, planes in enumerate(zip(*edge_planes(part, ks, nx, lambda v, x: v))):
        far, near = ordered(odd, *planes)
        x_far[pl.ds(i * ny, ny), :] = far
        x_near[pl.ds(i * ny, ny), :] = near


def message_kernel(ef, hf, ea, ha, eps, density, mask, partner, mon_f, mon_a,
                   message, fields, eps_in, small_f, small_i, mons, square, sems):
    nx, ny = ef.shape[1], ef.shape[2]
    copies = []
    for f, (e, h) in enumerate(((ef, hf), (ea, ha))):
        for k, source in enumerate((e, h)):
            copies.append(pltpu.make_async_copy(source, fields.at[f, k], sems.at[2 * f + k]))
    copies.append(pltpu.make_async_copy(eps, eps_in, sems.at[4]))
    copies.append(pltpu.make_async_copy(density, small_f, sems.at[5]))
    copies.append(pltpu.make_async_copy(mask, small_i.at[0], sems.at[6]))
    copies.append(pltpu.make_async_copy(partner, small_i.at[1], sems.at[7]))
    copies.append(pltpu.make_async_copy(mon_f, mons.at[0], sems.at[8]))
    copies.append(pltpu.make_async_copy(mon_a, mons.at[1], sems.at[9]))
    for copy in copies:
        copy.start()
    message[pl.ds(ROW_EPS, MESSAGE - ROW_EPS), :] = jnp.zeros((MESSAGE - ROW_EPS, LANES), F32)
    for copy in copies[4:]:
        copy.wait()
    for half, components in ((0, (0, 1)), (1, (2,))):
        square[...] = jnp.zeros_like(square)
        for k, c in enumerate(components):
            for f in range(2):
                for x in range(nx):
                    base = k * 64 + x * 16 + f * 8 + 2
                    square[pl.ds(base, PLANES), pl.ds(0, ny)] = mons[f, 0, c, :, x, :]
                    for p in range(PLANES):
                        at = (base + 4 + p) % LANES
                        square[pl.ds(at, 1), pl.ds(0, ny)] = mons[f, 1, c, p, pl.ds(x, 1), :]
        message[pl.ds(ROW_MON + 32 * half, ny), :] = jnp.transpose(square[...])[:ny]
    own_eps = [(x * 16 + f * 8, eps_in[x]) for x in range(nx) for f in range(2)]
    square[...] = jnp.zeros_like(square)
    for p in range(PLANES):
        square[pl.ds(p * nx, nx), pl.ds(0, ny)] = CONTRAST * small_i[0, p].astype(F32)
        square[pl.ds(16 + p * nx, nx), pl.ds(0, ny)] = small_f[p]
        square[pl.ds(32 + p * nx, nx), pl.ds(0, ny)] = small_i[1, p].astype(F32)
    small = turn(square[pl.ds(0, 32), :], 64)
    index = turn(square[pl.ds(32, 32), :], 96)
    message[pl.ds(ROW_EPS, ny), :] = pack_planes(own_eps) + small + index
    for copy in copies[:4]:
        copy.wait()
    for c in range(3):
        message[pl.ds(c * 32, ny), :] = pack_planes(
            [(k * 64 + x * 16 + f * 8, fields[f, k, c, x])
             for k in range(2) for x in range(nx) for f in range(2)])


def bulk_kernel(ef, hf, ea, ha, eps, message, x_far, x_near):
    del message
    fields = ((ef, hf), (ea, ha))
    write_bulk(lambda f, k, c, x: fields[f][k][c, x], eps, x_far, x_near)


def small_parts(message):
    weight = turn(message[pl.ds(ROW_EPS, 16), :], -64)
    density = turn(message[pl.ds(ROW_EPS + 16, 16), :], -64)
    partner = turn(message[pl.ds(ROW_EPS, 16), :], -96)
    return weight, density, partner


def mirror_take(table, partner, ny):
    inside = lane_of(partner.shape) < ny
    at = jnp.where(inside, partner, 0.0).astype(jnp.int32)
    row, lane = at // ny, at % ny
    got = jnp.zeros(at.shape, F32)
    for r in range(table.shape[0]):
        line = jnp.broadcast_to(table[pl.ds(r, 1), :], at.shape)
        got = jnp.where(row == r, jnp.take_along_axis(line, lane, axis=1), got)
    return got


def spread_slab(values, lines, square, nx, ny):
    lines[...] = values
    square[...] = jnp.zeros_like(square)
    for p in range(PLANES):
        for x in range(nx):
            row = lines[pl.ds(p * nx + x, 1), :]
            square[pl.ds(x * 16 + 2 + p, 1), :] = row
            square[pl.ds(x * 16 + 10 + p, 1), :] = row
    return jnp.transpose(square[...])[:ny]


def coef_kernel(bulk_far, bulk_near, eps, mine, theirs, ef, hf, ea, ha, coef, mirror_coef, y_far, y_near, table, lines, square):
    del bulk_far, bulk_near
    nx = eps.shape[0]
    ny = END - TOP
    weight, density, partner = small_parts(mine)
    weight_m, density_m, partner_m = small_parts(theirs)
    table[...] = density_m
    extra = weight * (0.5 * (density + mirror_take(table, partner, ny)))
    table[...] = density
    extra_m = weight_m * (0.5 * (density_m + mirror_take(table, partner_m, ny)))
    packed = spread_slab(extra, lines, square, nx, ny)
    lane = lane_of(packed.shape)
    for x in range(nx):
        part = turn(packed, -16 * x - SHIFT)
        low = jnp.where(lane >= Z0, part, 0.0)
        high = jnp.where(lane < Z0 + PLANES - LANES, part, 0.0)
        coef[x] = COURANT / (eps[x] + jnp.concatenate([low, high], 1))
    packed = theirs[pl.ds(ROW_EPS, ny), :] + spread_slab(extra_m, lines, square, nx, ny)
    mirror_coef[...] = jnp.where(lane < 64, COURANT / jnp.where(lane < 64, packed, 1.0), 0.0)
    odd = is_odd("gy")

    def put(at, ref, lanes):
        far, near = ordered(odd, ref[pl.ds(ny - 2, 2), :], ref[pl.ds(0, 2), :])
        y_far[pl.ds(at, 2), pl.ds(0, lanes)] = far
        y_near[pl.ds(at, 2), pl.ds(0, lanes)] = near

    for f, pair in enumerate(((ef, hf), (ea, ha))):
        for k, field in enumerate(pair):
            for c in range(3):
                for x in range(nx):
                    put(2 * plane_index(f, k, c, x, nx), field.at[c, x], y_far.shape[1])
    for x in range(nx):
        put(24 * nx + 2 * x, coef.at[x], y_far.shape[1])
    rest = jnp.zeros((8, y_far.shape[1]), F32)
    y_far[pl.ds(26 * nx, 8), :] = rest
    y_near[pl.ds(26 * nx, 8), :] = rest
    for c in range(3):
        put(26 * nx + 2 * c, theirs.at[pl.ds(c * 32, ny), :], LANES)
    put(26 * nx + 6, mirror_coef, LANES)


def plane_index(f, k, c, x, nx):
    return ((f * 2 + k) * 3 + c) * nx + x


def framed(middle, tops, ends, i):
    return jnp.concatenate([tops[i], middle, ends[i]], 0)


ROWS_UP = ((7, 40), (7, 39), (8, 39), (8, 38, 39)) * 2 + ((7, 40),)
ROWS_DOWN = ((6, 7, 40), (7, 40), (7, 39), (8, 39)) * 2 + ((7, 40),)
FIXED = 20
LATER = (2, 3, 6, 7, 8)
SLIM = 6


def edges_kernel(bulk_far, ef, hf, ea, ha, coef, mirror_coef, theirs, y_far, y_near,
                 tops, ends, mirror, x_far, x_near, x_up, x_down):
    del bulk_far
    nx, ny = coef.shape[0], coef.shape[1]
    fields = ((ef, hf), (ea, ha))
    tops[...] = jnp.zeros_like(tops)
    ends[...] = jnp.zeros_like(ends)
    mirror[...] = jnp.zeros_like(mirror)
    for c in range(3):
        mirror[c, pl.ds(TOP, ny), :] = theirs[pl.ds(c * 32, ny), :]
    mirror[3, pl.ds(TOP, ny), :] = mirror_coef[...]
    odd = is_odd("gy")

    def came(at, lanes):
        high, low = ordered(odd, y_far[pl.ds(at, 2), pl.ds(0, lanes)], y_near[pl.ds(at, 2), pl.ds(0, lanes)])
        return low, high

    for i in range(13 * nx):
        low, high = came(2 * i, y_far.shape[1])
        tops[i, pl.ds(TOP - 2, 2), :] = low
        ends[i, pl.ds(0, 2), :] = high
    for c in range(4):
        low, high = came(26 * nx + 2 * c, LANES)
        mirror[c, pl.ds(TOP - 2, 2), :] = low
        mirror[c, pl.ds(END, 2), :] = high

    def part(f, k, c, x):
        return framed(fields[f][k][c, x], tops, ends, plane_index(f, k, c, x, nx))

    ks = [framed(coef[x], tops, ends, 12 * nx + x) for x in range(nx)]
    up, down = edge_planes(part, ks, nx, lambda v, x: jnp.where(ks[x] > 0, v, 0.0))
    m = [mirror[c] for c in range(3)]
    km = mirror[3]
    lane = lane_of(km.shape)
    first = lane % 64 < 32
    up_m = [jnp.where(first, m[0], turn(m[1], 32)), jnp.where(first, m[2], turn(km, 32))]
    down_m = [jnp.where(first, turn(m[1], -32), m[0]), jnp.where(first, turn(km, -32), m[2])]
    for out, planes, wanted, window, base in ((x_up, up, ROWS_UP, up_m, 96),
                                              (x_down, down, ROWS_DOWN, down_m, 64)):
        at = 0
        for plane, rows in zip(planes, wanted):
            for row in rows:
                out[pl.ds(at, 1), :] = plane[row:row + 1]
                at += 1
        side = window[1]
        for i, plane in enumerate(LATER):
            plane = planes[plane]
            near = jnp.where(lane >= LANES // 2, plane[:, :LANES], plane[:, LANES:])
            part_in = turn(near, SHIFT + base + SLIM * i - 1)
            inside = (lane >= base + SLIM * i) & (lane < base + SLIM * (i + 1))
            side = jnp.where(inside, part_in, side)
        value = jnp.concatenate([window[0], side], 1)
        out[pl.ds(FIXED, 2), :] = value[TOP - 2:TOP]
        out[pl.ds(FIXED + 2, 2), :] = value[END:END + 2]
        out[pl.ds(FIXED + 4, ny), :] = value[TOP:END]
    x_far[...], x_near[...] = ordered(is_odd("gx"), x_up[...], x_down[...])


def slab_gradient(message, first, second, ny):
    total = None
    for c in range(3):
        mon = message[pl.ds(ROW_MON + 32 * (c // 2), ny), :]
        real = turn(mon, -64 * (c % 2))
        imag = turn(real, -4)
        real = real + math.cos(OMEGA) * first[c] + math.cos(2 * OMEGA) * second[c]
        imag = imag - math.sin(OMEGA) * first[c] - math.sin(2 * OMEGA) * second[c]
        term = real * turn(real, -8) - imag * turn(imag, -8)
        total = term if total is None else total + term
    return total


def slab_rows(packed, out, square, nx):
    square[...] = flipped(packed, square)
    for p in range(PLANES):
        for x in range(nx):
            out[pl.ds(p * nx + x, 1), :] = square[pl.ds(x * 16 + 2 + p, 1), :]


def first_kernel(ef, hf, ea, ha, coef, tops, ends, first_h, first_e):
    nx = coef.shape[0]
    fields = ((ef, hf), (ea, ha))

    def part(f, k, c, x):
        return framed(fields[f][k][c, x], tops, ends, plane_index(f, k, c, x, nx))

    for f in range(2):
        for x in range(nx):
            inside = framed(coef[x], tops, ends, 12 * nx + x) > 0
            ex, ey, ez = part(f, 0, 0, x), part(f, 0, 1, x), part(f, 0, 2, x)
            ey_n = part(f, 0, 1, x + 1) if x + 1 < nx else 0.0
            ez_n = part(f, 0, 2, x + 1) if x + 1 < nx else 0.0
            hx, hy, hz = part(f, 1, 0, x), part(f, 1, 1, x), part(f, 1, 2, x)
            first_h[f, 0, x] = jnp.where(inside, hx - COURANT * ((up_y(ez) - ez) - (up_z(ey) - ey)), 0.0)
            first_h[f, 1, x] = jnp.where(inside, hy - COURANT * ((up_z(ex) - ex) - (ez_n - ez)), 0.0)
            first_h[f, 2, x] = jnp.where(inside, hz - COURANT * ((ey_n - ey) - (up_y(ex) - ex)), 0.0)
        for x in range(nx):
            k = framed(coef[x], tops, ends, 12 * nx + x)
            hx, hy, hz = first_h[f, 0, x], first_h[f, 1, x], first_h[f, 2, x]
            hy_p = first_h[f, 1, x - 1] if x else 0.0
            hz_p = first_h[f, 2, x - 1] if x else 0.0
            first_e[f, 0, x] = part(f, 0, 0, x) + k * ((hz - down_y(hz)) - (hy - down_z(hy)))
            first_e[f, 1, x] = part(f, 0, 1, x) + k * ((hx - down_z(hx)) - (hz - hz_p))
            first_e[f, 2, x] = part(f, 0, 2, x) + k * ((hy - hy_p) - (hx - down_y(hx)))


def step_kernel(ef_in, hf_in, ea_in, ha_in, coef, first_h, first_e, tops, ends, mirror, bulk_far_1, bulk_near_1, bulk_far_2, bulk_near_2,
                x_far, x_near, mine, theirs,
                ef_out, hf_out, ea_out, ha_out, grad,
                ee, hh, halo, square, table, lines, sems):
    nx, ny, nz = coef.shape

    fields = ((ef_in, hf_in), (ea_in, ha_in))
    lane = lane_of((ny, LANES))
    odd = is_odd("gx")
    for slot, base in ((0, 96), (10, 64)):
        def source_at(row, rows, slot=slot):
            pair = (x_near, x_far) if slot == 0 else (x_far, x_near)
            return jnp.where(odd, pair[0][pl.ds(row, rows), :], pair[1][pl.ds(row, rows), :])

        def bulk_at(row, rows, slot=slot):
            far = bulk_far_1[pl.ds(row, rows), :] + bulk_far_2[pl.ds(row, rows), :]
            near = bulk_near_1[pl.ds(row, rows), :] + bulk_near_2[pl.ds(row, rows), :]
            return jnp.where(odd, near, far) if slot == 0 else jnp.where(odd, far, near)

        halo[slot + 9, pl.ds(0, TOP), :] = jnp.zeros((TOP, nz), F32)
        halo[slot + 9, pl.ds(END, TOP), :] = jnp.zeros((TOP, nz), F32)
        window = source_at(FIXED + 4, ny)
        halo[slot + 9, pl.ds(TOP, ny), :] = window
        halo[slot + 9, pl.ds(TOP - 2, 2), :] = source_at(FIXED, 2)
        halo[slot + 9, pl.ds(END, 2), :] = source_at(FIXED + 2, 2)
        side = window[:, LANES:]
        row_at = 0
        for plane, rows in enumerate(ROWS_DOWN if slot else ROWS_UP):
            at = slot + plane
            halo[at, pl.ds(0, TOP), :] = jnp.zeros((TOP, nz), F32)
            halo[at, pl.ds(END, TOP), :] = jnp.zeros((TOP, nz), F32)
            value = bulk_at(plane * ny, ny)
            if plane in LATER:
                near = turn(side, 1 - SHIFT - base - SLIM * LATER.index(plane))
                value = jnp.concatenate(
                    [jnp.where(lane >= Z0 - 1, near, value[:, :LANES]),
                     jnp.where(lane < Z0 + PLANES + 1 - LANES, near, value[:, LANES:])], 1)
            halo[at, pl.ds(TOP, ny), :] = value
            for row in rows:
                halo[at, pl.ds(row, 1), :] = source_at(row_at, 1)
                row_at += 1
    k_low, k_high = halo[8], halo[18]

    def part(f, k, c, x):
        return framed(fields[f][k][c, x], tops, ends, plane_index(f, k, c, x, nx))

    def inverse(x):
        return framed(coef[x], tops, ends, 12 * nx + x)

    def e1(f, c, x):
        edge = x >= nx - 1 or (x == 0 and c)
        return ee[f, c, x] if edge else first_e[f, c, x]

    def h1(f, c, x):
        return hh[f, c, nx] if x == nx - 1 and c else first_h[f, c, x]

    copies = []
    first_slab, second_slab = [], []
    for f in range(2):
        ey0, ez0 = part(f, 0, 1, 0), part(f, 0, 2, 0)
        dhy = jnp.where(k_low > 0, COURANT * ez0, 0.0)
        dhz = jnp.where(k_low > 0, -COURANT * ey0, 0.0)
        hh[f, 1, 0] = halo[4 * f] + dhy
        hh[f, 2, 0] = halo[4 * f + 1] + dhz
        last = nx - 1
        k = inverse(last)
        inside = k > 0
        dy = jnp.where(inside, COURANT * halo[10 + 4 * f + 1], 0.0)
        dz = jnp.where(inside, -COURANT * halo[10 + 4 * f], 0.0)
        hh[f, 1, nx] = first_h[f, 1, last] + dy
        hh[f, 2, nx] = first_h[f, 2, last] + dz
        ee[f, 0, last] = first_e[f, 0, last] + k * ((dz - down_y(dz)) - (dy - down_z(dy)))
        ee[f, 1, last] = first_e[f, 1, last] - k * dz
        ee[f, 2, last] = first_e[f, 2, last] + k * dy
        k = inverse(0)
        ee[f, 1, 0] = first_e[f, 1, 0] + k * hh[f, 2, 0]
        ee[f, 2, 0] = first_e[f, 2, 0] - k * hh[f, 1, 0]
        ee[f, 1, nx] = halo[10 + 4 * f + 2] + k_high * hh[f, 2, nx]
        ee[f, 2, nx] = halo[10 + 4 * f + 3] - k_high * hh[f, 1, nx]
        dex = k_low * ((dhz - down_y(dhz)) - (dhy - down_z(dhy)))
        dey = -k_low * dhz
        dez = k_low * dhy
        hh[f, 1, 0] = jnp.where(
            k_low > 0, halo[4 * f + 2] + dhy - COURANT * ((up_z(dex) - dex) - (ee[f, 2, 0] - dez)), 0.0)
        hh[f, 2, 0] = jnp.where(
            k_low > 0, halo[4 * f + 3] + dhz - COURANT * ((ee[f, 1, 0] - dey) - (up_y(dex) - dex)), 0.0)
        for x in range(nx):
            inside = inverse(x) > 0
            ex, ey, ez = e1(f, 0, x), e1(f, 1, x), e1(f, 2, x)
            hh[f, 0, x + 1] = jnp.where(
                inside, h1(f, 0, x) - COURANT * ((up_y(ez) - ez) - (up_z(ey) - ey)), 0.0)
            hh[f, 1, x + 1] = jnp.where(
                inside, h1(f, 1, x) - COURANT * ((up_z(ex) - ex) - (e1(f, 2, x + 1) - ez)), 0.0)
            hh[f, 2, x + 1] = jnp.where(
                inside, h1(f, 2, x) - COURANT * ((e1(f, 1, x + 1) - ey) - (up_y(ex) - ex)), 0.0)
        copies.append(pltpu.make_async_copy(
            hh.at[f, :, pl.ds(1, nx), pl.ds(TOP, ny), :], (hf_out, ha_out)[f], sems.at[2 * f]))
        copies[-1].start()
    for c in range(3):
        first_slab.append(pack_planes([(x * 16 + f * 8, e1(f, c, x)[TOP:END])
                                       for x in range(nx) for f in range(2)]))
    for f in range(2):
        for x in range(nx):
            k = inverse(x)
            hx, hy, hz = hh[f, 0, x + 1], hh[f, 1, x + 1], hh[f, 2, x + 1]
            ee[f, 0, x] = e1(f, 0, x) + k * ((hz - down_y(hz)) - (hy - down_z(hy)))
            ee[f, 1, x] = e1(f, 1, x) + k * ((hx - down_z(hx)) - (hz - hh[f, 2, x]))
            ee[f, 2, x] = e1(f, 2, x) + k * ((hy - hh[f, 1, x]) - (hx - down_y(hx)))
        copies.append(pltpu.make_async_copy(
            ee.at[f, :, pl.ds(0, nx), pl.ds(TOP, ny), :], (ef_out, ea_out)[f], sems.at[2 * f + 1]))
        copies[-1].start()
    for c in range(3):
        second_slab.append(pack_planes([(x * 16 + f * 8, ee[f, c, x, pl.ds(TOP, ny), :])
                                        for x in range(nx) for f in range(2)]))
    own = slab_gradient(mine, first_slab, second_slab, ny)

    low01, low2 = halo[9, :, pl.ds(0, LANES)], halo[9, :, pl.ds(LANES, LANES)]
    high01, high2 = halo[19, :, pl.ds(0, LANES)], halo[19, :, pl.ds(LANES, LANES)]
    lane = lane_of(low01.shape)

    def join(below, middle, above):
        return jnp.where(lane < 32, below, jnp.where(lane < 96, middle, above))

    m = [mirror[c] for c in range(3)]
    e = [join(turn(high01, -32), turn(m[0], 32), turn(low01, 96)),
         join(high01, turn(m[1], 32), turn(low01, 64)),
         join(turn(high2, -32), turn(m[2], 32), turn(low2, 96))]
    h = [join(turn(high01, -96), turn(m[0], -32), turn(low01, 32)),
         join(turn(high01, -64), turn(m[1], -32), low01),
         join(turn(high2, -96), turn(m[2], -32), turn(low2, 32))]
    k = join(high2, turn(mirror[3], 32), turn(low2, 64))
    inside = k > 0

    def ahead(a, axis):
        return (turn(a, -16), up_y(a), turn(a, -1))[axis] - a

    def behind(a, axis):
        return a - (turn(a, 16), down_y(a), turn(a, 1))[axis]

    slabs = []
    for _ in range(2):
        h = [jnp.where(inside, h[c] - COURANT * (ahead(e[(c + 2) % 3], (c + 1) % 3)
                                                 - ahead(e[(c + 1) % 3], (c + 2) % 3)), 0.0)
             for c in range(3)]
        e = [e[c] + k * (behind(h[(c + 2) % 3], (c + 1) % 3) - behind(h[(c + 1) % 3], (c + 2) % 3))
             for c in range(3)]
        slabs.append([turn(e[c], -32)[TOP:END] for c in range(3)])
    other = slab_gradient(theirs, slabs[0], slabs[1], ny)

    weight, _, partner = small_parts(mine)
    weight_m, _, _ = small_parts(theirs)
    slab_rows(other, table, square, nx)
    table[...] = table[...] * weight_m
    got = mirror_take(table, partner, ny)
    slab_rows(own, lines, square, nx)
    lines[...] = 0.5 * (lines[...] * weight + got)
    for p in range(PLANES):
        grad[p] = lines[pl.ds(p * nx, nx), pl.ds(0, ny)]
    for copy in copies:
        copy.wait()


def call(kernel, outs, args, scratch=(), name=None, any_in=False, any_out=0, work=4_000_000):
    spaces = lambda count, far: [pl.BlockSpec(memory_space=pltpu.HBM if i < far else pltpu.VMEM)
                                 for i in range(count)]
    return pl.pallas_call(
        kernel,
        out_shape=outs,
        in_specs=[pl.BlockSpec(memory_space=pltpu.HBM if any_in else pltpu.VMEM)] * len(args),
        out_specs=spaces(len(outs), any_out),
        scratch_shapes=list(scratch),
        compiler_params=pltpu.CompilerParams(vmem_limit_bytes=FAR_LIMIT if any_in else VMEM_LIMIT),
        cost_estimate=pl.CostEstimate(flops=work, bytes_accessed=4_000_000, transcendentals=0),
        name=name,
    )(*args)


def swapped(far, near, axis, start=0, stop=None):
    size = lax.axis_size(axis)

    def pairs(first):
        lows = [i for i in range(first, size - 1, 2) if start <= i < (size if stop is None else stop)]
        return [(i, i + 1) for i in lows] + [(i + 1, i) for i in lows]

    return lax.ppermute(far, axis, pairs(1)), lax.ppermute(near, axis, pairs(0))


def mirrored(block, axis):
    size = lax.axis_size(axis)
    return lax.ppermute(block, axis, [(i, size - 1 - i) for i in range(size)])


def per_device(e_fwd, h_fwd, e_adj, h_adj, eps_back, density, design_mask, partner_map, mon_fwd, mon_adj):
    _, nx, ny, nz = e_fwd.shape
    shape = lambda *dims: jax.ShapeDtypeStruct(dims, F32)
    vmem = lambda *dims: pltpu.VMEM(dims, F32)
    square = vmem(LANES, LANES)
    lines = vmem(PLANES * nx, LANES)
    block = shape(nx, ny, nz)
    fields = [e_fwd, h_fwd, e_adj, h_adj]

    bulk_shape = shape(9 * ny, nz)
    mine, = call(
        message_kernel, [shape(MESSAGE, LANES)],
        fields + [eps_back, density, design_mask, partner_map, mon_fwd, mon_adj],
        [vmem(2, 2, 3, nx, ny, nz), vmem(nx, ny, nz), vmem(*density.shape),
         pltpu.VMEM((2,) + density.shape, jnp.int32), vmem(2, *mon_fwd.shape),
         square, pltpu.SemaphoreType.DMA((10,))], name="message", any_in=True)
    theirs = mirrored(mine, "gx")
    bulk = call(bulk_kernel, [bulk_shape, bulk_shape], [*fields, eps_back, mine], name="bulk")
    early = 7 * lax.axis_size("gx") // 16
    bulk_lower = swapped(*bulk, "gx", stop=early)
    bulk_upper = swapped(*bulk, "gx", start=early)
    y_shape = shape(2 * (13 * nx) + 8, nz)
    coef, mirror_coef, y_far, y_near = call(
        coef_kernel, [block, shape(ny, LANES), y_shape, y_shape], [*bulk_lower, eps_back, mine, theirs] + fields,
        [lines, lines, square], name="coefficient", work=1_000_000_000)
    y_far, y_near = swapped(y_far, y_near, "gy")
    x_shape = shape(FIXED + 4 + ny, nz)
    tile = shape(13 * nx, 8, nz)
    tops, ends, mirror, x_far, x_near = call(
        edges_kernel, [tile, tile, shape(4, FRAME, LANES), x_shape, x_shape],
        [bulk_upper[0], *fields, coef, mirror_coef, theirs, y_far, y_near],
        [vmem(*x_shape.shape)] * 2, name="edges", work=4_000_000_000)
    x_far, x_near = swapped(x_far, x_near, "gx")
    step = shape(2, 3, nx, FRAME, nz)
    first_h, first_e = call(first_kernel, [step, step], [*fields, coef, tops, ends], name="first")
    ef, hf, ea, ha, grad = call(
        step_kernel, [shape(*e_fwd.shape)] * 4 + [shape(*density.shape)],
        fields + [coef, first_h, first_e, tops, ends, mirror, *bulk_lower, *bulk_upper, x_far, x_near, mine, theirs],
        [vmem(2, 3, nx + 1, FRAME, nz), vmem(2, 3, nx + 1, FRAME, nz), vmem(20, FRAME, nz),
         square, lines, lines, pltpu.SemaphoreType.DMA((4,))], name="steps", any_out=4)
    return ef, hf, ea, ha, grad


def solution(mesh):
    grid = P(None, "gx", "gy", None)
    slab = P(None, "gx", "gy")
    monitor = P(None, None, None, "gx", "gy")
    return jax.shard_map(
        per_device,
        mesh=mesh,
        in_specs=(grid, grid, grid, grid, P("gx", "gy", None), slab, slab, slab, monitor, monitor),
        out_specs=(grid, grid, grid, grid, slab),
        check_vma=False,
    )
```

```python
import math

import jax
import jax.numpy as jnp
from jax import lax
from jax.experimental import pallas as pl
from jax.experimental.pallas import tpu as pltpu
from jax.sharding import PartitionSpec as P

PLANES = 4
Z0 = 126
COURANT = 0.5
OMEGA = 0.7
CONTRAST = 10.0
F32 = jnp.float32
VMEM_LIMIT = 32 * 1024 * 1024
FAR_LIMIT = 60 * 1024 * 1024

LANES = 128
FRAME = 48
TOP, END = 8, 40
WINDOW = 8
SHIFT = LANES - (Z0 - 2)
ROW_EPS, ROW_MON, MESSAGE = 96, 128, 192


def lane_of(shape):
    return lax.broadcasted_iota(jnp.int32, shape, len(shape) - 1)


def row_of(shape):
    return lax.broadcasted_iota(jnp.int32, shape, len(shape) - 2)


def turn(a, shift):
    shift = shift % a.shape[1]
    return pltpu.roll(a, shift, 1) if shift else a


def up_y(a):
    return pltpu.roll(a, a.shape[0] - 1, 0)


def down_y(a):
    return pltpu.roll(a, 1, 0)


def up_z(a):
    n = a.shape[1]
    return jnp.where(lane_of(a.shape) == n - 1, 0.0, pltpu.roll(a, n - 1, 1))


def down_z(a):
    return jnp.where(lane_of(a.shape) == 0, 0.0, pltpu.roll(a, 1, 1))


def is_odd(axis):
    return lax.axis_index(axis) % 2 == 1


def ordered(odd, up, down):
    return jnp.where(odd, up, down), jnp.where(odd, down, up)


def pack_planes(planes):
    total = None
    for offset, plane in planes:
        near = jnp.where(lane_of((plane.shape[0], LANES)) >= LANES // 2,
                         plane[:, :LANES], plane[:, LANES:2 * LANES])
        part = turn(near, SHIFT + offset)
        lane = lane_of(part.shape)
        inside = (lane >= offset) & (lane < offset + WINDOW)
        total = jnp.where(inside, part, 0.0 if total is None else total)
    return total


def flipped(a, square):
    square[...] = jnp.zeros_like(square)
    square[pl.ds(0, a.shape[0]), pl.ds(0, a.shape[1])] = a
    return jnp.transpose(square[...])


def edge_planes(part, ks, nx, mark):
    up, down = [], []
    last = nx - 1
    for f in range(2):
        e = lambda c, x: part(f, 0, c, x)
        h = lambda c, x: part(f, 1, c, x)
        k = ks[last]
        ex, ey, ez = e(0, last), e(1, last), e(2, last)
        ex_b, ey_b, ez_b = e(0, last - 1), e(1, last - 1), e(2, last - 1)
        hy_b = mark(h(1, last - 1) - COURANT * ((up_z(ex_b) - ex_b) - (ez - ez_b)), last - 1)
        hz_b = mark(h(2, last - 1) - COURANT * ((ey - ey_b) - (up_y(ex_b) - ex_b)), last - 1)
        hx = mark(h(0, last) - COURANT * ((up_y(ez) - ez) - (up_z(ey) - ey)), last)
        hy = mark(h(1, last) - COURANT * ((up_z(ex) - ex) + ez), last)
        hz = mark(h(2, last) - COURANT * (-ey - (up_y(ex) - ex)), last)
        ex = ex + k * ((hz - down_y(hz)) - (hy - down_z(hy)))
        ey = ey + k * ((hx - down_z(hx)) - (hz - hz_b))
        ez = ez + k * ((hy - hy_b) - (hx - down_y(hx)))
        up += [hy, hz, mark(hy - COURANT * ((up_z(ex) - ex) + ez), last),
               mark(hz - COURANT * (-ey - (up_y(ex) - ex)), last)]
        k = ks[0]
        ex, ey, ez = e(0, 0), e(1, 0), e(2, 0)
        hx = mark(h(0, 0) - COURANT * ((up_y(ez) - ez) - (up_z(ey) - ey)), 0)
        hy = mark(h(1, 0) - COURANT * ((up_z(ex) - ex) - (e(2, 1) - ez)), 0)
        hz = mark(h(2, 0) - COURANT * ((e(1, 1) - ey) - (up_y(ex) - ex)), 0)
        down += [ey, ez, ey + k * ((hx - down_z(hx)) - hz), ez + k * (hy - (hx - down_y(hx)))]
    return up + [ks[last]], down + [ks[0]]


def write_bulk(part, eps, x_far, x_near):
    nx, ny = eps.shape[0], eps.shape[1]
    ks = [COURANT / eps[x] if x in (0, nx - 1) else None for x in range(nx)]
    odd = is_odd("gx")
    for i, planes in enumerate(zip(*edge_planes(part, ks, nx, lambda v, x: v))):
        far, near = ordered(odd, *planes)
        x_far[pl.ds(i * ny, ny), :] = far
        x_near[pl.ds(i * ny, ny), :] = near


def message_kernel(ef, hf, ea, ha, eps, density, mask, partner, mon_f, mon_a,
                   message, x_far, x_near, fields, eps_in, small_f, small_i, mons, square, sems):
    nx, ny = ef.shape[1], ef.shape[2]
    copies = []
    for f, (e, h) in enumerate(((ef, hf), (ea, ha))):
        for k, source in enumerate((e, h)):
            copies.append(pltpu.make_async_copy(source, fields.at[f, k], sems.at[2 * f + k]))
    copies.append(pltpu.make_async_copy(eps, eps_in, sems.at[4]))
    copies.append(pltpu.make_async_copy(density, small_f, sems.at[5]))
    copies.append(pltpu.make_async_copy(mask, small_i.at[0], sems.at[6]))
    copies.append(pltpu.make_async_copy(partner, small_i.at[1], sems.at[7]))
    copies.append(pltpu.make_async_copy(mon_f, mons.at[0], sems.at[8]))
    copies.append(pltpu.make_async_copy(mon_a, mons.at[1], sems.at[9]))
    for copy in copies:
        copy.start()
    message[pl.ds(ROW_EPS, MESSAGE - ROW_EPS), :] = jnp.zeros((MESSAGE - ROW_EPS, LANES), F32)
    for copy in copies[4:]:
        copy.wait()
    for half, components in ((0, (0, 1)), (1, (2,))):
        square[...] = jnp.zeros_like(square)
        for k, c in enumerate(components):
            for f in range(2):
                for x in range(nx):
                    base = k * 64 + x * 16 + f * 8 + 2
                    square[pl.ds(base, PLANES), pl.ds(0, ny)] = mons[f, 0, c, :, x, :]
                    for p in range(PLANES):
                        at = (base + 4 + p) % LANES
                        square[pl.ds(at, 1), pl.ds(0, ny)] = mons[f, 1, c, p, pl.ds(x, 1), :]
        message[pl.ds(ROW_MON + 32 * half, ny), :] = jnp.transpose(square[...])[:ny]
    own_eps = [(x * 16 + f * 8, eps_in[x]) for x in range(nx) for f in range(2)]
    square[...] = jnp.zeros_like(square)
    for p in range(PLANES):
        square[pl.ds(p * nx, nx), pl.ds(0, ny)] = CONTRAST * small_i[0, p].astype(F32)
        square[pl.ds(16 + p * nx, nx), pl.ds(0, ny)] = small_f[p]
        square[pl.ds(32 + p * nx, nx), pl.ds(0, ny)] = small_i[1, p].astype(F32)
    small = turn(square[pl.ds(0, 32), :], 64)
    index = turn(square[pl.ds(32, 32), :], 96)
    message[pl.ds(ROW_EPS, ny), :] = pack_planes(own_eps) + small + index
    for copy in copies[:4]:
        copy.wait()
    for c in range(3):
        message[pl.ds(c * 32, ny), :] = pack_planes(
            [(k * 64 + x * 16 + f * 8, fields[f, k, c, x])
             for k in range(2) for x in range(nx) for f in range(2)])
    write_bulk(lambda f, k, c, x: fields[f, k, c, x], eps_in, x_far, x_near)


def keep_kernel(message, out):
    out[...] = message[...]


def small_parts(message):
    weight = turn(message[pl.ds(ROW_EPS, 16), :], -64)
    density = turn(message[pl.ds(ROW_EPS + 16, 16), :], -64)
    partner = turn(message[pl.ds(ROW_EPS, 16), :], -96)
    return weight, density, partner


def mirror_take(table, partner, ny):
    inside = lane_of(partner.shape) < ny
    at = jnp.where(inside, partner, 0.0).astype(jnp.int32)
    row, lane = at // ny, at % ny
    got = jnp.zeros(at.shape, F32)
    for r in range(table.shape[0]):
        line = jnp.broadcast_to(table[pl.ds(r, 1), :], at.shape)
        got = jnp.where(row == r, jnp.take_along_axis(line, lane, axis=1), got)
    return got


def spread_slab(values, lines, square, nx, ny):
    lines[...] = values
    square[...] = jnp.zeros_like(square)
    for p in range(PLANES):
        for x in range(nx):
            row = lines[pl.ds(p * nx + x, 1), :]
            square[pl.ds(x * 16 + 2 + p, 1), :] = row
            square[pl.ds(x * 16 + 10 + p, 1), :] = row
    return jnp.transpose(square[...])[:ny]


def coef_kernel(bulk_far, bulk_near, eps, mine, theirs, ef, hf, ea, ha, coef, mirror_coef, y_far, y_near, table, lines, square):
    del bulk_far, bulk_near
    nx = eps.shape[0]
    ny = END - TOP
    weight, density, partner = small_parts(mine)
    weight_m, density_m, partner_m = small_parts(theirs)
    table[...] = density_m
    extra = weight * (0.5 * (density + mirror_take(table, partner, ny)))
    table[...] = density
    extra_m = weight_m * (0.5 * (density_m + mirror_take(table, partner_m, ny)))
    packed = spread_slab(extra, lines, square, nx, ny)
    lane = lane_of(packed.shape)
    for x in range(nx):
        part = turn(packed, -16 * x - SHIFT)
        low = jnp.where(lane >= Z0, part, 0.0)
        high = jnp.where(lane < Z0 + PLANES - LANES, part, 0.0)
        coef[x] = COURANT / (eps[x] + jnp.concatenate([low, high], 1))
    packed = theirs[pl.ds(ROW_EPS, ny), :] + spread_slab(extra_m, lines, square, nx, ny)
    mirror_coef[...] = jnp.where(lane < 64, COURANT / jnp.where(lane < 64, packed, 1.0), 0.0)
    odd = is_odd("gy")

    def put(at, ref, lanes):
        far, near = ordered(odd, ref[pl.ds(ny - 2, 2), :], ref[pl.ds(0, 2), :])
        y_far[pl.ds(at, 2), pl.ds(0, lanes)] = far
        y_near[pl.ds(at, 2), pl.ds(0, lanes)] = near

    for f, pair in enumerate(((ef, hf), (ea, ha))):
        for k, field in enumerate(pair):
            for c in range(3):
                for x in range(nx):
                    put(2 * plane_index(f, k, c, x, nx), field.at[c, x], y_far.shape[1])
    for x in range(nx):
        put(24 * nx + 2 * x, coef.at[x], y_far.shape[1])
    rest = jnp.zeros((8, y_far.shape[1]), F32)
    y_far[pl.ds(26 * nx, 8), :] = rest
    y_near[pl.ds(26 * nx, 8), :] = rest
    for c in range(3):
        put(26 * nx + 2 * c, theirs.at[pl.ds(c * 32, ny), :], LANES)
    put(26 * nx + 6, mirror_coef, LANES)


def plane_index(f, k, c, x, nx):
    return ((f * 2 + k) * 3 + c) * nx + x


def framed(middle, tops, ends, i):
    return jnp.concatenate([tops[i], middle, ends[i]], 0)


ROWS_UP = ((7, 40), (7, 39), (8, 39), (8, 38, 39)) * 2 + ((7, 40),)
ROWS_DOWN = ((6, 7, 40), (7, 40), (7, 39), (8, 39)) * 2 + ((7, 40),)
FIXED = 20
LATER = (2, 3, 6, 7, 8)
SLIM = 6


def edges_kernel(bulk_far, ef, hf, ea, ha, coef, mirror_coef, theirs, y_far, y_near,
                 tops, ends, mirror, x_far, x_near, x_up, x_down):
    del bulk_far
    nx, ny = coef.shape[0], coef.shape[1]
    fields = ((ef, hf), (ea, ha))
    tops[...] = jnp.zeros_like(tops)
    ends[...] = jnp.zeros_like(ends)
    mirror[...] = jnp.zeros_like(mirror)
    for c in range(3):
        mirror[c, pl.ds(TOP, ny), :] = theirs[pl.ds(c * 32, ny), :]
    mirror[3, pl.ds(TOP, ny), :] = mirror_coef[...]
    odd = is_odd("gy")

    def came(at, lanes):
        high, low = ordered(odd, y_far[pl.ds(at, 2), pl.ds(0, lanes)], y_near[pl.ds(at, 2), pl.ds(0, lanes)])
        return low, high

    for i in range(13 * nx):
        low, high = came(2 * i, y_far.shape[1])
        tops[i, pl.ds(TOP - 2, 2), :] = low
        ends[i, pl.ds(0, 2), :] = high
    for c in range(4):
        low, high = came(26 * nx + 2 * c, LANES)
        mirror[c, pl.ds(TOP - 2, 2), :] = low
        mirror[c, pl.ds(END, 2), :] = high

    def part(f, k, c, x):
        return framed(fields[f][k][c, x], tops, ends, plane_index(f, k, c, x, nx))

    ks = [framed(coef[x], tops, ends, 12 * nx + x) for x in range(nx)]
    up, down = edge_planes(part, ks, nx, lambda v, x: jnp.where(ks[x] > 0, v, 0.0))
    m = [mirror[c] for c in range(3)]
    km = mirror[3]
    lane = lane_of(km.shape)
    first = lane % 64 < 32
    up_m = [jnp.where(first, m[0], turn(m[1], 32)), jnp.where(first, m[2], turn(km, 32))]
    down_m = [jnp.where(first, turn(m[1], -32), m[0]), jnp.where(first, turn(km, -32), m[2])]
    for out, planes, wanted, window, base in ((x_up, up, ROWS_UP, up_m, 96),
                                              (x_down, down, ROWS_DOWN, down_m, 64)):
        at = 0
        for plane, rows in zip(planes, wanted):
            for row in rows:
                out[pl.ds(at, 1), :] = plane[row:row + 1]
                at += 1
        side = window[1]
        for i, plane in enumerate(LATER):
            plane = planes[plane]
            near = jnp.where(lane >= LANES // 2, plane[:, :LANES], plane[:, LANES:])
            part_in = turn(near, SHIFT + base + SLIM * i - 1)
            inside = (lane >= base + SLIM * i) & (lane < base + SLIM * (i + 1))
            side = jnp.where(inside, part_in, side)
        value = jnp.concatenate([window[0], side], 1)
        out[pl.ds(FIXED, 2), :] = value[TOP - 2:TOP]
        out[pl.ds(FIXED + 2, 2), :] = value[END:END + 2]
        out[pl.ds(FIXED + 4, ny), :] = value[TOP:END]
    x_far[...], x_near[...] = ordered(is_odd("gx"), x_up[...], x_down[...])


def slab_gradient(message, first, second, ny):
    total = None
    for c in range(3):
        mon = message[pl.ds(ROW_MON + 32 * (c // 2), ny), :]
        real = turn(mon, -64 * (c % 2))
        imag = turn(real, -4)
        real = real + math.cos(OMEGA) * first[c] + math.cos(2 * OMEGA) * second[c]
        imag = imag - math.sin(OMEGA) * first[c] - math.sin(2 * OMEGA) * second[c]
        term = real * turn(real, -8) - imag * turn(imag, -8)
        total = term if total is None else total + term
    return total


def slab_rows(packed, out, square, nx):
    square[...] = flipped(packed, square)
    for p in range(PLANES):
        for x in range(nx):
            out[pl.ds(p * nx + x, 1), :] = square[pl.ds(x * 16 + 2 + p, 1), :]


def first_kernel(ef, hf, ea, ha, coef, tops, ends, first_h, first_e):
    nx = coef.shape[0]
    fields = ((ef, hf), (ea, ha))

    def part(f, k, c, x):
        return framed(fields[f][k][c, x], tops, ends, plane_index(f, k, c, x, nx))

    for f in range(2):
        for x in range(nx):
            inside = framed(coef[x], tops, ends, 12 * nx + x) > 0
            ex, ey, ez = part(f, 0, 0, x), part(f, 0, 1, x), part(f, 0, 2, x)
            ey_n = part(f, 0, 1, x + 1) if x + 1 < nx else 0.0
            ez_n = part(f, 0, 2, x + 1) if x + 1 < nx else 0.0
            hx, hy, hz = part(f, 1, 0, x), part(f, 1, 1, x), part(f, 1, 2, x)
            first_h[f, 0, x] = jnp.where(inside, hx - COURANT * ((up_y(ez) - ez) - (up_z(ey) - ey)), 0.0)
            first_h[f, 1, x] = jnp.where(inside, hy - COURANT * ((up_z(ex) - ex) - (ez_n - ez)), 0.0)
            first_h[f, 2, x] = jnp.where(inside, hz - COURANT * ((ey_n - ey) - (up_y(ex) - ex)), 0.0)
        for x in range(nx):
            k = framed(coef[x], tops, ends, 12 * nx + x)
            hx, hy, hz = first_h[f, 0, x], first_h[f, 1, x], first_h[f, 2, x]
            hy_p = first_h[f, 1, x - 1] if x else 0.0
            hz_p = first_h[f, 2, x - 1] if x else 0.0
            first_e[f, 0, x] = part(f, 0, 0, x) + k * ((hz - down_y(hz)) - (hy - down_z(hy)))
            first_e[f, 1, x] = part(f, 0, 1, x) + k * ((hx - down_z(hx)) - (hz - hz_p))
            first_e[f, 2, x] = part(f, 0, 2, x) + k * ((hy - hy_p) - (hx - down_y(hx)))


def step_kernel(ef_in, hf_in, ea_in, ha_in, coef, first_h, first_e, tops, ends, mirror, bulk_far_1, bulk_near_1, bulk_far_2, bulk_near_2,
                x_far, x_near, mine, theirs,
                ef_out, hf_out, ea_out, ha_out, grad,
                ee, hh, halo, square, table, lines, sems):
    nx, ny, nz = coef.shape

    fields = ((ef_in, hf_in), (ea_in, ha_in))
    lane = lane_of((ny, LANES))
    odd = is_odd("gx")
    for slot, base in ((0, 96), (10, 64)):
        def source_at(row, rows, slot=slot):
            pair = (x_near, x_far) if slot == 0 else (x_far, x_near)
            return jnp.where(odd, pair[0][pl.ds(row, rows), :], pair[1][pl.ds(row, rows), :])

        def bulk_at(row, rows, slot=slot):
            far = bulk_far_1[pl.ds(row, rows), :] + bulk_far_2[pl.ds(row, rows), :]
            near = bulk_near_1[pl.ds(row, rows), :] + bulk_near_2[pl.ds(row, rows), :]
            return jnp.where(odd, near, far) if slot == 0 else jnp.where(odd, far, near)

        halo[slot + 9, pl.ds(0, TOP), :] = jnp.zeros((TOP, nz), F32)
        halo[slot + 9, pl.ds(END, TOP), :] = jnp.zeros((TOP, nz), F32)
        window = source_at(FIXED + 4, ny)
        halo[slot + 9, pl.ds(TOP, ny), :] = window
        halo[slot + 9, pl.ds(TOP - 2, 2), :] = source_at(FIXED, 2)
        halo[slot + 9, pl.ds(END, 2), :] = source_at(FIXED + 2, 2)
        side = window[:, LANES:]
        row_at = 0
        for plane, rows in enumerate(ROWS_DOWN if slot else ROWS_UP):
            at = slot + plane
            halo[at, pl.ds(0, TOP), :] = jnp.zeros((TOP, nz), F32)
            halo[at, pl.ds(END, TOP), :] = jnp.zeros((TOP, nz), F32)
            value = bulk_at(plane * ny, ny)
            if plane in LATER:
                near = turn(side, 1 - SHIFT - base - SLIM * LATER.index(plane))
                value = jnp.concatenate(
                    [jnp.where(lane >= Z0 - 1, near, value[:, :LANES]),
                     jnp.where(lane < Z0 + PLANES + 1 - LANES, near, value[:, LANES:])], 1)
            halo[at, pl.ds(TOP, ny), :] = value
            for row in rows:
                halo[at, pl.ds(row, 1), :] = source_at(row_at, 1)
                row_at += 1
    k_low, k_high = halo[8], halo[18]

    def part(f, k, c, x):
        return framed(fields[f][k][c, x], tops, ends, plane_index(f, k, c, x, nx))

    def inverse(x):
        return framed(coef[x], tops, ends, 12 * nx + x)

    def e1(f, c, x):
        edge = x >= nx - 1 or (x == 0 and c)
        return ee[f, c, x] if edge else first_e[f, c, x]

    def h1(f, c, x):
        return hh[f, c, nx] if x == nx - 1 and c else first_h[f, c, x]

    copies = []
    first_slab, second_slab = [], []
    for f in range(2):
        ey0, ez0 = part(f, 0, 1, 0), part(f, 0, 2, 0)
        dhy = jnp.where(k_low > 0, COURANT * ez0, 0.0)
        dhz = jnp.where(k_low > 0, -COURANT * ey0, 0.0)
        hh[f, 1, 0] = halo[4 * f] + dhy
        hh[f, 2, 0] = halo[4 * f + 1] + dhz
        last = nx - 1
        k = inverse(last)
        inside = k > 0
        dy = jnp.where(inside, COURANT * halo[10 + 4 * f + 1], 0.0)
        dz = jnp.where(inside, -COURANT * halo[10 + 4 * f], 0.0)
        hh[f, 1, nx] = first_h[f, 1, last] + dy
        hh[f, 2, nx] = first_h[f, 2, last] + dz
        ee[f, 0, last] = first_e[f, 0, last] + k * ((dz - down_y(dz)) - (dy - down_z(dy)))
        ee[f, 1, last] = first_e[f, 1, last] - k * dz
        ee[f, 2, last] = first_e[f, 2, last] + k * dy
        k = inverse(0)
        ee[f, 1, 0] = first_e[f, 1, 0] + k * hh[f, 2, 0]
        ee[f, 2, 0] = first_e[f, 2, 0] - k * hh[f, 1, 0]
        ee[f, 1, nx] = halo[10 + 4 * f + 2] + k_high * hh[f, 2, nx]
        ee[f, 2, nx] = halo[10 + 4 * f + 3] - k_high * hh[f, 1, nx]
        dex = k_low * ((dhz - down_y(dhz)) - (dhy - down_z(dhy)))
        dey = -k_low * dhz
        dez = k_low * dhy
        hh[f, 1, 0] = jnp.where(
            k_low > 0, halo[4 * f + 2] + dhy - COURANT * ((up_z(dex) - dex) - (ee[f, 2, 0] - dez)), 0.0)
        hh[f, 2, 0] = jnp.where(
            k_low > 0, halo[4 * f + 3] + dhz - COURANT * ((ee[f, 1, 0] - dey) - (up_y(dex) - dex)), 0.0)
        for x in range(nx):
            inside = inverse(x) > 0
            ex, ey, ez = e1(f, 0, x), e1(f, 1, x), e1(f, 2, x)
            hh[f, 0, x + 1] = jnp.where(
                inside, h1(f, 0, x) - COURANT * ((up_y(ez) - ez) - (up_z(ey) - ey)), 0.0)
            hh[f, 1, x + 1] = jnp.where(
                inside, h1(f, 1, x) - COURANT * ((up_z(ex) - ex) - (e1(f, 2, x + 1) - ez)), 0.0)
            hh[f, 2, x + 1] = jnp.where(
                inside, h1(f, 2, x) - COURANT * ((e1(f, 1, x + 1) - ey) - (up_y(ex) - ex)), 0.0)
        copies.append(pltpu.make_async_copy(
            hh.at[f, :, pl.ds(1, nx), pl.ds(TOP, ny), :], (hf_out, ha_out)[f], sems.at[2 * f]))
        copies[-1].start()
    for c in range(3):
        first_slab.append(pack_planes([(x * 16 + f * 8, e1(f, c, x)[TOP:END])
                                       for x in range(nx) for f in range(2)]))
    for f in range(2):
        for x in range(nx):
            k = inverse(x)
            hx, hy, hz = hh[f, 0, x + 1], hh[f, 1, x + 1], hh[f, 2, x + 1]
            ee[f, 0, x] = e1(f, 0, x) + k * ((hz - down_y(hz)) - (hy - down_z(hy)))
            ee[f, 1, x] = e1(f, 1, x) + k * ((hx - down_z(hx)) - (hz - hh[f, 2, x]))
            ee[f, 2, x] = e1(f, 2, x) + k * ((hy - hh[f, 1, x]) - (hx - down_y(hx)))
        copies.append(pltpu.make_async_copy(
            ee.at[f, :, pl.ds(0, nx), pl.ds(TOP, ny), :], (ef_out, ea_out)[f], sems.at[2 * f + 1]))
        copies[-1].start()
    for c in range(3):
        second_slab.append(pack_planes([(x * 16 + f * 8, ee[f, c, x, pl.ds(TOP, ny), :])
                                        for x in range(nx) for f in range(2)]))
    own = slab_gradient(mine, first_slab, second_slab, ny)

    low01, low2 = halo[9, :, pl.ds(0, LANES)], halo[9, :, pl.ds(LANES, LANES)]
    high01, high2 = halo[19, :, pl.ds(0, LANES)], halo[19, :, pl.ds(LANES, LANES)]
    lane = lane_of(low01.shape)

    def join(below, middle, above):
        return jnp.where(lane < 32, below, jnp.where(lane < 96, middle, above))

    m = [mirror[c] for c in range(3)]
    e = [join(turn(high01, -32), turn(m[0], 32), turn(low01, 96)),
         join(high01, turn(m[1], 32), turn(low01, 64)),
         join(turn(high2, -32), turn(m[2], 32), turn(low2, 96))]
    h = [join(turn(high01, -96), turn(m[0], -32), turn(low01, 32)),
         join(turn(high01, -64), turn(m[1], -32), low01),
         join(turn(high2, -96), turn(m[2], -32), turn(low2, 32))]
    k = join(high2, turn(mirror[3], 32), turn(low2, 64))
    inside = k > 0

    def ahead(a, axis):
        return (turn(a, -16), up_y(a), turn(a, -1))[axis] - a

    def behind(a, axis):
        return a - (turn(a, 16), down_y(a), turn(a, 1))[axis]

    slabs = []
    for _ in range(2):
        h = [jnp.where(inside, h[c] - COURANT * (ahead(e[(c + 2) % 3], (c + 1) % 3)
                                                 - ahead(e[(c + 1) % 3], (c + 2) % 3)), 0.0)
             for c in range(3)]
        e = [e[c] + k * (behind(h[(c + 2) % 3], (c + 1) % 3) - behind(h[(c + 1) % 3], (c + 2) % 3))
             for c in range(3)]
        slabs.append([turn(e[c], -32)[TOP:END] for c in range(3)])
    other = slab_gradient(theirs, slabs[0], slabs[1], ny)

    weight, _, partner = small_parts(mine)
    weight_m, _, _ = small_parts(theirs)
    slab_rows(other, table, square, nx)
    table[...] = table[...] * weight_m
    got = mirror_take(table, partner, ny)
    slab_rows(own, lines, square, nx)
    lines[...] = 0.5 * (lines[...] * weight + got)
    for p in range(PLANES):
        grad[p] = lines[pl.ds(p * nx, nx), pl.ds(0, ny)]
    for copy in copies:
        copy.wait()


def call(kernel, outs, args, scratch=(), name=None, any_in=False, any_out=0, work=4_000_000):
    spaces = lambda count, far: [pl.BlockSpec(memory_space=pltpu.HBM if i < far else pltpu.VMEM)
                                 for i in range(count)]
    return pl.pallas_call(
        kernel,
        out_shape=outs,
        in_specs=[pl.BlockSpec(memory_space=pltpu.HBM if any_in else pltpu.VMEM)] * len(args),
        out_specs=spaces(len(outs), any_out),
        scratch_shapes=list(scratch),
        compiler_params=pltpu.CompilerParams(vmem_limit_bytes=FAR_LIMIT if any_in else VMEM_LIMIT),
        cost_estimate=pl.CostEstimate(flops=work, bytes_accessed=4_000_000, transcendentals=0),
        name=name,
    )(*args)


def swapped(far, near, axis, start=0, stop=None):
    size = lax.axis_size(axis)

    def pairs(first):
        lows = [i for i in range(first, size - 1, 2) if start <= i < (size if stop is None else stop)]
        return [(i, i + 1) for i in lows] + [(i + 1, i) for i in lows]

    return lax.ppermute(far, axis, pairs(1)), lax.ppermute(near, axis, pairs(0))


def mirrored(block, axis):
    size = lax.axis_size(axis)
    return lax.ppermute(block, axis, [(i, size - 1 - i) for i in range(size)])


def per_device(e_fwd, h_fwd, e_adj, h_adj, eps_back, density, design_mask, partner_map, mon_fwd, mon_adj):
    _, nx, ny, nz = e_fwd.shape
    shape = lambda *dims: jax.ShapeDtypeStruct(dims, F32)
    vmem = lambda *dims: pltpu.VMEM(dims, F32)
    square = vmem(LANES, LANES)
    lines = vmem(PLANES * nx, LANES)
    block = shape(nx, ny, nz)
    fields = [e_fwd, h_fwd, e_adj, h_adj]

    bulk_shape = shape(9 * ny, nz)
    mine, *bulk = call(
        message_kernel, [shape(MESSAGE, LANES), bulk_shape, bulk_shape],
        fields + [eps_back, density, design_mask, partner_map, mon_fwd, mon_adj],
        [vmem(2, 2, 3, nx, ny, nz), vmem(nx, ny, nz), vmem(*density.shape),
         pltpu.VMEM((2,) + density.shape, jnp.int32), vmem(2, *mon_fwd.shape),
         square, pltpu.SemaphoreType.DMA((10,))], name="message", any_in=True)
    theirs = mirrored(mine, "gx")
    mine, = call(keep_kernel, [shape(MESSAGE, LANES)], [mine], name="keep")
    early = 7 * lax.axis_size("gx") // 16
    bulk_lower = swapped(*bulk, "gx", stop=early)
    bulk_upper = swapped(*bulk, "gx", start=early)
    y_shape = shape(2 * (13 * nx) + 8, nz)
    coef, mirror_coef, y_far, y_near = call(
        coef_kernel, [block, shape(ny, LANES), y_shape, y_shape], [*bulk_lower, eps_back, mine, theirs] + fields,
        [lines, lines, square], name="coefficient", work=1_000_000_000)
    y_far, y_near = swapped(y_far, y_near, "gy")
    x_shape = shape(FIXED + 4 + ny, nz)
    tile = shape(13 * nx, 8, nz)
    tops, ends, mirror, x_far, x_near = call(
        edges_kernel, [tile, tile, shape(4, FRAME, LANES), x_shape, x_shape],
        [bulk_upper[0], *fields, coef, mirror_coef, theirs, y_far, y_near],
        [vmem(*x_shape.shape)] * 2, name="edges", work=4_000_000_000)
    x_far, x_near = swapped(x_far, x_near, "gx")
    step = shape(2, 3, nx, FRAME, nz)
    first_h, first_e = call(first_kernel, [step, step], [*fields, coef, tops, ends], name="first")
    ef, hf, ea, ha, grad = call(
        step_kernel, [shape(*e_fwd.shape)] * 4 + [shape(*density.shape)],
        fields + [coef, first_h, first_e, tops, ends, mirror, *bulk_lower, *bulk_upper, x_far, x_near, mine, theirs],
        [vmem(2, 3, nx + 1, FRAME, nz), vmem(2, 3, nx + 1, FRAME, nz), vmem(20, FRAME, nz),
         square, lines, lines, pltpu.SemaphoreType.DMA((4,))], name="steps", any_out=4)
    return ef, hf, ea, ha, grad


def solution(mesh):
    grid = P(None, "gx", "gy", None)
    slab = P(None, "gx", "gy")
    monitor = P(None, None, None, "gx", "gy")
    return jax.shard_map(
        per_device,
        mesh=mesh,
        in_specs=(grid, grid, grid, grid, P("gx", "gy", None), slab, slab, slab, monitor, monitor),
        out_specs=(grid, grid, grid, grid, slab),
        check_vma=False,
    )
```
